32 devices in a mesh: group: 4 (over x, core), ctx: 8 (over z, y).
Axes of the slice: x: 2, y: 2, z: 4, core: 2. Of those that a mesh axis runs over, the one named last changes fastest.
Arguments:
- outer_gate: bfloat16 [4096, 4096], P('group', 'ctx'), may hold values from -6 to 6
- inner_gate: bfloat16 [4096, 4096], P('group', 'ctx'), may hold values from -6 to 6
- signal: bfloat16 [4096, 4096], P('group', 'ctx'), may hold values from -6 to 6
- cotangent: bfloat16 [4096, 4096], P('group', 'ctx'), may hold values from -6 to 6
- out_weight: bfloat16 [4096, 4096], P('group'), may hold values from -0.09375 to 0.09375
- filter_taps: float32 [4096, 4096], P('group', 'ctx'), may hold values from -6 to 6
- skip_gain: float32 [4096], P('group'), may hold values from -4 to 4
Outputs:
- grad_outer: bfloat16 [4096, 4096], P('group', 'ctx')
- grad_inner: bfloat16 [4096, 4096], P('group', 'ctx')
- grad_signal: bfloat16 [4096, 4096], P('group', 'ctx')
- grad_taps: float32 [4096, 4096], P('group', 'ctx')
The draws below stay inside these ranges and needn't reach their ends.
All inputs are finite; a program needn't handle non-finite values.
Results may differ from the reference program's by a relative error of at most 0.014.
Values may be sent and summed in bfloat16 or wider, within the bound.
No kernel may reach another device: no remote copies, remote signals or barrier semaphores. Data moves between devices by JAX's collectives and lax.ppermute only.
A program may use at most 128 MiB of HBM per device.

```python
import math
import jax
import jax.numpy as jnp
from jax import lax

D = 4096
TOKENS = 4096


def shard_levels(stream_key, dims, cuts, smallest, high):
    def one(axis_at, blocks):
        draws = jax.random.uniform(jax.random.fold_in(jax.random.fold_in(stream_key, 6), axis_at), (blocks,), jnp.float32, smallest / len(cuts), high / len(cuts))
        return jnp.repeat(jnp.exp(draws), dims[axis_at] // blocks).reshape((-1,) + (1,) * (len(dims) - axis_at - 1))

    level = one(*cuts[0])
    for cut in cuts[1:]:
        level = level * one(*cut)
    return level


def noise(key, shape, spread, limit, pieces=(), dtype=jnp.bfloat16):
    drawn = spread * jax.random.normal(key, shape, jnp.float32)
    if pieces:
        drawn = drawn * shard_levels(key, shape, pieces, -0.22, 0.18)
    return jnp.clip(drawn, -limit, limit).astype(dtype)


def setup_inputs(seed: int = 0) -> dict:
    key_of = jax.random.split(jax.random.key(seed), 8)
    outer_gate = noise(key_of[0], (D, TOKENS), 1.0, 6.0, ((0, 4), (1, 8)))
    inner_gate = noise(key_of[1], (D, TOKENS), 1.0, 6.0, ((0, 4), (1, 8)))
    signal = noise(key_of[2], (D, TOKENS), 1.0, 6.0, ((0, 4), (1, 8)))
    cotangent = noise(key_of[3], (D, TOKENS), 1.0, 6.0, ((0, 4), (1, 8)))
    out_weight = noise(key_of[4], (D, D), D ** -0.5, 0.09375, ((0, 4),))
    filter_taps = noise(key_of[5], (D, TOKENS), 1.0, 6.0, ((0, 4), (1, 8)), jnp.float32)
    skip_gain = noise(key_of[6], (D,), 1.0, 4.0, ((0, 4),), jnp.float32)
    return dict(outer_gate=outer_gate, inner_gate=inner_gate, signal=signal, cotangent=cotangent, out_weight=out_weight, filter_taps=filter_taps, skip_gain=skip_gain)


def reference(outer_gate, inner_gate, signal, cotangent, out_weight, filter_taps, skip_gain):
    seq_len = TOKENS
    fft_len = 2 * seq_len
    scale = 1.0 / math.sqrt(seq_len)
    block = 128
    count = D // block

    def one_block(items):
        outer, inner, sig, weights, taps, gain = items
        upstream = jnp.dot(weights, cotangent, preferred_element_type=jnp.float32).astype(jnp.bfloat16)
        product = (inner.astype(jnp.float32) * sig.astype(jnp.float32)).astype(jnp.bfloat16)
        grad_prod = (upstream.astype(jnp.float32) * outer.astype(jnp.float32)).astype(jnp.bfloat16)
        eff_taps = taps * scale
        eff_taps = eff_taps.at[:, 0].add(gain)
        spec_prod = jnp.fft.rfft(product.astype(jnp.float32), n=fft_len, axis=1)
        spec_grad = jnp.fft.rfft(grad_prod.astype(jnp.float32), n=fft_len, axis=1)
        spec_taps = jnp.fft.rfft(eff_taps, n=fft_len, axis=1)
        response = jnp.fft.irfft(spec_prod * spec_taps, n=fft_len, axis=1)[:, :seq_len].astype(jnp.bfloat16)
        back_signal = jnp.fft.irfft(spec_grad * jnp.conj(spec_taps), n=fft_len, axis=1)[:, :seq_len].astype(jnp.bfloat16)
        grad_taps = scale * jnp.fft.irfft(spec_grad * jnp.conj(spec_prod), n=fft_len, axis=1)[:, :seq_len]
        grad_outer = (upstream.astype(jnp.float32) * response.astype(jnp.float32)).astype(jnp.bfloat16)
        grad_inner = (back_signal.astype(jnp.float32) * sig.astype(jnp.float32)).astype(jnp.bfloat16)
        grad_signal = (back_signal.astype(jnp.float32) * inner.astype(jnp.float32)).astype(jnp.bfloat16)
        return (grad_outer, grad_inner, grad_signal, grad_taps.astype(jnp.float32))

    def split(array):
        return array.reshape((count, block) + array.shape[1:])
    results = lax.map(one_block, (split(outer_gate), split(inner_gate), split(signal), split(out_weight), split(filter_taps), split(skip_gain)))
    grad_outer = results[0].reshape(D, seq_len)
    grad_inner = results[1].reshape(D, seq_len)
    grad_signal = results[2].reshape(D, seq_len)
    grad_taps = results[3].reshape(D, seq_len)
    return (grad_outer, grad_inner, grad_signal, grad_taps)
```

```python
import functools
import math

import jax
import jax.numpy as jnp
import ml_dtypes
import numpy as np
from jax import lax
from jax.experimental import pallas as pl
from jax.experimental.pallas import tpu as pltpu
from jax.sharding import PartitionSpec as P

SLABS = 32
GROUP = 8
STEP = 2 * GROUP
F32 = jnp.float32
BF16 = jnp.bfloat16


def make_tables(inner):
    slab = np.arange(SLABS)
    freq = np.arange(SLABS) + 0.5
    angle = 2.0 * np.pi / (2 * SLABS) * np.outer(freq, slab)
    eye = np.eye(GROUP)
    first = np.concatenate([np.kron(np.cos(angle), eye), np.kron(-np.sin(angle), eye)], axis=0)
    last = first.T
    within = np.arange(inner)
    turn = np.repeat(2.0 * np.pi / (2 * SLABS * inner) * np.outer(freq, within), GROUP, axis=0)
    circle = 2.0 * np.pi / inner * (np.outer(within, within) % inner)
    cos, sin = np.cos(circle), np.sin(circle)
    forward = np.block([[cos, -sin], [sin, cos]])
    narrow = ml_dtypes.bfloat16
    return (
        first.astype(narrow),
        last.astype(narrow),
        np.cos(turn).astype(np.float32),
        np.sin(turn).astype(np.float32),
        forward.astype(narrow),
        forward.T.astype(narrow),
    )


def gather_slabs(block, inner):
    sources, _, local = block.shape
    wide = block.astype(F32)
    halves = []
    for half in range(2):
        pieces = [
            wide[src, half * GROUP : (half + 1) * GROUP, at : at + inner]
            for src in range(sources)
            for at in range(0, local, inner)
        ]
        halves.append(jnp.concatenate(pieces, axis=0))
    return jnp.concatenate(halves, axis=1).astype(BF16)


def forward_dft(rows, first, cos, sin, forward, inner):
    stage = jnp.dot(first, rows, preferred_element_type=F32)
    half_rows = SLABS * GROUP
    turned = []
    for half in range(2):
        lanes = slice(half * inner, (half + 1) * inner)
        real, imag = stage[:half_rows, lanes], stage[half_rows:, lanes]
        turned.append(
            jnp.concatenate([real * cos + imag * sin, imag * cos - real * sin], axis=1).astype(BF16)
        )
    spec = jnp.dot(jnp.concatenate(turned, axis=0), forward, preferred_element_type=F32)
    return (spec[:, :inner], spec[:, inner:])


def inverse_dft(spec, last, cos, sin, backward, inner):
    both = jnp.concatenate(spec, axis=1).astype(BF16)
    stage = jnp.dot(both, backward, preferred_element_type=F32)
    half_rows = SLABS * GROUP
    turned = []
    for half in range(2):
        rows = slice(half * half_rows, (half + 1) * half_rows)
        real, imag = stage[rows, :inner], stage[rows, inner:]
        turned.append(
            jnp.concatenate([real * cos - imag * sin, imag * cos + real * sin], axis=0).astype(BF16)
        )
    return jnp.dot(last, jnp.concatenate(turned, axis=1), preferred_element_type=F32)


def scatter_slabs(rows, scale, out, lead, inner):
    sources, local = out.shape[0], out.shape[-1]
    per = local // inner
    scaled = rows * scale
    for src in range(sources):
        for part in range(per):
            at = (src * per + part) * GROUP
            tile = jnp.concatenate(
                [scaled[at : at + GROUP, :inner], scaled[at : at + GROUP, inner:]], axis=0
            ).astype(BF16)
            lanes = slice(part * inner, (part + 1) * inner)
            if lead is None:
                out[src, :, lanes] = tile
            else:
                out[src, lead, :, lanes] = tile


def times_plain(left, right):
    return (left[0] * right[0] - left[1] * right[1], left[0] * right[1] + left[1] * right[0])


def times_conj(left, right):
    return (left[0] * right[0] + left[1] * right[1], left[1] * right[0] - left[0] * right[1])


def response_kernel(inner, pair, first, last, cos, sin, forward, backward, out):
    tables = (first[...], cos[...], sin[...], forward[...], inner)
    prod = forward_dft(gather_slabs(pair[:, 0], inner), *tables)
    taps = forward_dft(gather_slabs(pair[:, 1], inner), *tables)
    rows = inverse_dft(times_plain(prod, taps), last[...], cos[...], sin[...], backward[...], inner)
    scatter_slabs(rows, 1.0 / (SLABS * inner), out, None, inner)


def backward_kernel(inner, scale, pair, grad, first, last, cos, sin, forward, backward, out):
    tables = (first[...], cos[...], sin[...], forward[...], inner)
    back_tables = (last[...], cos[...], sin[...], backward[...], inner)
    grad_spec = forward_dft(gather_slabs(grad[...], inner), *tables)
    taps = forward_dft(gather_slabs(pair[:, 1], inner), *tables)
    rows = inverse_dft(times_conj(grad_spec, taps), *back_tables)
    scatter_slabs(rows, 1.0 / (SLABS * inner), out, 0, inner)
    prod = forward_dft(gather_slabs(pair[:, 0], inner), *tables)
    rows = inverse_dft(times_conj(grad_spec, prod), *back_tables)
    scatter_slabs(rows, scale / (SLABS * inner), out, 1, inner)


def conv_call(kernel, operands, lead, inner, transforms):
    sources, channels, local = operands[0].shape[0], operands[0].shape[-2], operands[0].shape[-1]
    tables = make_tables(inner)

    def moved(shape):
        middle = shape[1:-2]
        return pl.BlockSpec(
            (sources,) + middle + (STEP, local), lambda i: (0,) * (1 + len(middle)) + (i, 0)
        )

    def whole(table):
        return pl.BlockSpec(table.shape, lambda i: (0, 0))

    out_shape = (sources,) + lead + (channels, local)
    rows = channels * SLABS
    flops = transforms * rows * (2 * (2 * inner) ** 2 + 4 * SLABS * GROUP * inner)
    return pl.pallas_call(
        kernel,
        grid=(channels // STEP,),
        in_specs=[moved(op.shape) for op in operands] + [whole(t) for t in tables],
        out_specs=moved(out_shape),
        out_shape=jax.ShapeDtypeStruct(out_shape, BF16),
        compiler_params=pltpu.CompilerParams(vmem_limit_bytes=40 * 1024 * 1024),
        cost_estimate=pl.CostEstimate(
            flops=flops, bytes_accessed=2 * rows * inner * 4, transcendentals=0
        ),
    )(*operands, *[jnp.asarray(t) for t in tables])


def elementwise(left, right):
    return (left.astype(F32) * right.astype(F32)).astype(BF16)


def per_device(outer_gate, inner_gate, signal, cotangent, out_weight, filter_taps, skip_gain):
    ch_dev, tok_local = outer_gate.shape
    n_ctx = lax.axis_size("ctx")
    ch_slice = ch_dev // n_ctx
    seq_len = n_ctx * tok_local
    inner = seq_len // SLABS
    scale = 1.0 / math.sqrt(seq_len)

    def swap(array):
        return lax.all_to_all(array, "ctx", split_axis=0, concat_axis=0, tiled=True)

    def split(array):
        return array.reshape(n_ctx, ch_slice, tok_local)

    gathered = lax.all_gather(cotangent, "group", axis=0, tiled=True)
    product = elementwise(inner_gate, signal)
    at_zero = (lax.axis_index("ctx") == 0) & (
        lax.broadcasted_iota(jnp.int32, (ch_dev, tok_local), 1) == 0
    )
    eff_taps = (filter_taps * scale + jnp.where(at_zero, skip_gain[:, None], 0.0)).astype(BF16)
    pair = swap(jnp.stack([split(product), split(eff_taps)], axis=1))
    upstream = jnp.dot(out_weight, gathered, preferred_element_type=F32).astype(BF16)
    grad_prod = elementwise(upstream, outer_gate)
    grad = swap(split(grad_prod))
    response = conv_call(functools.partial(response_kernel, inner), (pair,), (), inner, 3)
    resp_home = swap(response)
    backs = conv_call(functools.partial(backward_kernel, inner, scale), (pair, grad), (2,), inner, 5)
    backs_home = swap(backs)
    back_home = backs_home[:, 0].reshape(ch_dev, tok_local)
    grad_outer = elementwise(upstream, resp_home.reshape(ch_dev, tok_local))
    grad_inner = elementwise(back_home, signal)
    grad_signal = elementwise(back_home, inner_gate)
    grad_taps = backs_home[:, 1].reshape(ch_dev, tok_local).astype(F32)
    return (grad_outer, grad_inner, grad_signal, grad_taps)


def solution(mesh):
    in_specs = (
        P("group", "ctx"),
        P("group", "ctx"),
        P("group", "ctx"),
        P("group", "ctx"),
        P("group", None),
        P("group", "ctx"),
        P("group"),
    )
    out_specs = (P("group", "ctx"), P("group", "ctx"), P("group", "ctx"), P("group", "ctx"))
    return jax.shard_map(
        per_device, mesh=mesh, in_specs=in_specs, out_specs=out_specs, check_vma=False
    )
```

```python
import functools
import math

import jax
import jax.numpy as jnp
import ml_dtypes
import numpy as np
from jax import lax
from jax.experimental import pallas as pl
from jax.experimental.pallas import tpu as pltpu
from jax.sharding import PartitionSpec as P

SLABS = 32
GROUP = 8
STEP = 2 * GROUP
F32 = jnp.float32
BF16 = jnp.bfloat16


def make_tables(inner):
    slab = np.arange(SLABS)
    freq = np.arange(SLABS) + 0.5
    angle = 2.0 * np.pi / (2 * SLABS) * np.outer(freq, slab)
    eye = np.eye(GROUP)
    first = np.concatenate([np.kron(np.cos(angle), eye), np.kron(-np.sin(angle), eye)], axis=0)
    last = first.T
    within = np.arange(inner)
    turn = np.repeat(2.0 * np.pi / (2 * SLABS * inner) * np.outer(freq, within), GROUP, axis=0)
    circle = 2.0 * np.pi / inner * (np.outer(within, within) % inner)
    cos, sin = np.cos(circle), np.sin(circle)
    forward = np.block([[cos, -sin], [sin, cos]])
    narrow = ml_dtypes.bfloat16
    return (
        first.astype(narrow),
        last.astype(narrow),
        np.cos(turn).astype(np.float32),
        np.sin(turn).astype(np.float32),
        forward.astype(narrow),
        forward.T.astype(narrow),
    )


def gather_slabs(block, inner):
    sources, _, local = block.shape
    wide = block.astype(F32)
    halves = []
    for half in range(2):
        pieces = [
            wide[src, half * GROUP : (half + 1) * GROUP, at : at + inner]
            for src in range(sources)
            for at in range(0, local, inner)
        ]
        halves.append(jnp.concatenate(pieces, axis=0))
    return jnp.concatenate(halves, axis=1).astype(BF16)


def forward_dft(rows, first, cos, sin, forward, inner):
    stage = jnp.dot(first, rows, preferred_element_type=F32)
    half_rows = SLABS * GROUP
    turned = []
    for half in range(2):
        lanes = slice(half * inner, (half + 1) * inner)
        real, imag = stage[:half_rows, lanes], stage[half_rows:, lanes]
        turned.append(
            jnp.concatenate([real * cos + imag * sin, imag * cos - real * sin], axis=1).astype(BF16)
        )
    spec = jnp.dot(jnp.concatenate(turned, axis=0), forward, preferred_element_type=F32)
    return (spec[:, :inner], spec[:, inner:])


def inverse_dft(spec, last, cos, sin, backward, inner):
    both = jnp.concatenate(spec, axis=1).astype(BF16)
    stage = jnp.dot(both, backward, preferred_element_type=F32)
    half_rows = SLABS * GROUP
    turned = []
    for half in range(2):
        rows = slice(half * half_rows, (half + 1) * half_rows)
        real, imag = stage[rows, :inner], stage[rows, inner:]
        turned.append(
            jnp.concatenate([real * cos - imag * sin, imag * cos + real * sin], axis=0).astype(BF16)
        )
    return jnp.dot(last, jnp.concatenate(turned, axis=1), preferred_element_type=F32)


def scatter_slabs(rows, scale, out, lead, inner):
    sources, local = out.shape[0], out.shape[-1]
    per = local // inner
    scaled = rows * scale
    for src in range(sources):
        for part in range(per):
            at = (src * per + part) * GROUP
            tile = jnp.concatenate(
                [scaled[at : at + GROUP, :inner], scaled[at : at + GROUP, inner:]], axis=0
            ).astype(BF16)
            lanes = slice(part * inner, (part + 1) * inner)
            if lead is None:
                out[src, :, lanes] = tile
            else:
                out[src, lead, :, lanes] = tile


def times_plain(left, right):
    return (left[0] * right[0] - left[1] * right[1], left[0] * right[1] + left[1] * right[0])


def times_conj(left, right):
    return (left[0] * right[0] + left[1] * right[1], left[1] * right[0] - left[0] * right[1])


def response_kernel(inner, pair, first, last, cos, sin, forward, backward, out):
    tables = (first[...], cos[...], sin[...], forward[...], inner)
    prod = forward_dft(gather_slabs(pair[:, 0], inner), *tables)
    taps = forward_dft(gather_slabs(pair[:, 1], inner), *tables)
    rows = inverse_dft(times_plain(prod, taps), last[...], cos[...], sin[...], backward[...], inner)
    scatter_slabs(rows, 1.0 / (SLABS * inner), out, None, inner)


def backward_kernel(inner, scale, pair, grad, first, last, cos, sin, forward, backward, out):
    tables = (first[...], cos[...], sin[...], forward[...], inner)
    back_tables = (last[...], cos[...], sin[...], backward[...], inner)
    grad_spec = forward_dft(gather_slabs(grad[...], inner), *tables)
    taps = forward_dft(gather_slabs(pair[:, 1], inner), *tables)
    rows = inverse_dft(times_conj(grad_spec, taps), *back_tables)
    scatter_slabs(rows, 1.0 / (SLABS * inner), out, 0, inner)
    prod = forward_dft(gather_slabs(pair[:, 0], inner), *tables)
    rows = inverse_dft(times_conj(grad_spec, prod), *back_tables)
    scatter_slabs(rows, scale / (SLABS * inner), out, 1, inner)


def conv_call(kernel, operands, lead, inner, transforms):
    sources, channels, local = operands[0].shape[0], operands[0].shape[-2], operands[0].shape[-1]
    tables = make_tables(inner)

    def moved(shape):
        middle = shape[1:-2]
        return pl.BlockSpec(
            (sources,) + middle + (STEP, local), lambda i: (0,) * (1 + len(middle)) + (i, 0)
        )

    def whole(table):
        return pl.BlockSpec(table.shape, lambda i: (0, 0))

    out_shape = (sources,) + lead + (channels, local)
    rows = channels * SLABS
    flops = transforms * rows * (2 * (2 * inner) ** 2 + 4 * SLABS * GROUP * inner)
    return pl.pallas_call(
        kernel,
        grid=(channels // STEP,),
        in_specs=[moved(op.shape) for op in operands] + [whole(t) for t in tables],
        out_specs=moved(out_shape),
        out_shape=jax.ShapeDtypeStruct(out_shape, BF16),
        compiler_params=pltpu.CompilerParams(vmem_limit_bytes=40 * 1024 * 1024),
        cost_estimate=pl.CostEstimate(
            flops=flops, bytes_accessed=2 * rows * inner * 4, transcendentals=0
        ),
    )(*operands, *[jnp.asarray(t) for t in tables])


def elementwise(left, right):
    return (left.astype(F32) * right.astype(F32)).astype(BF16)


def per_device(outer_gate, inner_gate, signal, cotangent, out_weight, filter_taps, skip_gain):
    ch_dev, tok_local = outer_gate.shape
    n_ctx = lax.axis_size("ctx")
    ch_slice = ch_dev // n_ctx
    seq_len = n_ctx * tok_local
    inner = seq_len // SLABS
    scale = 1.0 / math.sqrt(seq_len)

    def swap(array):
        return lax.all_to_all(array, "ctx", split_axis=0, concat_axis=0, tiled=True)

    def split(array):
        return array.reshape(n_ctx, ch_slice, tok_local)

    gathered = lax.all_gather(cotangent, "group", axis=0, tiled=True)
    product = elementwise(inner_gate, signal)
    at_zero = (lax.axis_index("ctx") == 0) & (
        lax.broadcasted_iota(jnp.int32, (ch_dev, tok_local), 1) == 0
    )
    eff_taps = (filter_taps * scale + jnp.where(at_zero, skip_gain[:, None], 0.0)).astype(BF16)
    pair = swap(jnp.stack([split(product), split(eff_taps)], axis=1))
    upstream = jnp.dot(out_weight, gathered, preferred_element_type=F32).astype(BF16)
    grad_prod = elementwise(upstream, outer_gate)
    pair, grad_prod = lax.optimization_barrier((pair, grad_prod))
    grad = swap(split(grad_prod))
    response = conv_call(functools.partial(response_kernel, inner), (pair,), (), inner, 3)
    grad, response = lax.optimization_barrier((grad, response))
    backs = conv_call(functools.partial(backward_kernel, inner, scale), (pair, grad), (2,), inner, 5)
    resp_home = swap(response)
    resp_home, backs = lax.optimization_barrier((resp_home, backs))
    backs_home = swap(backs)
    back_home = backs_home[:, 0].reshape(ch_dev, tok_local)
    grad_outer = elementwise(upstream, resp_home.reshape(ch_dev, tok_local))
    grad_inner = elementwise(back_home, signal)
    grad_signal = elementwise(back_home, inner_gate)
    grad_taps = backs_home[:, 1].reshape(ch_dev, tok_local).astype(F32)
    return (grad_outer, grad_inner, grad_signal, grad_taps)


def solution(mesh):
    in_specs = (
        P("group", "ctx"),
        P("group", "ctx"),
        P("group", "ctx"),
        P("group", "ctx"),
        P("group", None),
        P("group", "ctx"),
        P("group"),
    )
    out_specs = (P("group", "ctx"), P("group", "ctx"), P("group", "ctx"), P("group", "ctx"))
    return jax.shard_map(
        per_device, mesh=mesh, in_specs=in_specs, out_specs=out_specs, check_vma=False
    )
```

```python
import functools
import math

import jax
import jax.numpy as jnp
import ml_dtypes
import numpy as np
from jax import lax
from jax.experimental import pallas as pl
from jax.experimental.pallas import tpu as pltpu
from jax.sharding import PartitionSpec as P

SLABS = 32
GROUP = 8
STEP = 2 * GROUP
F32 = jnp.float32
BF16 = jnp.bfloat16


def make_tables(inner, chunks):
    slab = np.arange(SLABS)
    freq = np.arange(SLABS) + 0.5
    angle = 2.0 * np.pi / (2 * SLABS) * np.outer(freq, slab)
    eye = np.eye(GROUP)
    first = np.concatenate([np.kron(np.cos(angle), eye), np.kron(-np.sin(angle), eye)], axis=0)
    blocks = first.reshape(first.shape[0], chunks, -1)
    order = np.arange(chunks)
    first = np.stack([blocks[:, order ^ p].reshape(first.shape) for p in range(chunks)])
    last = first.transpose(0, 2, 1)
    within = np.arange(inner)
    turn = np.repeat(2.0 * np.pi / (2 * SLABS * inner) * np.outer(freq, within), GROUP, axis=0)
    circle = 2.0 * np.pi / inner * (np.outer(within, within) % inner)
    cos, sin = np.cos(circle), np.sin(circle)
    forward = np.block([[cos, -sin], [sin, cos]])
    narrow = ml_dtypes.bfloat16
    return (
        first.astype(narrow),
        last.astype(narrow),
        np.cos(turn).astype(np.float32),
        np.sin(turn).astype(np.float32),
        forward.astype(narrow),
        forward.T.astype(narrow),
    )


def gather_slabs(blocks, inner):
    local = blocks[0].shape[1]
    wide = [block.astype(F32) for block in blocks]
    halves = []
    for half in range(2):
        rows = slice(half * GROUP, (half + 1) * GROUP)
        pieces = [block[rows, at : at + inner] for block in wide for at in range(0, local, inner)]
        halves.append(jnp.concatenate(pieces, axis=0))
    return jnp.concatenate(halves, axis=1).astype(BF16)


def forward_dft(rows, first, cos, sin, forward, inner):
    stage = jnp.dot(first, rows, preferred_element_type=F32)
    half_rows = SLABS * GROUP
    turned = []
    for half in range(2):
        lanes = slice(half * inner, (half + 1) * inner)
        real, imag = stage[:half_rows, lanes], stage[half_rows:, lanes]
        turned.append(
            jnp.concatenate([real * cos + imag * sin, imag * cos - real * sin], axis=1).astype(BF16)
        )
    spec = jnp.dot(jnp.concatenate(turned, axis=0), forward, preferred_element_type=F32)
    return (spec[:, :inner], spec[:, inner:])


def inverse_dft(spec, last, cos, sin, backward, inner):
    both = jnp.concatenate(spec, axis=1).astype(BF16)
    stage = jnp.dot(both, backward, preferred_element_type=F32)
    half_rows = SLABS * GROUP
    turned = []
    for half in range(2):
        rows = slice(half * half_rows, (half + 1) * half_rows)
        real, imag = stage[rows, :inner], stage[rows, inner:]
        turned.append(
            jnp.concatenate([real * cos - imag * sin, imag * cos + real * sin], axis=0).astype(BF16)
        )
    return jnp.dot(last, jnp.concatenate(turned, axis=1), preferred_element_type=F32)


def scatter_slabs(rows, scale, outs, lead, inner):
    local = outs[0].shape[-1]
    per = local // inner
    scaled = rows * scale
    for src, out in enumerate(outs):
        for part in range(per):
            at = (src * per + part) * GROUP
            tile = jnp.concatenate(
                [scaled[at : at + GROUP, :inner], scaled[at : at + GROUP, inner:]], axis=0
            ).astype(BF16)
            lanes = slice(part * inner, (part + 1) * inner)
            if lead is None:
                out[:, lanes] = tile
            else:
                out[lead, :, lanes] = tile


def times_plain(left, right):
    return (left[0] * right[0] - left[1] * right[1], left[0] * right[1] + left[1] * right[0])


def times_conj(left, right):
    return (left[0] * right[0] + left[1] * right[1], left[1] * right[0] - left[0] * right[1])


def response_kernel(chunks, inner, me, *refs):
    pair, refs = refs[:chunks], refs[chunks:]
    (first, last, cos, sin, forward, backward), outs = refs[:6], refs[6:]
    tables = (first[...], cos[...], sin[...], forward[...], inner)
    prod = forward_dft(gather_slabs([ref[0] for ref in pair], inner), *tables)
    taps = forward_dft(gather_slabs([ref[1] for ref in pair], inner), *tables)
    rows = inverse_dft(times_plain(prod, taps), last[...], cos[...], sin[...], backward[...], inner)
    scatter_slabs(rows, 1.0 / (SLABS * inner), outs, None, inner)


def backward_kernel(chunks, inner, scale, me, *refs):
    pair, grad, refs = refs[:chunks], refs[chunks : 2 * chunks], refs[2 * chunks :]
    (first, last, cos, sin, forward, backward), outs = refs[:6], refs[6:]
    tables = (first[...], cos[...], sin[...], forward[...], inner)
    back_tables = (last[...], cos[...], sin[...], backward[...], inner)
    grad_spec = forward_dft(gather_slabs([ref[...] for ref in grad], inner), *tables)
    taps = forward_dft(gather_slabs([ref[1] for ref in pair], inner), *tables)
    rows = inverse_dft(times_conj(grad_spec, taps), *back_tables)
    scatter_slabs(rows, 1.0 / (SLABS * inner), outs, 0, inner)
    prod = forward_dft(gather_slabs([ref[0] for ref in pair], inner), *tables)
    rows = inverse_dft(times_conj(grad_spec, prod), *back_tables)
    scatter_slabs(rows, scale / (SLABS * inner), outs, 1, inner)


def conv_call(kernel, me, operands, tables, lead, inner, transforms):
    chunks, shape = len(operands[0]), operands[0][0].shape
    channels, local = shape[-2:]
    def rows_of(shape):
        middle = shape[:-2]
        return pl.BlockSpec(
            middle + (STEP, local), lambda i, me: (0,) * len(middle) + (i, 0)
        )

    def whole(table):
        return pl.BlockSpec(table.shape, lambda i, me: (0, 0))

    out_shape = lead + (channels, local)
    rows = channels * SLABS
    flops = transforms * rows * (2 * (2 * inner) ** 2 + 4 * SLABS * GROUP * inner)
    flat = [chunk for operand in operands for chunk in operand]
    return pl.pallas_call(
        kernel,
        grid_spec=pltpu.PrefetchScalarGridSpec(
            num_scalar_prefetch=1,
            grid=(channels // STEP,),
            in_specs=[rows_of(chunk.shape) for chunk in flat] + [whole(t) for t in tables],
            out_specs=[rows_of(out_shape)] * chunks,
        ),
        out_shape=[jax.ShapeDtypeStruct(out_shape, BF16)] * chunks,
        compiler_params=pltpu.CompilerParams(vmem_limit_bytes=40 * 1024 * 1024),
        cost_estimate=pl.CostEstimate(
            flops=flops, bytes_accessed=2 * rows * inner * 4, transcendentals=0
        ),
    )(me, *flat, *tables)


def elementwise(left, right):
    return (left.astype(F32) * right.astype(F32)).astype(BF16)


def prepare_kernel(chunks, scale, me, inner_gate, signal, taps, gain, *outs):
    at_zero = (me[0] == 0) & (lax.broadcasted_iota(jnp.int32, taps.shape[1:], 1) == 0)
    for d, out in enumerate(outs):
        at = me[0] ^ d
        out[0] = elementwise(inner_gate[at], signal[at])
        out[1] = (taps[at] * scale + jnp.where(at_zero, gain[at], 0.0)).astype(BF16)


def project_kernel(chunks, me, weight, gathered, gate, upstream, *outs):
    step = pl.program_id(0)
    rows = weight.shape[0] // 2
    total = jnp.dot(weight[...], gathered[...], preferred_element_type=F32).astype(BF16)
    upstream[...] = total.reshape(upstream.shape)
    low = elementwise(total[:rows], gate[0])
    high = elementwise(total[rows:], gate[1])
    swapped = (me[0] & 1) == 1
    for pair in range(chunks // 2):

        @pl.when(step == pair)
        def _():
            outs[2 * pair][...] = jnp.where(swapped, high, low)
            outs[2 * pair + 1][...] = jnp.where(swapped, low, high)


def outer_kernel(chunks, me, upstream, *refs):
    chunk, out = refs[:chunks], refs[chunks]
    for d in range(chunks):
        at = me[0] ^ d
        out[at] = elementwise(upstream[at], chunk[d][...])


def finish_kernel(chunks, me, inner_gate, signal, *refs):
    chunk, (grad_inner, grad_signal, grad_taps) = refs[:chunks], refs[chunks:]
    for d in range(chunks):
        at = me[0] ^ d
        back = chunk[d][0]
        grad_inner[at] = elementwise(back, signal[at])
        grad_signal[at] = elementwise(back, inner_gate[at])
        grad_taps[at] = chunk[d][1].astype(F32)


def rowwise_call(kernel, me, wholes, pieces, out_shapes, rows):
    def spec(shape):
        lead = shape[:-2]
        return pl.BlockSpec(
            lead + (rows, shape[-1]), lambda i, me: (0,) * len(lead) + (i, 0)
        )

    channels = wholes[0].shape[1]
    size = sum(math.prod(x.shape) * x.dtype.itemsize for x in (*wholes, *pieces, *out_shapes))
    return pl.pallas_call(
        kernel,
        grid_spec=pltpu.PrefetchScalarGridSpec(
            num_scalar_prefetch=1,
            grid=(channels // rows,),
            in_specs=[spec(x.shape) for x in (*wholes, *pieces)],
            out_specs=[spec(x.shape) for x in out_shapes],
        ),
        out_shape=out_shapes,
        compiler_params=pltpu.CompilerParams(vmem_limit_bytes=32 * 1024 * 1024),
        cost_estimate=pl.CostEstimate(flops=size, bytes_accessed=size, transcendentals=0),
    )(me, *wholes, *pieces)


def project_call(me, weight, gathered, gate):
    chunks, channels, local = gate.shape
    depth = weight.shape[1]

    def pair(i, me):
        return (me[0] >> 1) ^ i

    rows = 2 * channels
    return pl.pallas_call(
        functools.partial(project_kernel, chunks),
        grid_spec=pltpu.PrefetchScalarGridSpec(
            num_scalar_prefetch=1,
            grid=(chunks // 2,),
            in_specs=[
                pl.BlockSpec((rows, depth), lambda i, me: (pair(i, me), 0)),
                pl.BlockSpec((depth, local), lambda i, me: (0, 0)),
                pl.BlockSpec((2, channels, local), lambda i, me: (pair(i, me), 0, 0)),
            ],
            out_specs=[pl.BlockSpec((2, channels, local), lambda i, me: (pair(i, me), 0, 0))]
            + [pl.BlockSpec((channels, local), lambda i, me: (0, 0))] * chunks,
        ),
        out_shape=[jax.ShapeDtypeStruct(gate.shape, BF16)]
        + [jax.ShapeDtypeStruct((channels, local), BF16)] * chunks,
        compiler_params=pltpu.CompilerParams(vmem_limit_bytes=40 * 1024 * 1024),
        cost_estimate=pl.CostEstimate(
            flops=2 * weight.size * local, bytes_accessed=2 * weight.size, transcendentals=0
        ),
    )(me, weight, gathered, gate)


def exchange(parts):
    count = len(parts)
    if count > 8:
        order = lax.axis_index("ctx") ^ jnp.arange(count)
        sent = jnp.take(jnp.stack(parts), order, axis=0)
        came = lax.all_to_all(sent, "ctx", split_axis=0, concat_axis=0, tiled=True)
        return list(jnp.take(came, order, axis=0))
    came = [None] * count
    came[0] = parts[0]
    for d in reversed(range(1, count)):
        came[d] = lax.ppermute(parts[d], "ctx", [(p, p ^ d) for p in range(count)])
    return came


def after(parts, other):
    held, _ = lax.optimization_barrier((parts[0], other))
    return [held] + list(parts[1:])


def per_device(outer_gate, inner_gate, signal, cotangent, out_weight, filter_taps, skip_gain):
    ch_dev, tok_local = outer_gate.shape
    n_ctx = lax.axis_size("ctx")
    ch_slice = ch_dev // n_ctx
    seq_len = n_ctx * tok_local
    inner = seq_len // SLABS
    scale = 1.0 / math.sqrt(seq_len)
    me = lax.axis_index("ctx").reshape(1)

    def split(array):
        return array.reshape(n_ctx, ch_slice, -1)

    def flat(array):
        return array.reshape(ch_dev, tok_local)

    def shapes(lead, dtype, count):
        return [jax.ShapeDtypeStruct(lead + (ch_slice, tok_local), dtype)] * count

    tables = [jnp.asarray(table) for table in make_tables(inner, n_ctx)]
    tables = [table if table.ndim == 2 else table[me[0]] for table in tables]
    gathered = lax.all_gather(cotangent, "group", axis=0, tiled=True)
    pair = exchange(
        rowwise_call(
            functools.partial(prepare_kernel, n_ctx, scale),
            me,
            (split(inner_gate), split(signal), split(filter_taps), split(skip_gain)),
            (),
            shapes((2,), BF16, n_ctx),
            32,
        )
    )
    upstream, *grad = project_call(me, out_weight, gathered, split(outer_gate))
    grad_came = exchange(grad)
    response = conv_call(
        functools.partial(response_kernel, n_ctx, inner), me, (after(pair, grad[0]),), tables, (), inner, 3
    )
    resp_came = exchange(response)
    backs = conv_call(
        functools.partial(backward_kernel, n_ctx, inner, scale),
        me,
        (pair, after(grad_came, response[0])),
        tables,
        (2,),
        inner,
        5,
    )
    backs_came = exchange(backs)
    (grad_outer,) = rowwise_call(
        functools.partial(outer_kernel, n_ctx),
        me,
        (upstream,),
        after(resp_came, backs[0]),
        shapes((n_ctx,), BF16, 1),
        32,
    )
    grad_inner, grad_signal, grad_taps = rowwise_call(
        functools.partial(finish_kernel, n_ctx),
        me,
        (split(inner_gate), split(signal)),
        backs_came,
        shapes((n_ctx,), BF16, 2) + shapes((n_ctx,), F32, 1),
        32,
    )
    return (flat(grad_outer), flat(grad_inner), flat(grad_signal), flat(grad_taps))


def solution(mesh):
    in_specs = (
        P("group", "ctx"),
        P("group", "ctx"),
        P("group", "ctx"),
        P("group", "ctx"),
        P("group", None),
        P("group", "ctx"),
        P("group"),
    )
    out_specs = (P("group", "ctx"), P("group", "ctx"), P("group", "ctx"), P("group", "ctx"))
    return jax.shard_map(
        per_device, mesh=mesh, in_specs=in_specs, out_specs=out_specs, check_vma=False
    )
```

```python
import functools
import math

import jax
import jax.numpy as jnp
import ml_dtypes
import numpy as np
from jax import lax
from jax.experimental import pallas as pl
from jax.experimental.pallas import tpu as pltpu
from jax.sharding import PartitionSpec as P

SLABS = 32
GROUP = 8
STEP = 2 * GROUP
F32 = jnp.float32
BF16 = jnp.bfloat16


def partners(count):
    half = count // 2
    far_near = [d for low in reversed(range(half)) for d in (half + low, low)]
    return [0] + [d for d in far_near if d]


def make_tables(inner, chunks):
    slab = np.arange(SLABS)
    freq = np.arange(SLABS) + 0.5
    angle = 2.0 * np.pi / (2 * SLABS) * np.outer(freq, slab)
    eye = np.eye(GROUP)
    first = np.concatenate([np.kron(np.cos(angle), eye), np.kron(-np.sin(angle), eye)], axis=0)
    blocks = first.reshape(first.shape[0], chunks, -1)
    order = np.array(partners(chunks))
    first = np.stack([blocks[:, order ^ p].reshape(first.shape) for p in range(chunks)])
    last = first.transpose(0, 2, 1)
    within = np.arange(inner)
    turn = np.repeat(2.0 * np.pi / (2 * SLABS * inner) * np.outer(freq, within), GROUP, axis=0)
    circle = 2.0 * np.pi / inner * (np.outer(within, within) % inner)
    cos, sin = np.cos(circle), np.sin(circle)
    forward = np.block([[cos, -sin], [sin, cos]])
    narrow = ml_dtypes.bfloat16
    return (
        first.astype(narrow),
        last.astype(narrow),
        np.cos(turn).astype(np.float32),
        np.sin(turn).astype(np.float32),
        forward.astype(narrow),
        forward.T.astype(narrow),
    )


def gather_slabs(blocks, inner):
    local = blocks[0].shape[1]
    wide = [block.astype(F32) for block in blocks]
    halves = []
    for half in range(2):
        rows = slice(half * GROUP, (half + 1) * GROUP)
        pieces = [block[rows, at : at + inner] for block in wide for at in range(0, local, inner)]
        halves.append(jnp.concatenate(pieces, axis=0))
    return jnp.concatenate(halves, axis=1).astype(BF16)


def forward_dft(rows, first, cos, sin, forward, inner):
    stage = jnp.dot(first, rows, preferred_element_type=F32)
    half_rows = SLABS * GROUP
    turned = []
    for half in range(2):
        lanes = slice(half * inner, (half + 1) * inner)
        real, imag = stage[:half_rows, lanes], stage[half_rows:, lanes]
        turned.append(
            jnp.concatenate([real * cos + imag * sin, imag * cos - real * sin], axis=1).astype(BF16)
        )
    spec = jnp.dot(jnp.concatenate(turned, axis=0), forward, preferred_element_type=F32)
    return (spec[:, :inner], spec[:, inner:])


def inverse_dft(spec, last, cos, sin, backward, inner):
    both = jnp.concatenate(spec, axis=1).astype(BF16)
    stage = jnp.dot(both, backward, preferred_element_type=F32)
    half_rows = SLABS * GROUP
    turned = []
    for half in range(2):
        rows = slice(half * half_rows, (half + 1) * half_rows)
        real, imag = stage[rows, :inner], stage[rows, inner:]
        turned.append(
            jnp.concatenate([real * cos - imag * sin, imag * cos + real * sin], axis=0).astype(BF16)
        )
    return jnp.dot(last, jnp.concatenate(turned, axis=1), preferred_element_type=F32)


def scatter_slabs(rows, scale, outs, lead, inner):
    local = outs[0].shape[-1]
    per = local // inner
    scaled = rows * scale
    for src, out in enumerate(outs):
        for part in range(per):
            at = (src * per + part) * GROUP
            tile = jnp.concatenate(
                [scaled[at : at + GROUP, :inner], scaled[at : at + GROUP, inner:]], axis=0
            ).astype(BF16)
            lanes = slice(part * inner, (part + 1) * inner)
            if lead is None:
                out[:, lanes] = tile
            else:
                out[lead, :, lanes] = tile


def times_plain(left, right):
    return (left[0] * right[0] - left[1] * right[1], left[0] * right[1] + left[1] * right[0])


def times_conj(left, right):
    return (left[0] * right[0] + left[1] * right[1], left[1] * right[0] - left[0] * right[1])


def response_kernel(chunks, inner, me, *refs):
    pair, refs = refs[:chunks], refs[chunks:]
    (first, last, cos, sin, forward, backward), outs = refs[:6], refs[6:]
    tables = (first[...], cos[...], sin[...], forward[...], inner)
    prod = forward_dft(gather_slabs([ref[0] for ref in pair], inner), *tables)
    taps = forward_dft(gather_slabs([ref[1] for ref in pair], inner), *tables)
    rows = inverse_dft(times_plain(prod, taps), last[...], cos[...], sin[...], backward[...], inner)
    scatter_slabs(rows, 1.0 / (SLABS * inner), outs, None, inner)


def backward_kernel(chunks, inner, scale, me, *refs):
    pair, grad, refs = refs[:chunks], refs[chunks : 2 * chunks], refs[2 * chunks :]
    (first, last, cos, sin, forward, backward), outs = refs[:6], refs[6:]
    tables = (first[...], cos[...], sin[...], forward[...], inner)
    back_tables = (last[...], cos[...], sin[...], backward[...], inner)
    grad_spec = forward_dft(gather_slabs([ref[...] for ref in grad], inner), *tables)
    taps = forward_dft(gather_slabs([ref[1] for ref in pair], inner), *tables)
    rows = inverse_dft(times_conj(grad_spec, taps), *back_tables)
    scatter_slabs(rows, 1.0 / (SLABS * inner), outs, 0, inner)
    prod = forward_dft(gather_slabs([ref[0] for ref in pair], inner), *tables)
    rows = inverse_dft(times_conj(grad_spec, prod), *back_tables)
    scatter_slabs(rows, scale / (SLABS * inner), outs, 1, inner)


def conv_call(kernel, me, operands, tables, lead, inner, transforms):
    chunks, shape = len(operands[0]), operands[0][0].shape
    channels, local = shape[-2:]
    def rows_of(shape):
        middle = shape[:-2]
        return pl.BlockSpec(
            middle + (STEP, local), lambda i, me: (0,) * len(middle) + (i, 0)
        )

    def whole(table):
        return pl.BlockSpec(table.shape, lambda i, me: (0, 0))

    out_shape = lead + (channels, local)
    rows = channels * SLABS
    flops = transforms * rows * (2 * (2 * inner) ** 2 + 4 * SLABS * GROUP * inner)
    flat = [chunk for operand in operands for chunk in operand]
    return pl.pallas_call(
        kernel,
        grid_spec=pltpu.PrefetchScalarGridSpec(
            num_scalar_prefetch=1,
            grid=(channels // STEP,),
            in_specs=[rows_of(chunk.shape) for chunk in flat] + [whole(t) for t in tables],
            out_specs=[rows_of(out_shape)] * chunks,
        ),
        out_shape=[jax.ShapeDtypeStruct(out_shape, BF16)] * chunks,
        compiler_params=pltpu.CompilerParams(vmem_limit_bytes=40 * 1024 * 1024),
        cost_estimate=pl.CostEstimate(
            flops=flops, bytes_accessed=2 * rows * inner * 4, transcendentals=0
        ),
    )(me, *flat, *tables)


def elementwise(left, right):
    return (left.astype(F32) * right.astype(F32)).astype(BF16)


def prepare_kernel(chunks, scale, me, inner_gate, signal, taps, gain, *outs):
    at_zero = (me[0] == 0) & (lax.broadcasted_iota(jnp.int32, taps.shape[1:], 1) == 0)
    for d, out in zip(partners(chunks), outs):
        at = me[0] ^ d
        out[0] = elementwise(inner_gate[at], signal[at])
        out[1] = (taps[at] * scale + jnp.where(at_zero, gain[at], 0.0)).astype(BF16)


def project_kernel(chunks, members, me, *refs):
    weights, blocks = refs[:members], refs[members : 2 * members]
    gate, upstream, *outs = refs[2 * members :]
    step = pl.program_id(0)
    rows = weights[0].shape[0] // 2
    total = jnp.dot(weights[0][...], blocks[0][...], preferred_element_type=F32)
    for weight, block in zip(weights[1:], blocks[1:]):
        total += jnp.dot(weight[...], block[...], preferred_element_type=F32)
    total = total.astype(BF16)
    upstream[...] = total.reshape(upstream.shape)
    low = elementwise(total[:rows], gate[0])
    high = elementwise(total[rows:], gate[1])
    swapped = (me[0] & 1) == 1
    place = partners(chunks).index
    for pair in range(chunks // 2):

        @pl.when(step == pair)
        def _():
            outs[place(2 * pair)][...] = jnp.where(swapped, high, low)
            outs[place(2 * pair + 1)][...] = jnp.where(swapped, low, high)


def outer_kernel(chunks, me, upstream, *refs):
    chunk, out = refs[:chunks], refs[chunks]
    for d, piece in zip(partners(chunks), chunk):
        at = me[0] ^ d
        out[at] = elementwise(upstream[at], piece[...])


def finish_kernel(chunks, me, inner_gate, signal, *refs):
    chunk, (grad_inner, grad_signal, grad_taps) = refs[:chunks], refs[chunks:]
    for d, piece in zip(partners(chunks), chunk):
        at = me[0] ^ d
        back = piece[0]
        grad_inner[at] = elementwise(back, signal[at])
        grad_signal[at] = elementwise(back, inner_gate[at])
        grad_taps[at] = piece[1].astype(F32)


def rowwise_call(kernel, me, wholes, pieces, out_shapes, rows, limit=32):
    def spec(shape):
        lead = shape[:-2]
        return pl.BlockSpec(
            lead + (rows, shape[-1]), lambda i, me: (0,) * len(lead) + (i, 0)
        )

    channels = wholes[0].shape[1]
    size = sum(math.prod(x.shape) * x.dtype.itemsize for x in (*wholes, *pieces, *out_shapes))
    return pl.pallas_call(
        kernel,
        grid_spec=pltpu.PrefetchScalarGridSpec(
            num_scalar_prefetch=1,
            grid=(channels // rows,),
            in_specs=[spec(x.shape) for x in (*wholes, *pieces)],
            out_specs=[spec(x.shape) for x in out_shapes],
        ),
        out_shape=out_shapes,
        compiler_params=pltpu.CompilerParams(vmem_limit_bytes=limit * 1024 * 1024),
        cost_estimate=pl.CostEstimate(flops=size, bytes_accessed=size, transcendentals=0),
    )(me, *wholes, *pieces)


def project_call(me, weight, blocks, gate):
    chunks, channels, local = gate.shape
    members, depth = len(blocks), blocks[0].shape[0]

    def pair(i, me):
        return (me[0] >> 1) ^ i

    rows = 2 * channels
    return pl.pallas_call(
        functools.partial(project_kernel, chunks, members),
        grid_spec=pltpu.PrefetchScalarGridSpec(
            num_scalar_prefetch=1,
            grid=(chunks // 2,),
            in_specs=[
                pl.BlockSpec((rows, depth), lambda i, me, j=j: (pair(i, me), me[1] ^ j))
                for j in range(members)
            ]
            + [pl.BlockSpec((depth, local), lambda i, me: (0, 0))] * members
            + [pl.BlockSpec((2, channels, local), lambda i, me: (pair(i, me), 0, 0))],
            out_specs=[pl.BlockSpec((2, channels, local), lambda i, me: (pair(i, me), 0, 0))]
            + [pl.BlockSpec((channels, local), lambda i, me: (0, 0))] * chunks,
        ),
        out_shape=[jax.ShapeDtypeStruct(gate.shape, BF16)]
        + [jax.ShapeDtypeStruct((channels, local), BF16)] * chunks,
        compiler_params=pltpu.CompilerParams(vmem_limit_bytes=40 * 1024 * 1024),
        cost_estimate=pl.CostEstimate(
            flops=2 * weight.size * local, bytes_accessed=2 * weight.size, transcendentals=0
        ),
    )(me, *[weight] * members, *blocks, gate)


def gather_group(block):
    count = lax.axis_size("group")
    held, bit = {0: block}, count // 2
    while bit:
        for j in list(held):
            pairs = [(g, g ^ bit) for g in range(count)]
            held[j ^ bit] = lax.ppermute(held[j], "group", pairs)
        bit //= 2
    return [held[j] for j in range(count)]


def exchange(parts):
    count = len(parts)
    order = partners(count)
    if count > 8:
        blocks = lax.axis_index("ctx") ^ jnp.arange(count)
        where = np.argsort(order)
        sent = jnp.take(jnp.take(jnp.stack(parts), where, axis=0), blocks, axis=0)
        came = lax.all_to_all(sent, "ctx", split_axis=0, concat_axis=0, tiled=True)
        return list(jnp.take(jnp.take(came, blocks, axis=0), np.array(order), axis=0))
    return [parts[0]] + [
        lax.ppermute(part, "ctx", [(p, p ^ d) for p in range(count)])
        for d, part in zip(order[1:], parts[1:])
    ]


def after(parts, other):
    held, _ = lax.optimization_barrier((parts[0], other))
    return [held] + list(parts[1:])


def per_device(outer_gate, inner_gate, signal, cotangent, out_weight, filter_taps, skip_gain):
    ch_dev, tok_local = outer_gate.shape
    n_ctx = lax.axis_size("ctx")
    ch_slice = ch_dev // n_ctx
    seq_len = n_ctx * tok_local
    inner = seq_len // SLABS
    scale = 1.0 / math.sqrt(seq_len)
    me = jnp.stack([lax.axis_index("ctx"), lax.axis_index("group")])

    def split(array):
        return array.reshape(n_ctx, ch_slice, -1)

    def flat(array):
        return array.reshape(ch_dev, tok_local)

    def shapes(lead, dtype, count):
        return [jax.ShapeDtypeStruct(lead + (ch_slice, tok_local), dtype)] * count

    tables = [jnp.asarray(table) for table in make_tables(inner, n_ctx)]
    tables = [table if table.ndim == 2 else table[me[0]] for table in tables]
    gathered = gather_group(cotangent)
    pair = exchange(
        rowwise_call(
            functools.partial(prepare_kernel, n_ctx, scale),
            me,
            (split(inner_gate), split(signal), split(filter_taps), split(skip_gain)),
            (),
            shapes((2,), BF16, n_ctx),
            32,
            limit=60,
        )
    )
    upstream, *grad = project_call(me, out_weight, gathered, split(outer_gate))
    response = conv_call(
        functools.partial(response_kernel, n_ctx, inner), me, (after(pair, grad[0]),), tables, (), inner, 3
    )
    grad[-2:], _ = lax.optimization_barrier((grad[-2:], response[0]))
    grad_came = exchange(grad)
    resp_came = exchange(response)
    backs = conv_call(
        functools.partial(backward_kernel, n_ctx, inner, scale),
        me,
        (pair, after(grad_came, response[0])),
        tables,
        (2,),
        inner,
        5,
    )
    backs_came = exchange(backs)
    (grad_outer,) = rowwise_call(
        functools.partial(outer_kernel, n_ctx),
        me,
        (upstream,),
        after(resp_came, backs[0]),
        shapes((n_ctx,), BF16, 1),
        32,
    )
    grad_inner, grad_signal, grad_taps = rowwise_call(
        functools.partial(finish_kernel, n_ctx),
        me,
        (split(inner_gate), split(signal)),
        backs_came,
        shapes((n_ctx,), BF16, 2) + shapes((n_ctx,), F32, 1),
        32,
    )
    return (flat(grad_outer), flat(grad_inner), flat(grad_signal), flat(grad_taps))


def solution(mesh):
    in_specs = (
        P("group", "ctx"),
        P("group", "ctx"),
        P("group", "ctx"),
        P("group", "ctx"),
        P("group", None),
        P("group", "ctx"),
        P("group"),
    )
    out_specs = (P("group", "ctx"), P("group", "ctx"), P("group", "ctx"), P("group", "ctx"))
    return jax.shard_map(
        per_device, mesh=mesh, in_specs=in_specs, out_specs=out_specs, check_vma=False
    )
```

```python
import functools
import math

import jax
import jax.numpy as jnp
import ml_dtypes
import numpy as np
from jax import lax
from jax.experimental import pallas as pl
from jax.experimental.pallas import tpu as pltpu
from jax.sharding import PartitionSpec as P

SLABS = 32
GROUP = 8
STEP = 2 * GROUP
F32 = jnp.float32
BF16 = jnp.bfloat16


def partners(count):
    half = count // 2
    far_near = [d for low in reversed(range(half)) for d in (half + low, low)]
    return [0] + [d for d in far_near if d]


def make_tables(inner, chunks):
    slab = np.arange(SLABS)
    freq = np.arange(SLABS) + 0.5
    angle = 2.0 * np.pi / (2 * SLABS) * np.outer(freq, slab)
    eye = np.eye(GROUP)
    first = np.concatenate([np.kron(np.cos(angle), eye), np.kron(-np.sin(angle), eye)], axis=0)
    blocks = first.reshape(first.shape[0], chunks, -1)
    order = np.array(partners(chunks))
    first = np.stack([blocks[:, order ^ p].reshape(first.shape) for p in range(chunks)])
    last = first.transpose(0, 2, 1)
    within = np.arange(inner)
    turn = np.repeat(2.0 * np.pi / (2 * SLABS * inner) * np.outer(freq, within), GROUP, axis=0)
    circle = 2.0 * np.pi / inner * (np.outer(within, within) % inner)
    cos, sin = np.cos(circle), np.sin(circle)
    forward = np.block([[cos, -sin], [sin, cos]])
    narrow = ml_dtypes.bfloat16
    return (
        first.astype(narrow),
        last.astype(narrow),
        np.cos(turn).astype(np.float32),
        np.sin(turn).astype(np.float32),
        forward.astype(narrow),
        forward.T.astype(narrow),
    )


def gather_slabs(blocks, inner):
    local = blocks[0].shape[1]
    wide = [block.astype(F32) for block in blocks]
    halves = []
    for half in range(2):
        rows = slice(half * GROUP, (half + 1) * GROUP)
        pieces = [block[rows, at : at + inner] for block in wide for at in range(0, local, inner)]
        halves.append(jnp.concatenate(pieces, axis=0))
    return jnp.concatenate(halves, axis=1).astype(BF16)


def forward_dft(rows, first, cos, sin, forward, inner):
    stage = jnp.dot(first, rows, preferred_element_type=F32)
    half_rows = SLABS * GROUP
    turned = []
    for half in range(2):
        lanes = slice(half * inner, (half + 1) * inner)
        real, imag = stage[:half_rows, lanes], stage[half_rows:, lanes]
        turned.append(
            jnp.concatenate([real * cos + imag * sin, imag * cos - real * sin], axis=1).astype(BF16)
        )
    spec = jnp.dot(jnp.concatenate(turned, axis=0), forward, preferred_element_type=F32)
    return (spec[:, :inner], spec[:, inner:])


def inverse_dft(spec, last, cos, sin, backward, inner):
    both = jnp.concatenate(spec, axis=1).astype(BF16)
    stage = jnp.dot(both, backward, preferred_element_type=F32)
    half_rows = SLABS * GROUP
    turned = []
    for half in range(2):
        rows = slice(half * half_rows, (half + 1) * half_rows)
        real, imag = stage[rows, :inner], stage[rows, inner:]
        turned.append(
            jnp.concatenate([real * cos - imag * sin, imag * cos + real * sin], axis=0).astype(BF16)
        )
    return jnp.dot(last, jnp.concatenate(turned, axis=1), preferred_element_type=F32)


def scatter_slabs(rows, scale, outs, lead, inner):
    local = outs[0].shape[-1]
    per = local // inner
    scaled = rows * scale
    for src, out in enumerate(outs):
        for part in range(per):
            at = (src * per + part) * GROUP
            tile = jnp.concatenate(
                [scaled[at : at + GROUP, :inner], scaled[at : at + GROUP, inner:]], axis=0
            ).astype(BF16)
            lanes = slice(part * inner, (part + 1) * inner)
            if lead is None:
                out[:, lanes] = tile
            else:
                out[lead, :, lanes] = tile


def times_plain(left, right):
    return (left[0] * right[0] - left[1] * right[1], left[0] * right[1] + left[1] * right[0])


def times_conj(left, right):
    return (left[0] * right[0] + left[1] * right[1], left[1] * right[0] - left[0] * right[1])


def response_kernel(chunks, inner, me, *refs):
    pair, refs = refs[:chunks], refs[chunks:]
    (first, last, cos, sin, forward, backward), outs = refs[:6], refs[6:]
    tables = (first[...], cos[...], sin[...], forward[...], inner)
    prod = forward_dft(gather_slabs([ref[0] for ref in pair], inner), *tables)
    taps = forward_dft(gather_slabs([ref[1] for ref in pair], inner), *tables)
    rows = inverse_dft(times_plain(prod, taps), last[...], cos[...], sin[...], backward[...], inner)
    scatter_slabs(rows, 1.0 / (SLABS * inner), outs, None, inner)


def backward_kernel(chunks, inner, scale, me, *refs):
    pair, grad, refs = refs[:chunks], refs[chunks : 2 * chunks], refs[2 * chunks :]
    (first, last, cos, sin, forward, backward), outs = refs[:6], refs[6:]
    tables = (first[...], cos[...], sin[...], forward[...], inner)
    back_tables = (last[...], cos[...], sin[...], backward[...], inner)
    grad_spec = forward_dft(gather_slabs([ref[...] for ref in grad], inner), *tables)
    taps = forward_dft(gather_slabs([ref[1] for ref in pair], inner), *tables)
    rows = inverse_dft(times_conj(grad_spec, taps), *back_tables)
    scatter_slabs(rows, 1.0 / (SLABS * inner), outs, 0, inner)
    prod = forward_dft(gather_slabs([ref[0] for ref in pair], inner), *tables)
    rows = inverse_dft(times_conj(grad_spec, prod), *back_tables)
    scatter_slabs(rows, scale / (SLABS * inner), outs, 1, inner)


def conv_call(kernel, me, operands, tables, lead, inner, transforms):
    chunks, shape = len(operands[0]), operands[0][0].shape
    channels, local = shape[-2:]
    def rows_of(shape):
        middle = shape[:-2]
        return pl.BlockSpec(
            middle + (STEP, local), lambda i, me: (0,) * len(middle) + (i, 0)
        )

    def whole(table):
        return pl.BlockSpec(table.shape, lambda i, me: (0, 0))

    out_shape = lead + (channels, local)
    rows = channels * SLABS
    flops = transforms * rows * (2 * (2 * inner) ** 2 + 4 * SLABS * GROUP * inner)
    flat = [chunk for operand in operands for chunk in operand]
    return pl.pallas_call(
        kernel,
        grid_spec=pltpu.PrefetchScalarGridSpec(
            num_scalar_prefetch=1,
            grid=(channels // STEP,),
            in_specs=[rows_of(chunk.shape) for chunk in flat] + [whole(t) for t in tables],
            out_specs=[rows_of(out_shape)] * chunks,
        ),
        out_shape=[jax.ShapeDtypeStruct(out_shape, BF16)] * chunks,
        compiler_params=pltpu.CompilerParams(vmem_limit_bytes=40 * 1024 * 1024),
        cost_estimate=pl.CostEstimate(
            flops=flops, bytes_accessed=2 * rows * inner * 4, transcendentals=0
        ),
    )(me, *flat, *tables)


def elementwise(left, right):
    return (left.astype(F32) * right.astype(F32)).astype(BF16)


def prepare_kernel(chunks, scale, me, inner_gate, signal, taps, gain, *outs):
    at_zero = (me[0] == 0) & (lax.broadcasted_iota(jnp.int32, taps.shape[1:], 1) == 0)
    for d, out in zip(partners(chunks), outs):
        at = me[0] ^ d
        out[0] = elementwise(inner_gate[at], signal[at])
        out[1] = (taps[at] * scale + jnp.where(at_zero, gain[at], 0.0)).astype(BF16)


def project_kernel(chunks, members, me, *refs):
    weights, blocks = refs[:members], refs[members : 2 * members]
    gate, upstream, *outs = refs[2 * members :]
    step = pl.program_id(0)
    rows = weights[0].shape[0] // 2
    total = jnp.dot(weights[0][...], blocks[0][...], preferred_element_type=F32)
    for weight, block in zip(weights[1:], blocks[1:]):
        total += jnp.dot(weight[...], block[...], preferred_element_type=F32)
    total = total.astype(BF16)
    upstream[...] = total.reshape(upstream.shape)
    low = elementwise(total[:rows], gate[0])
    high = elementwise(total[rows:], gate[1])
    swapped = (me[0] & 1) == 1
    place = partners(chunks).index
    for pair in range(chunks // 2):

        @pl.when(step == pair)
        def _():
            outs[place(2 * pair)][...] = jnp.where(swapped, high, low)
            outs[place(2 * pair + 1)][...] = jnp.where(swapped, low, high)


def outer_kernel(chunks, me, upstream, *refs):
    chunk, out = refs[:chunks], refs[chunks]
    for d, piece in zip(partners(chunks), chunk):
        at = me[0] ^ d
        out[at] = elementwise(upstream[at], piece[...])


def finish_kernel(chunks, me, inner_gate, signal, *refs):
    chunk, (grad_inner, grad_signal, grad_taps) = refs[:chunks], refs[chunks:]
    for d, piece in zip(partners(chunks), chunk):
        at = me[0] ^ d
        back = piece[0]
        grad_inner[at] = elementwise(back, signal[at])
        grad_signal[at] = elementwise(back, inner_gate[at])
        grad_taps[at] = piece[1].astype(F32)


def rowwise_call(kernel, me, wholes, pieces, out_shapes, rows, limit=32):
    def spec(shape):
        lead = shape[:-2]
        return pl.BlockSpec(
            lead + (rows, shape[-1]), lambda i, me: (0,) * len(lead) + (i, 0)
        )

    channels = wholes[0].shape[1]
    size = sum(math.prod(x.shape) * x.dtype.itemsize for x in (*wholes, *pieces, *out_shapes))
    return pl.pallas_call(
        kernel,
        grid_spec=pltpu.PrefetchScalarGridSpec(
            num_scalar_prefetch=1,
            grid=(channels // rows,),
            in_specs=[spec(x.shape) for x in (*wholes, *pieces)],
            out_specs=[spec(x.shape) for x in out_shapes],
        ),
        out_shape=out_shapes,
        compiler_params=pltpu.CompilerParams(vmem_limit_bytes=limit * 1024 * 1024),
        cost_estimate=pl.CostEstimate(flops=size, bytes_accessed=size, transcendentals=0),
    )(me, *wholes, *pieces)


def project_call(me, weight, blocks, gate):
    chunks, channels, local = gate.shape
    members, depth = len(blocks), blocks[0].shape[0]

    def pair(i, me):
        return (me[0] >> 1) ^ i

    rows = 2 * channels
    return pl.pallas_call(
        functools.partial(project_kernel, chunks, members),
        grid_spec=pltpu.PrefetchScalarGridSpec(
            num_scalar_prefetch=1,
            grid=(chunks // 2,),
            in_specs=[
                pl.BlockSpec((rows, depth), lambda i, me, j=j: (pair(i, me), me[1] ^ j))
                for j in range(members)
            ]
            + [pl.BlockSpec((depth, local), lambda i, me: (0, 0))] * members
            + [pl.BlockSpec((2, channels, local), lambda i, me: (pair(i, me), 0, 0))],
            out_specs=[pl.BlockSpec((2, channels, local), lambda i, me: (pair(i, me), 0, 0))]
            + [pl.BlockSpec((channels, local), lambda i, me: (0, 0))] * chunks,
        ),
        out_shape=[jax.ShapeDtypeStruct(gate.shape, BF16)]
        + [jax.ShapeDtypeStruct((channels, local), BF16)] * chunks,
        compiler_params=pltpu.CompilerParams(vmem_limit_bytes=40 * 1024 * 1024),
        cost_estimate=pl.CostEstimate(
            flops=2 * weight.size * local, bytes_accessed=2 * weight.size, transcendentals=0
        ),
    )(me, *[weight] * members, *blocks, gate)


def gather_start(block):
    count = lax.axis_size("group")
    return lax.ppermute(block, "group", [(g, g ^ (count // 2)) for g in range(count)])


def gather_rest(block, far, other):
    count = lax.axis_size("group")
    bit = count // 2
    (block, far), _ = lax.optimization_barrier(((block, far), other))
    held = {0: block, bit: far}
    bit //= 2
    while bit:
        pairs = [(g, g ^ bit) for g in range(count)]
        for j in list(held):
            held[j ^ bit] = lax.ppermute(held[j], "group", pairs)
        bit //= 2
    return [held[j] for j in range(count)]


def exchange(parts):
    count = len(parts)
    order = partners(count)
    if count > 8:
        blocks = lax.axis_index("ctx") ^ jnp.arange(count)
        where = np.argsort(order)
        sent = jnp.take(jnp.take(jnp.stack(parts), where, axis=0), blocks, axis=0)
        came = lax.all_to_all(sent, "ctx", split_axis=0, concat_axis=0, tiled=True)
        return list(jnp.take(jnp.take(came, blocks, axis=0), np.array(order), axis=0))
    return [parts[0]] + [
        lax.ppermute(part, "ctx", [(p, p ^ d) for p in range(count)])
        for d, part in zip(order[1:], parts[1:])
    ]


def after(parts, other):
    held, _ = lax.optimization_barrier((parts[0], other))
    return [held] + list(parts[1:])


def per_device(outer_gate, inner_gate, signal, cotangent, out_weight, filter_taps, skip_gain):
    ch_dev, tok_local = outer_gate.shape
    n_ctx = lax.axis_size("ctx")
    ch_slice = ch_dev // n_ctx
    seq_len = n_ctx * tok_local
    inner = seq_len // SLABS
    scale = 1.0 / math.sqrt(seq_len)
    me = jnp.stack([lax.axis_index("ctx"), lax.axis_index("group")])

    def split(array):
        return array.reshape(n_ctx, ch_slice, -1)

    def flat(array):
        return array.reshape(ch_dev, tok_local)

    def shapes(lead, dtype, count):
        return [jax.ShapeDtypeStruct(lead + (ch_slice, tok_local), dtype)] * count

    tables = [jnp.asarray(table) for table in make_tables(inner, n_ctx)]
    tables = [table if table.ndim == 2 else table[me[0]] for table in tables]
    far = gather_start(cotangent)
    pair = exchange(
        rowwise_call(
            functools.partial(prepare_kernel, n_ctx, scale),
            me,
            (split(inner_gate), split(signal), split(filter_taps), split(skip_gain)),
            (),
            shapes((2,), BF16, n_ctx),
            32,
            limit=60,
        )
    )
    gathered = gather_rest(cotangent, far, pair[2])
    upstream, *grad = project_call(me, out_weight, gathered, split(outer_gate))
    response = conv_call(
        functools.partial(response_kernel, n_ctx, inner), me, (after(pair, grad[0]),), tables, (), inner, 3
    )
    grad[-2:], _ = lax.optimization_barrier((grad[-2:], response[0]))
    grad_came = exchange(grad)
    resp_came = exchange(response)
    backs = conv_call(
        functools.partial(backward_kernel, n_ctx, inner, scale),
        me,
        (pair, after(grad_came, response[0])),
        tables,
        (2,),
        inner,
        5,
    )
    backs_came = exchange(backs)
    (grad_outer,) = rowwise_call(
        functools.partial(outer_kernel, n_ctx),
        me,
        (upstream,),
        after(resp_came, backs[0]),
        shapes((n_ctx,), BF16, 1),
        32,
    )
    grad_inner, grad_signal, grad_taps = rowwise_call(
        functools.partial(finish_kernel, n_ctx),
        me,
        (split(inner_gate), split(signal)),
        backs_came,
        shapes((n_ctx,), BF16, 2) + shapes((n_ctx,), F32, 1),
        32,
    )
    return (flat(grad_outer), flat(grad_inner), flat(grad_signal), flat(grad_taps))


def solution(mesh):
    in_specs = (
        P("group", "ctx"),
        P("group", "ctx"),
        P("group", "ctx"),
        P("group", "ctx"),
        P("group", None),
        P("group", "ctx"),
        P("group"),
    )
    out_specs = (P("group", "ctx"), P("group", "ctx"), P("group", "ctx"), P("group", "ctx"))
    return jax.shard_map(
        per_device, mesh=mesh, in_specs=in_specs, out_specs=out_specs, check_vma=False
    )
```

```python
import functools
import math

import jax
import jax.numpy as jnp
import ml_dtypes
import numpy as np
from jax import lax
from jax.experimental import pallas as pl
from jax.experimental.pallas import tpu as pltpu
from jax.sharding import PartitionSpec as P

SLABS = 32
GROUP = 8
STEP = 2 * GROUP
F32 = jnp.float32
BF16 = jnp.bfloat16


def partners(count):
    half = count // 2
    far_near = [d for low in reversed(range(half)) for d in (half + low, low)]
    return [0] + [d for d in far_near if d]


def make_tables(inner, chunks):
    slab = np.arange(SLABS)
    freq = np.arange(SLABS) + 0.5
    angle = 2.0 * np.pi / (2 * SLABS) * np.outer(freq, slab)
    eye = np.eye(GROUP)
    first = np.concatenate([np.kron(np.cos(angle), eye), np.kron(-np.sin(angle), eye)], axis=0)
    blocks = first.reshape(first.shape[0], chunks, -1)
    order = np.array(partners(chunks))
    first = np.stack([blocks[:, order ^ p].reshape(first.shape) for p in range(chunks)])
    last = first.transpose(0, 2, 1)
    within = np.arange(inner)
    turn = np.repeat(2.0 * np.pi / (2 * SLABS * inner) * np.outer(freq, within), GROUP, axis=0)
    circle = 2.0 * np.pi / inner * (np.outer(within, within) % inner)
    cos, sin = np.cos(circle), np.sin(circle)
    forward = np.block([[cos, -sin], [sin, cos]])
    narrow = ml_dtypes.bfloat16
    return (
        first.astype(narrow),
        last.astype(narrow),
        np.cos(turn).astype(np.float32),
        np.sin(turn).astype(np.float32),
        forward.astype(narrow),
        forward.T.astype(narrow),
    )


def gather_slabs(blocks, inner):
    local = blocks[0].shape[1]
    wide = [block.astype(F32) for block in blocks]
    halves = []
    for half in range(2):
        rows = slice(half * GROUP, (half + 1) * GROUP)
        pieces = [block[rows, at : at + inner] for block in wide for at in range(0, local, inner)]
        halves.append(jnp.concatenate(pieces, axis=0))
    return jnp.concatenate(halves, axis=1).astype(BF16)


def forward_dft(rows, first, cos, sin, forward, inner):
    stage = jnp.dot(first, rows, preferred_element_type=F32)
    half_rows = SLABS * GROUP
    turned = []
    for half in range(2):
        lanes = slice(half * inner, (half + 1) * inner)
        real, imag = stage[:half_rows, lanes], stage[half_rows:, lanes]
        turned.append(
            jnp.concatenate([real * cos + imag * sin, imag * cos - real * sin], axis=1).astype(BF16)
        )
    spec = jnp.dot(jnp.concatenate(turned, axis=0), forward, preferred_element_type=F32)
    return (spec[:, :inner], spec[:, inner:])


def inverse_dft(spec, last, cos, sin, backward, inner):
    both = jnp.concatenate(spec, axis=1).astype(BF16)
    stage = jnp.dot(both, backward, preferred_element_type=F32)
    half_rows = SLABS * GROUP
    turned = []
    for half in range(2):
        rows = slice(half * half_rows, (half + 1) * half_rows)
        real, imag = stage[rows, :inner], stage[rows, inner:]
        turned.append(
            jnp.concatenate([real * cos - imag * sin, imag * cos + real * sin], axis=0).astype(BF16)
        )
    return jnp.dot(last, jnp.concatenate(turned, axis=1), preferred_element_type=F32)


def scatter_slabs(rows, scale, outs, lead, inner):
    local = outs[0].shape[-1]
    per = local // inner
    scaled = rows * scale
    for src, out in enumerate(outs):
        for part in range(per):
            at = (src * per + part) * GROUP
            tile = jnp.concatenate(
                [scaled[at : at + GROUP, :inner], scaled[at : at + GROUP, inner:]], axis=0
            ).astype(BF16)
            lanes = slice(part * inner, (part + 1) * inner)
            if lead is None:
                out[:, lanes] = tile
            else:
                out[lead, :, lanes] = tile


def times_plain(left, right):
    return (left[0] * right[0] - left[1] * right[1], left[0] * right[1] + left[1] * right[0])


def times_conj(left, right):
    return (left[0] * right[0] + left[1] * right[1], left[1] * right[0] - left[0] * right[1])


def response_kernel(chunks, inner, me, *refs):
    pair, refs = refs[:chunks], refs[chunks:]
    (first, last, cos, sin, forward, backward), outs = refs[:6], refs[6:]
    tables = (first[...], cos[...], sin[...], forward[...], inner)
    prod = forward_dft(gather_slabs([ref[0] for ref in pair], inner), *tables)
    taps = forward_dft(gather_slabs([ref[1] for ref in pair], inner), *tables)
    rows = inverse_dft(times_plain(prod, taps), last[...], cos[...], sin[...], backward[...], inner)
    scatter_slabs(rows, 1.0 / (SLABS * inner), outs, None, inner)


def backward_kernel(chunks, inner, scale, me, *refs):
    pair, grad, refs = refs[:chunks], refs[chunks : 2 * chunks], refs[2 * chunks :]
    (first, last, cos, sin, forward, backward), outs = refs[:6], refs[6:]
    tables = (first[...], cos[...], sin[...], forward[...], inner)
    back_tables = (last[...], cos[...], sin[...], backward[...], inner)
    grad_spec = forward_dft(gather_slabs([ref[...] for ref in grad], inner), *tables)
    taps = forward_dft(gather_slabs([ref[1] for ref in pair], inner), *tables)
    rows = inverse_dft(times_conj(grad_spec, taps), *back_tables)
    scatter_slabs(rows, 1.0 / (SLABS * inner), outs, 0, inner)
    prod = forward_dft(gather_slabs([ref[0] for ref in pair], inner), *tables)
    rows = inverse_dft(times_conj(grad_spec, prod), *back_tables)
    scatter_slabs(rows, scale / (SLABS * inner), outs, 1, inner)


def conv_call(kernel, me, operands, tables, lead, inner, transforms):
    chunks, shape = len(operands[0]), operands[0][0].shape
    channels, local = shape[-2:]
    def rows_of(shape):
        middle = shape[:-2]
        return pl.BlockSpec(
            middle + (STEP, local), lambda i, me: (0,) * len(middle) + (i, 0)
        )

    def whole(table):
        return pl.BlockSpec(table.shape, lambda i, me: (0, 0))

    out_shape = lead + (channels, local)
    rows = channels * SLABS
    flops = transforms * rows * (2 * (2 * inner) ** 2 + 4 * SLABS * GROUP * inner)
    flat = [chunk for operand in operands for chunk in operand]
    return pl.pallas_call(
        kernel,
        grid_spec=pltpu.PrefetchScalarGridSpec(
            num_scalar_prefetch=1,
            grid=(channels // STEP,),
            in_specs=[rows_of(chunk.shape) for chunk in flat] + [whole(t) for t in tables],
            out_specs=[rows_of(out_shape)] * chunks,
        ),
        out_shape=[jax.ShapeDtypeStruct(out_shape, BF16)] * chunks,
        compiler_params=pltpu.CompilerParams(vmem_limit_bytes=40 * 1024 * 1024),
        cost_estimate=pl.CostEstimate(
            flops=flops, bytes_accessed=2 * rows * inner * 4, transcendentals=0
        ),
    )(me, *flat, *tables)


def elementwise(left, right):
    return (left.astype(F32) * right.astype(F32)).astype(BF16)


def prepare_kernel(masks, scale, inner_gate, signal, taps, gain, *refs):
    count = len(masks)
    outs, (gates, values, filters, sems) = refs[:count], refs[count:]
    me = lax.axis_index("ctx")
    copies = []
    for k, mask in enumerate(masks):
        at = me ^ mask
        pairs = ((inner_gate, gates), (signal, values), (taps, filters))
        copies.append(
            [
                pltpu.make_async_copy(src.at[at], dst.at[k], sems.at[k, n])
                for n, (src, dst) in enumerate(pairs)
            ]
        )
    for group in copies:
        for copy in group:
            copy.start()
    rows, lanes = gates.shape[1], gain.shape[1]
    shape = (rows, lanes)
    diagonal = lax.broadcasted_iota(jnp.int32, shape, 0) == lax.broadcasted_iota(jnp.int32, shape, 1)
    at_zero = (me == 0) & (lax.broadcasted_iota(jnp.int32, filters.shape[1:], 1) == 0)
    for k, (mask, group, out) in enumerate(zip(masks, copies, outs)):
        row = gain[pl.ds(me ^ mask, 1), :]
        column = jnp.sum(jnp.where(diagonal, row, 0.0), axis=1, keepdims=True)
        for copy in group:
            copy.wait()
        out[0] = elementwise(gates[k], values[k])
        out[1] = (filters[k] * scale + jnp.where(at_zero, column, 0.0)).astype(BF16)


def prepare_call(masks, scale, inner_gate, signal, taps, gain):
    count, (rows, lanes) = len(masks), taps.shape[1:]
    out = jax.ShapeDtypeStruct((2, rows, lanes), BF16)
    anywhere = pl.BlockSpec(memory_space=pl.ANY)
    inside = pl.BlockSpec(memory_space=pltpu.VMEM)
    return pl.pallas_call(
        functools.partial(prepare_kernel, masks, scale),
        in_specs=[anywhere, anywhere, anywhere, inside],
        out_specs=[inside] * count,
        out_shape=[out] * count,
        scratch_shapes=[
            pltpu.VMEM((count, rows, lanes), BF16),
            pltpu.VMEM((count, rows, lanes), BF16),
            pltpu.VMEM((count, rows, lanes), F32),
            pltpu.SemaphoreType.DMA((count, 3)),
        ],
        compiler_params=pltpu.CompilerParams(vmem_limit_bytes=48 * 1024 * 1024),
        cost_estimate=pl.CostEstimate(
            flops=8 * count * rows * lanes, bytes_accessed=12 * count * rows * lanes, transcendentals=0
        ),
    )(inner_gate, signal, taps, gain)


def project_kernel(chunks, members, me, *refs):
    weights, blocks = refs[:members], refs[members : 2 * members]
    gate, upstream, *outs = refs[2 * members :]
    step = pl.program_id(0)
    rows = weights[0].shape[0] // 2
    total = jnp.dot(weights[0][...], blocks[0][...], preferred_element_type=F32)
    for weight, block in zip(weights[1:], blocks[1:]):
        total += jnp.dot(weight[...], block[...], preferred_element_type=F32)
    total = total.astype(BF16)
    upstream[...] = total.reshape(upstream.shape)
    low = elementwise(total[:rows], gate[0])
    high = elementwise(total[rows:], gate[1])
    swapped = (me[0] & 1) == 1
    place = partners(chunks).index
    for pair in range(chunks // 2):

        @pl.when(step == pair)
        def _():
            outs[place(2 * pair)][...] = jnp.where(swapped, high, low)
            outs[place(2 * pair + 1)][...] = jnp.where(swapped, low, high)


def outer_kernel(chunks, me, upstream, *refs):
    chunk, out = refs[:chunks], refs[chunks]
    for d, piece in zip(partners(chunks), chunk):
        at = me[0] ^ d
        out[at] = elementwise(upstream[at], piece[...])


def finish_kernel(count, me, *refs):
    gates, refs = refs[:count], refs[count:]
    values, refs = refs[:count], refs[count:]
    chunk, (grad_inner, grad_signal, grad_taps) = refs[:count], refs[-3:]
    step = pl.program_id(0)
    for k in range(count):

        @pl.when(step == k)
        def _(k=k):
            back = chunk[k][0]
            grad_inner[0] = elementwise(back, values[k][0])
            grad_signal[0] = elementwise(back, gates[k][0])
            grad_taps[0] = chunk[k][1].astype(F32)


def finish_call(me, masks, inner_gate, signal, chunks, earlier):
    count, shape = len(masks), inner_gate.shape
    block = (1,) + shape[1:]

    def place(i, me):
        mask = masks[0]
        for k in range(1, count):
            mask = jnp.where(i == k, masks[k], mask)
        return (me[0] ^ mask, 0, 0)

    gates = [pl.BlockSpec(block, lambda i, me, mask=mask: (me[0] ^ mask, 0, 0)) for mask in masks]
    pieces = [pl.BlockSpec(chunk.shape, lambda i, me: (0, 0, 0)) for chunk in chunks]
    return pl.pallas_call(
        functools.partial(finish_kernel, count),
        grid_spec=pltpu.PrefetchScalarGridSpec(
            num_scalar_prefetch=1,
            grid=(count,),
            in_specs=gates * 2 + pieces + [pl.BlockSpec(memory_space=pl.ANY)] * len(earlier),
            out_specs=[pl.BlockSpec(block, place)] * 3,
        ),
        out_shape=[jax.ShapeDtypeStruct(shape, dtype) for dtype in (BF16, BF16, F32)],
        input_output_aliases={1 + 3 * count + n: n for n in range(len(earlier))},
        compiler_params=pltpu.CompilerParams(vmem_limit_bytes=32 * 1024 * 1024),
        cost_estimate=pl.CostEstimate(
            flops=2 * count * math.prod(shape[1:]),
            bytes_accessed=16 * count * math.prod(shape[1:]),
            transcendentals=0,
        ),
    )(me, *[inner_gate] * count, *[signal] * count, *chunks, *earlier)


def rowwise_call(kernel, me, wholes, pieces, out_shapes, rows, limit=32):
    def spec(shape):
        lead = shape[:-2]
        return pl.BlockSpec(
            lead + (rows, shape[-1]), lambda i, me: (0,) * len(lead) + (i, 0)
        )

    channels = wholes[0].shape[1]
    size = sum(math.prod(x.shape) * x.dtype.itemsize for x in (*wholes, *pieces, *out_shapes))
    return pl.pallas_call(
        kernel,
        grid_spec=pltpu.PrefetchScalarGridSpec(
            num_scalar_prefetch=1,
            grid=(channels // rows,),
            in_specs=[spec(x.shape) for x in (*wholes, *pieces)],
            out_specs=[spec(x.shape) for x in out_shapes],
        ),
        out_shape=out_shapes,
        compiler_params=pltpu.CompilerParams(vmem_limit_bytes=limit * 1024 * 1024),
        cost_estimate=pl.CostEstimate(flops=size, bytes_accessed=size, transcendentals=0),
    )(me, *wholes, *pieces)


def project_call(me, weight, blocks, gate):
    chunks, channels, local = gate.shape
    members, depth = len(blocks), blocks[0].shape[0]

    def pair(i, me):
        return (me[0] >> 1) ^ i

    rows = 2 * channels
    return pl.pallas_call(
        functools.partial(project_kernel, chunks, members),
        grid_spec=pltpu.PrefetchScalarGridSpec(
            num_scalar_prefetch=1,
            grid=(chunks // 2,),
            in_specs=[
                pl.BlockSpec((rows, depth), lambda i, me, j=j: (pair(i, me), me[1] ^ j))
                for j in range(members)
            ]
            + [pl.BlockSpec((depth, local), lambda i, me: (0, 0))] * members
            + [pl.BlockSpec((2, channels, local), lambda i, me: (pair(i, me), 0, 0))],
            out_specs=[pl.BlockSpec((2, channels, local), lambda i, me: (pair(i, me), 0, 0))]
            + [pl.BlockSpec((channels, local), lambda i, me: (0, 0))] * chunks,
        ),
        out_shape=[jax.ShapeDtypeStruct(gate.shape, BF16)]
        + [jax.ShapeDtypeStruct((channels, local), BF16)] * chunks,
        compiler_params=pltpu.CompilerParams(vmem_limit_bytes=40 * 1024 * 1024),
        cost_estimate=pl.CostEstimate(
            flops=2 * weight.size * local, bytes_accessed=2 * weight.size, transcendentals=0
        ),
    )(me, *[weight] * members, *blocks, gate)


def gather_start(block):
    count = lax.axis_size("group")
    return lax.ppermute(block, "group", [(g, g ^ (count // 2)) for g in range(count)])


def gather_rest(block, far, other):
    count = lax.axis_size("group")
    bit = count // 2
    (block, far), _ = lax.optimization_barrier(((block, far), other))
    held = {0: block, bit: far}
    bit //= 2
    while bit:
        pairs = [(g, g ^ bit) for g in range(count)]
        for j in list(held):
            held[j ^ bit] = lax.ppermute(held[j], "group", pairs)
        bit //= 2
    return [held[j] for j in range(count)]


def exchange(parts):
    count = len(parts)
    order = partners(count)
    if count > 8:
        blocks = lax.axis_index("ctx") ^ jnp.arange(count)
        where = np.argsort(order)
        sent = jnp.take(jnp.take(jnp.stack(parts), where, axis=0), blocks, axis=0)
        came = lax.all_to_all(sent, "ctx", split_axis=0, concat_axis=0, tiled=True)
        return list(jnp.take(jnp.take(came, blocks, axis=0), np.array(order), axis=0))
    return [parts[0]] + [
        lax.ppermute(part, "ctx", [(p, p ^ d) for p in range(count)])
        for d, part in zip(order[1:], parts[1:])
    ]


def after(parts, other):
    held, _ = lax.optimization_barrier((parts[0], other))
    return [held] + list(parts[1:])


def per_device(outer_gate, inner_gate, signal, cotangent, out_weight, filter_taps, skip_gain):
    ch_dev, tok_local = outer_gate.shape
    n_ctx = lax.axis_size("ctx")
    ch_slice = ch_dev // n_ctx
    seq_len = n_ctx * tok_local
    inner = seq_len // SLABS
    scale = 1.0 / math.sqrt(seq_len)
    me = jnp.stack([lax.axis_index("ctx"), lax.axis_index("group")])

    def split(array):
        return array.reshape(n_ctx, ch_slice, -1)

    def flat(array):
        return array.reshape(ch_dev, tok_local)

    def shapes(lead, dtype, count):
        return [jax.ShapeDtypeStruct(lead + (ch_slice, tok_local), dtype)] * count

    tables = [jnp.asarray(table) for table in make_tables(inner, n_ctx)]
    tables = [table if table.ndim == 2 else table[me[0]] for table in tables]
    masks = partners(n_ctx)
    first = min(4, n_ctx)
    sources = (scale, split(inner_gate), split(signal), split(filter_taps), split(skip_gain)[:, :, 0])
    head = prepare_call(masks[1:first], *sources)
    cotangent, _ = lax.optimization_barrier((cotangent, head[0]))
    far = gather_start(cotangent)
    own, *rest = prepare_call([0] + masks[first:], *sources)
    pair = exchange([own, *head, *rest])
    gathered = gather_rest(cotangent, far, (pair[1:first], rest[:1]))
    upstream, *grad = project_call(me, out_weight, gathered, split(outer_gate))
    response = conv_call(
        functools.partial(response_kernel, n_ctx, inner), me, (after(pair, grad[0]),), tables, (), inner, 3
    )
    grad[-2:], _ = lax.optimization_barrier((grad[-2:], response[0]))
    grad_came = exchange(grad)
    resp_came = exchange(response)
    backs = conv_call(
        functools.partial(backward_kernel, n_ctx, inner, scale),
        me,
        (pair, after(grad_came, response[0])),
        tables,
        (2,),
        inner,
        5,
    )
    backs_came = exchange(backs)
    (grad_outer,) = rowwise_call(
        functools.partial(outer_kernel, n_ctx),
        me,
        (upstream,),
        after(resp_came, backs[0]),
        shapes((n_ctx,), BF16, 1),
        32,
    )
    outs = []
    cut = n_ctx - 3
    for low, high in ((0, cut), (cut, n_ctx)):
        outs = finish_call(
            me, masks[low:high], split(inner_gate), split(signal), backs_came[low:high], outs
        )
    grad_inner, grad_signal, grad_taps = outs
    return (flat(grad_outer), flat(grad_inner), flat(grad_signal), flat(grad_taps))


def solution(mesh):
    in_specs = (
        P("group", "ctx"),
        P("group", "ctx"),
        P("group", "ctx"),
        P("group", "ctx"),
        P("group", None),
        P("group", "ctx"),
        P("group"),
    )
    out_specs = (P("group", "ctx"), P("group", "ctx"), P("group", "ctx"), P("group", "ctx"))
    return jax.shard_map(
        per_device, mesh=mesh, in_specs=in_specs, out_specs=out_specs, check_vma=False
    )
```

```python
import functools
import math

import jax
import jax.numpy as jnp
import ml_dtypes
import numpy as np
from jax import lax
from jax.experimental import pallas as pl
from jax.experimental.pallas import tpu as pltpu
from jax.sharding import PartitionSpec as P

SLABS = 32
GROUP = 8
STEP = 2 * GROUP
F32 = jnp.float32
BF16 = jnp.bfloat16


def partners(count):
    return [0] + list(reversed(range(1, count)))


def make_tables(inner, chunks):
    slab = np.arange(SLABS)
    freq = np.arange(SLABS) + 0.5
    angle = 2.0 * np.pi / (2 * SLABS) * np.outer(freq, slab)
    eye = np.eye(GROUP)
    first = np.concatenate([np.kron(np.cos(angle), eye), np.kron(-np.sin(angle), eye)], axis=0)
    blocks = first.reshape(first.shape[0], chunks, -1)
    order = np.array(partners(chunks))
    first = np.stack([blocks[:, order ^ p].reshape(first.shape) for p in range(chunks)])
    last = first.transpose(0, 2, 1)
    within = np.arange(inner)
    turn = np.repeat(2.0 * np.pi / (2 * SLABS * inner) * np.outer(freq, within), GROUP, axis=0)
    circle = 2.0 * np.pi / inner * (np.outer(within, within) % inner)
    cos, sin = np.cos(circle), np.sin(circle)
    forward = np.block([[cos, -sin], [sin, cos]])
    narrow = ml_dtypes.bfloat16
    return (
        first.astype(narrow),
        last.astype(narrow),
        np.cos(turn).astype(np.float32),
        np.sin(turn).astype(np.float32),
        forward.astype(narrow),
        forward.T.astype(narrow),
    )


def gather_slabs(blocks, inner):
    local = blocks[0].shape[1]
    wide = [block.astype(F32) for block in blocks]
    halves = []
    for half in range(2):
        rows = slice(half * GROUP, (half + 1) * GROUP)
        pieces = [block[rows, at : at + inner] for block in wide for at in range(0, local, inner)]
        halves.append(jnp.concatenate(pieces, axis=0))
    return jnp.concatenate(halves, axis=1).astype(BF16)


def forward_dft(rows, first, cos, sin, forward, inner):
    stage = jnp.dot(first, rows, preferred_element_type=F32)
    half_rows = SLABS * GROUP
    turned = []
    for half in range(2):
        lanes = slice(half * inner, (half + 1) * inner)
        real, imag = stage[:half_rows, lanes], stage[half_rows:, lanes]
        turned.append(
            jnp.concatenate([real * cos + imag * sin, imag * cos - real * sin], axis=1).astype(BF16)
        )
    spec = jnp.dot(jnp.concatenate(turned, axis=0), forward, preferred_element_type=F32)
    return (spec[:, :inner], spec[:, inner:])


def inverse_dft(spec, last, cos, sin, backward, inner):
    both = jnp.concatenate(spec, axis=1).astype(BF16)
    stage = jnp.dot(both, backward, preferred_element_type=F32)
    half_rows = SLABS * GROUP
    turned = []
    for half in range(2):
        rows = slice(half * half_rows, (half + 1) * half_rows)
        real, imag = stage[rows, :inner], stage[rows, inner:]
        turned.append(
            jnp.concatenate([real * cos - imag * sin, imag * cos + real * sin], axis=0).astype(BF16)
        )
    return jnp.dot(last, jnp.concatenate(turned, axis=1), preferred_element_type=F32)


def scatter_slabs(rows, scale, outs, lead, inner):
    local = outs[0].shape[-1]
    per = local // inner
    scaled = rows * scale
    for src, out in enumerate(outs):
        for part in range(per):
            at = (src * per + part) * GROUP
            tile = jnp.concatenate(
                [scaled[at : at + GROUP, :inner], scaled[at : at + GROUP, inner:]], axis=0
            ).astype(BF16)
            lanes = slice(part * inner, (part + 1) * inner)
            if lead is None:
                out[:, lanes] = tile
            else:
                out[lead, :, lanes] = tile


def times_plain(left, right):
    return (left[0] * right[0] - left[1] * right[1], left[0] * right[1] + left[1] * right[0])


def times_conj(left, right):
    return (left[0] * right[0] + left[1] * right[1], left[1] * right[0] - left[0] * right[1])


def response_kernel(chunks, inner, me, *refs):
    pair, refs = refs[:chunks], refs[chunks:]
    (first, last, cos, sin, forward, backward), outs = refs[:6], refs[6:]
    tables = (first[...], cos[...], sin[...], forward[...], inner)
    prod = forward_dft(gather_slabs([ref[0] for ref in pair], inner), *tables)
    taps = forward_dft(gather_slabs([ref[1] for ref in pair], inner), *tables)
    rows = inverse_dft(times_plain(prod, taps), last[...], cos[...], sin[...], backward[...], inner)
    scatter_slabs(rows, 1.0 / (SLABS * inner), outs, None, inner)


def backward_kernel(chunks, inner, scale, me, *refs):
    pair, grad, refs = refs[:chunks], refs[chunks : 2 * chunks], refs[2 * chunks :]
    (first, last, cos, sin, forward, backward), outs = refs[:6], refs[6:]
    tables = (first[...], cos[...], sin[...], forward[...], inner)
    back_tables = (last[...], cos[...], sin[...], backward[...], inner)
    grad_spec = forward_dft(gather_slabs([ref[...] for ref in grad], inner), *tables)
    taps = forward_dft(gather_slabs([ref[1] for ref in pair], inner), *tables)
    rows = inverse_dft(times_conj(grad_spec, taps), *back_tables)
    scatter_slabs(rows, 1.0 / (SLABS * inner), outs, 0, inner)
    prod = forward_dft(gather_slabs([ref[0] for ref in pair], inner), *tables)
    rows = inverse_dft(times_conj(grad_spec, prod), *back_tables)
    scatter_slabs(rows, scale / (SLABS * inner), outs, 1, inner)


def conv_call(kernel, me, operands, tables, lead, inner, transforms):
    chunks, shape = len(operands[0]), operands[0][0].shape
    channels, local = shape[-2:]
    def rows_of(shape):
        middle = shape[:-2]
        return pl.BlockSpec(
            middle + (STEP, local), lambda i, me: (0,) * len(middle) + (i, 0)
        )

    def whole(table):
        return pl.BlockSpec(table.shape, lambda i, me: (0, 0))

    out_shape = lead + (channels, local)
    rows = channels * SLABS
    flops = transforms * rows * (2 * (2 * inner) ** 2 + 4 * SLABS * GROUP * inner)
    flat = [chunk for operand in operands for chunk in operand]
    return pl.pallas_call(
        kernel,
        grid_spec=pltpu.PrefetchScalarGridSpec(
            num_scalar_prefetch=1,
            grid=(channels // STEP,),
            in_specs=[rows_of(chunk.shape) for chunk in flat] + [whole(t) for t in tables],
            out_specs=[rows_of(out_shape)] * chunks,
        ),
        out_shape=[jax.ShapeDtypeStruct(out_shape, BF16)] * chunks,
        compiler_params=pltpu.CompilerParams(vmem_limit_bytes=40 * 1024 * 1024),
        cost_estimate=pl.CostEstimate(
            flops=flops, bytes_accessed=2 * rows * inner * 4, transcendentals=0
        ),
    )(me, *flat, *tables)


def elementwise(left, right):
    return (left.astype(F32) * right.astype(F32)).astype(BF16)


def prepare_kernel(masks, scale, inner_gate, signal, taps, gain, *refs):
    count = len(masks)
    outs, (gates, values, filters, sems) = refs[:count], refs[count:]
    me = lax.axis_index("ctx")
    copies = []
    for k, mask in enumerate(masks):
        at = me ^ mask
        pairs = ((inner_gate, gates), (signal, values), (taps, filters))
        copies.append(
            [
                pltpu.make_async_copy(src.at[at], dst.at[k], sems.at[k, n])
                for n, (src, dst) in enumerate(pairs)
            ]
        )
    for group in copies:
        for copy in group:
            copy.start()
    rows, lanes = gates.shape[1], gain.shape[1]
    shape = (rows, lanes)
    diagonal = lax.broadcasted_iota(jnp.int32, shape, 0) == lax.broadcasted_iota(jnp.int32, shape, 1)
    at_zero = (me == 0) & (lax.broadcasted_iota(jnp.int32, filters.shape[1:], 1) == 0)
    for k, (mask, group, out) in enumerate(zip(masks, copies, outs)):
        row = gain[pl.ds(me ^ mask, 1), :]
        column = jnp.sum(jnp.where(diagonal, row, 0.0), axis=1, keepdims=True)
        for copy in group:
            copy.wait()
        out[0] = elementwise(gates[k], values[k])
        out[1] = (filters[k] * scale + jnp.where(at_zero, column, 0.0)).astype(BF16)


def prepare_call(masks, scale, inner_gate, signal, taps, gain):
    count, (rows, lanes) = len(masks), taps.shape[1:]
    out = jax.ShapeDtypeStruct((2, rows, lanes), BF16)
    anywhere = pl.BlockSpec(memory_space=pl.ANY)
    inside = pl.BlockSpec(memory_space=pltpu.VMEM)
    return pl.pallas_call(
        functools.partial(prepare_kernel, masks, scale),
        in_specs=[anywhere, anywhere, anywhere, inside],
        out_specs=[inside] * count,
        out_shape=[out] * count,
        scratch_shapes=[
            pltpu.VMEM((count, rows, lanes), BF16),
            pltpu.VMEM((count, rows, lanes), BF16),
            pltpu.VMEM((count, rows, lanes), F32),
            pltpu.SemaphoreType.DMA((count, 3)),
        ],
        compiler_params=pltpu.CompilerParams(vmem_limit_bytes=62 * 1024 * 1024),
        cost_estimate=pl.CostEstimate(
            flops=8 * count * rows * lanes, bytes_accessed=12 * count * rows * lanes, transcendentals=0
        ),
    )(inner_gate, signal, taps, gain)


def project_kernel(chunks, members, me, *refs):
    weights, blocks = refs[:members], refs[members : 2 * members]
    gate, upstream, *outs = refs[2 * members :]
    step = pl.program_id(0)
    rows = weights[0].shape[0] // 2
    total = jnp.dot(weights[0][...], blocks[0][...], preferred_element_type=F32)
    for weight, block in zip(weights[1:], blocks[1:]):
        total += jnp.dot(weight[...], block[...], preferred_element_type=F32)
    total = total.astype(BF16)
    upstream[...] = total.reshape(upstream.shape)
    low = elementwise(total[:rows], gate[0])
    high = elementwise(total[rows:], gate[1])
    swapped = (me[0] & 1) == 1
    place = partners(chunks).index
    for pair in range(chunks // 2):

        @pl.when(step == pair)
        def _():
            outs[place(2 * pair)][...] = jnp.where(swapped, high, low)
            outs[place(2 * pair + 1)][...] = jnp.where(swapped, low, high)


def outer_kernel(chunks, me, upstream, *refs):
    chunk, out = refs[:chunks], refs[chunks]
    for d, piece in zip(partners(chunks), chunk):
        at = me[0] ^ d
        out[at] = elementwise(upstream[at], piece[...])


def finish_kernel(count, me, *refs):
    gates, refs = refs[:count], refs[count:]
    values, refs = refs[:count], refs[count:]
    chunk, (grad_inner, grad_signal, grad_taps) = refs[:count], refs[-3:]
    step = pl.program_id(0)
    for k in range(count):

        @pl.when(step == k)
        def _(k=k):
            back = chunk[k][0]
            grad_inner[0] = elementwise(back, values[k][0])
            grad_signal[0] = elementwise(back, gates[k][0])
            grad_taps[0] = chunk[k][1].astype(F32)


def finish_call(me, masks, inner_gate, signal, chunks, earlier):
    count, shape = len(masks), inner_gate.shape
    block = (1,) + shape[1:]

    def place(i, me):
        mask = masks[0]
        for k in range(1, count):
            mask = jnp.where(i == k, masks[k], mask)
        return (me[0] ^ mask, 0, 0)

    gates = [pl.BlockSpec(block, lambda i, me, mask=mask: (me[0] ^ mask, 0, 0)) for mask in masks]
    pieces = [pl.BlockSpec(chunk.shape, lambda i, me: (0, 0, 0)) for chunk in chunks]
    return pl.pallas_call(
        functools.partial(finish_kernel, count),
        grid_spec=pltpu.PrefetchScalarGridSpec(
            num_scalar_prefetch=1,
            grid=(count,),
            in_specs=gates * 2 + pieces + [pl.BlockSpec(memory_space=pl.ANY)] * len(earlier),
            out_specs=[pl.BlockSpec(block, place)] * 3,
        ),
        out_shape=[jax.ShapeDtypeStruct(shape, dtype) for dtype in (BF16, BF16, F32)],
        input_output_aliases={1 + 3 * count + n: n for n in range(len(earlier))},
        compiler_params=pltpu.CompilerParams(vmem_limit_bytes=32 * 1024 * 1024),
        cost_estimate=pl.CostEstimate(
            flops=2 * count * math.prod(shape[1:]),
            bytes_accessed=16 * count * math.prod(shape[1:]),
            transcendentals=0,
        ),
    )(me, *[inner_gate] * count, *[signal] * count, *chunks, *earlier)


def rowwise_call(kernel, me, wholes, pieces, out_shapes, rows, limit=32):
    def spec(shape):
        lead = shape[:-2]
        return pl.BlockSpec(
            lead + (rows, shape[-1]), lambda i, me: (0,) * len(lead) + (i, 0)
        )

    channels = wholes[0].shape[1]
    size = sum(math.prod(x.shape) * x.dtype.itemsize for x in (*wholes, *pieces, *out_shapes))
    return pl.pallas_call(
        kernel,
        grid_spec=pltpu.PrefetchScalarGridSpec(
            num_scalar_prefetch=1,
            grid=(channels // rows,),
            in_specs=[spec(x.shape) for x in (*wholes, *pieces)],
            out_specs=[spec(x.shape) for x in out_shapes],
        ),
        out_shape=out_shapes,
        compiler_params=pltpu.CompilerParams(vmem_limit_bytes=limit * 1024 * 1024),
        cost_estimate=pl.CostEstimate(flops=size, bytes_accessed=size, transcendentals=0),
    )(me, *wholes, *pieces)


def project_call(me, weight, blocks, gate):
    chunks, channels, local = gate.shape
    members, depth = len(blocks), blocks[0].shape[0]

    def pair(i, me):
        return (me[0] >> 1) ^ i

    rows = 2 * channels
    return pl.pallas_call(
        functools.partial(project_kernel, chunks, members),
        grid_spec=pltpu.PrefetchScalarGridSpec(
            num_scalar_prefetch=1,
            grid=(chunks // 2,),
            in_specs=[
                pl.BlockSpec((rows, depth), lambda i, me, j=j: (pair(i, me), me[1] ^ j))
                for j in range(members)
            ]
            + [pl.BlockSpec((depth, local), lambda i, me: (0, 0))] * members
            + [pl.BlockSpec((2, channels, local), lambda i, me: (pair(i, me), 0, 0))],
            out_specs=[pl.BlockSpec((2, channels, local), lambda i, me: (pair(i, me), 0, 0))]
            + [pl.BlockSpec((channels, local), lambda i, me: (0, 0))] * chunks,
        ),
        out_shape=[jax.ShapeDtypeStruct(gate.shape, BF16)]
        + [jax.ShapeDtypeStruct((channels, local), BF16)] * chunks,
        compiler_params=pltpu.CompilerParams(vmem_limit_bytes=40 * 1024 * 1024),
        cost_estimate=pl.CostEstimate(
            flops=2 * weight.size * local, bytes_accessed=2 * weight.size, transcendentals=0
        ),
    )(me, *[weight] * members, *blocks, gate)


def gather_start(block):
    count = lax.axis_size("group")
    return lax.ppermute(block, "group", [(g, g ^ (count // 2)) for g in range(count)])


def gather_rest(block, far, other):
    count = lax.axis_size("group")
    bit = count // 2
    held = {0: block, bit: far}
    bit //= 2
    while bit:
        pairs = [(g, g ^ bit) for g in range(count)]
        for j in list(held):
            sent = held[j]
            if j:
                sent, _ = lax.optimization_barrier((sent, other))
            held[j ^ bit] = lax.ppermute(sent, "group", pairs)
        bit //= 2
    return [held[j] for j in range(count)]


def exchange(parts):
    count = len(parts)
    order = partners(count)
    if count > 8:
        blocks = lax.axis_index("ctx") ^ jnp.arange(count)
        where = np.argsort(order)
        sent = jnp.take(jnp.take(jnp.stack(parts), where, axis=0), blocks, axis=0)
        came = lax.all_to_all(sent, "ctx", split_axis=0, concat_axis=0, tiled=True)
        return list(jnp.take(jnp.take(came, blocks, axis=0), np.array(order), axis=0))
    return [parts[0]] + [
        lax.ppermute(part, "ctx", [(p, p ^ d) for p in range(count)])
        for d, part in zip(order[1:], parts[1:])
    ]


def after(parts, other):
    held, _ = lax.optimization_barrier((parts[0], other))
    return [held] + list(parts[1:])


def per_device(outer_gate, inner_gate, signal, cotangent, out_weight, filter_taps, skip_gain):
    ch_dev, tok_local = outer_gate.shape
    n_ctx = lax.axis_size("ctx")
    ch_slice = ch_dev // n_ctx
    seq_len = n_ctx * tok_local
    inner = seq_len // SLABS
    scale = 1.0 / math.sqrt(seq_len)
    me = jnp.stack([lax.axis_index("ctx"), lax.axis_index("group")])

    def split(array):
        return array.reshape(n_ctx, ch_slice, -1)

    def flat(array):
        return array.reshape(ch_dev, tok_local)

    def shapes(lead, dtype, count):
        return [jax.ShapeDtypeStruct(lead + (ch_slice, tok_local), dtype)] * count

    tables = [jnp.asarray(table) for table in make_tables(inner, n_ctx)]
    tables = [table if table.ndim == 2 else table[me[0]] for table in tables]
    masks = partners(n_ctx)
    first = min(4, n_ctx)
    sources = (scale, split(inner_gate), split(signal), split(filter_taps), split(skip_gain)[:, :, 0])
    head = prepare_call(masks[1:first], *sources)
    cotangent, _ = lax.optimization_barrier((cotangent, head[0]))
    far = gather_start(cotangent)
    own, *rest = prepare_call([0] + masks[first:], *sources)
    pair = exchange([own, *head, *rest])
    gathered = gather_rest(cotangent, far, (pair[1:first], rest[:1]))
    upstream, *grad = project_call(me, out_weight, gathered, split(outer_gate))
    response = conv_call(
        functools.partial(response_kernel, n_ctx, inner), me, (after(pair, grad[0]),), tables, (), inner, 3
    )
    grad[-2:], _ = lax.optimization_barrier((grad[-2:], response[0]))
    grad_came = exchange(grad)
    resp_came = exchange(response)
    backs = conv_call(
        functools.partial(backward_kernel, n_ctx, inner, scale),
        me,
        (pair, after(grad_came, response[0])),
        tables,
        (2,),
        inner,
        5,
    )
    backs_came = exchange(backs)
    (grad_outer,) = rowwise_call(
        functools.partial(outer_kernel, n_ctx),
        me,
        (upstream,),
        after(resp_came, backs[0]),
        shapes((n_ctx,), BF16, 1),
        32,
    )
    outs = []
    cut = n_ctx - 3
    for low, high in ((0, cut), (cut, n_ctx)):
        outs = finish_call(
            me, masks[low:high], split(inner_gate), split(signal), backs_came[low:high], outs
        )
    grad_inner, grad_signal, grad_taps = outs
    return (flat(grad_outer), flat(grad_inner), flat(grad_signal), flat(grad_taps))


def solution(mesh):
    in_specs = (
        P("group", "ctx"),
        P("group", "ctx"),
        P("group", "ctx"),
        P("group", "ctx"),
        P("group", None),
        P("group", "ctx"),
        P("group"),
    )
    out_specs = (P("group", "ctx"), P("group", "ctx"), P("group", "ctx"), P("group", "ctx"))
    return jax.shard_map(
        per_device, mesh=mesh, in_specs=in_specs, out_specs=out_specs, check_vma=False
    )
```

```python
import functools
import math

import jax
import jax.numpy as jnp
import ml_dtypes
import numpy as np
from jax import lax
from jax.experimental import pallas as pl
from jax.experimental.pallas import tpu as pltpu
from jax.sharding import PartitionSpec as P

SLABS = 32
GROUP = 8
STEP = 2 * GROUP
F32 = jnp.float32
BF16 = jnp.bfloat16


def partners(count):
    return [0] + list(reversed(range(1, count)))


def make_tables(inner, chunks):
    slab = np.arange(SLABS)
    freq = np.arange(SLABS) + 0.5
    angle = 2.0 * np.pi / (2 * SLABS) * np.outer(freq, slab)
    eye = np.eye(GROUP)
    first = np.concatenate([np.kron(np.cos(angle), eye), np.kron(-np.sin(angle), eye)], axis=0)
    blocks = first.reshape(first.shape[0], chunks, -1)
    order = np.array(partners(chunks))
    first = np.stack([blocks[:, order ^ p].reshape(first.shape) for p in range(chunks)])
    last = first.transpose(0, 2, 1)
    within = np.arange(inner)
    turn = np.repeat(2.0 * np.pi / (2 * SLABS * inner) * np.outer(freq, within), GROUP, axis=0)
    circle = 2.0 * np.pi / inner * (np.outer(within, within) % inner)
    cos, sin = np.cos(circle), np.sin(circle)
    forward = np.block([[cos, -sin], [sin, cos]])
    narrow = ml_dtypes.bfloat16
    return (
        first.astype(narrow),
        last.astype(narrow),
        np.cos(turn).astype(np.float32),
        np.sin(turn).astype(np.float32),
        forward.astype(narrow),
        forward.T.astype(narrow),
    )


def gather_slabs(blocks, inner):
    local = blocks[0].shape[1]
    wide = [block.astype(F32) for block in blocks]
    halves = []
    for half in range(2):
        rows = slice(half * GROUP, (half + 1) * GROUP)
        pieces = [block[rows, at : at + inner] for block in wide for at in range(0, local, inner)]
        halves.append(jnp.concatenate(pieces, axis=0))
    return jnp.concatenate(halves, axis=1).astype(BF16)


def forward_dft(rows, first, cos, sin, forward, inner):
    stage = jnp.dot(first, rows, preferred_element_type=F32)
    half_rows = SLABS * GROUP
    turned = []
    for half in range(2):
        lanes = slice(half * inner, (half + 1) * inner)
        real, imag = stage[:half_rows, lanes], stage[half_rows:, lanes]
        turned.append(
            jnp.concatenate([real * cos + imag * sin, imag * cos - real * sin], axis=1).astype(BF16)
        )
    spec = jnp.dot(jnp.concatenate(turned, axis=0), forward, preferred_element_type=F32)
    return (spec[:, :inner], spec[:, inner:])


def inverse_dft(spec, last, cos, sin, backward, inner):
    both = jnp.concatenate(spec, axis=1).astype(BF16)
    stage = jnp.dot(both, backward, preferred_element_type=F32)
    half_rows = SLABS * GROUP
    turned = []
    for half in range(2):
        rows = slice(half * half_rows, (half + 1) * half_rows)
        real, imag = stage[rows, :inner], stage[rows, inner:]
        turned.append(
            jnp.concatenate([real * cos - imag * sin, imag * cos + real * sin], axis=0).astype(BF16)
        )
    return jnp.dot(last, jnp.concatenate(turned, axis=1), preferred_element_type=F32)


def scatter_slabs(rows, scale, outs, lead, inner):
    local = outs[0].shape[-1]
    per = local // inner
    scaled = rows * scale
    for src, out in enumerate(outs):
        for part in range(per):
            at = (src * per + part) * GROUP
            tile = jnp.concatenate(
                [scaled[at : at + GROUP, :inner], scaled[at : at + GROUP, inner:]], axis=0
            ).astype(BF16)
            lanes = slice(part * inner, (part + 1) * inner)
            if lead is None:
                out[:, lanes] = tile
            else:
                out[lead, :, lanes] = tile


def times_plain(left, right):
    return (left[0] * right[0] - left[1] * right[1], left[0] * right[1] + left[1] * right[0])


def times_conj(left, right):
    return (left[0] * right[0] + left[1] * right[1], left[1] * right[0] - left[0] * right[1])


def response_kernel(chunks, inner, me, *refs):
    pair, refs = refs[:chunks], refs[chunks:]
    (first, last, cos, sin, forward, backward), outs = refs[:6], refs[6:]
    tables = (first[...], cos[...], sin[...], forward[...], inner)
    prod = forward_dft(gather_slabs([ref[0] for ref in pair], inner), *tables)
    taps = forward_dft(gather_slabs([ref[1] for ref in pair], inner), *tables)
    rows = inverse_dft(times_plain(prod, taps), last[...], cos[...], sin[...], backward[...], inner)
    scatter_slabs(rows, 1.0 / (SLABS * inner), outs, None, inner)


def backward_kernel(chunks, inner, scale, me, *refs):
    pair, grad, refs = refs[:chunks], refs[chunks : 2 * chunks], refs[2 * chunks :]
    (first, last, cos, sin, forward, backward), outs = refs[:6], refs[6:]
    tables = (first[...], cos[...], sin[...], forward[...], inner)
    back_tables = (last[...], cos[...], sin[...], backward[...], inner)
    grad_spec = forward_dft(gather_slabs([ref[...] for ref in grad], inner), *tables)
    taps = forward_dft(gather_slabs([ref[1] for ref in pair], inner), *tables)
    rows = inverse_dft(times_conj(grad_spec, taps), *back_tables)
    scatter_slabs(rows, 1.0 / (SLABS * inner), outs, 0, inner)
    prod = forward_dft(gather_slabs([ref[0] for ref in pair], inner), *tables)
    rows = inverse_dft(times_conj(grad_spec, prod), *back_tables)
    scatter_slabs(rows, scale / (SLABS * inner), outs, 1, inner)


def conv_call(kernel, me, operands, tables, lead, inner, transforms):
    chunks, shape = len(operands[0]), operands[0][0].shape
    channels, local = shape[-2:]
    def rows_of(shape):
        middle = shape[:-2]
        return pl.BlockSpec(
            middle + (STEP, local), lambda i, me: (0,) * len(middle) + (i, 0)
        )

    def whole(table):
        return pl.BlockSpec(table.shape, lambda i, me: (0, 0))

    out_shape = lead + (channels, local)
    rows = channels * SLABS
    flops = transforms * rows * (2 * (2 * inner) ** 2 + 4 * SLABS * GROUP * inner)
    flat = [chunk for operand in operands for chunk in operand]
    return pl.pallas_call(
        kernel,
        grid_spec=pltpu.PrefetchScalarGridSpec(
            num_scalar_prefetch=1,
            grid=(channels // STEP,),
            in_specs=[rows_of(chunk.shape) for chunk in flat] + [whole(t) for t in tables],
            out_specs=[rows_of(out_shape)] * chunks,
        ),
        out_shape=[jax.ShapeDtypeStruct(out_shape, BF16)] * chunks,
        compiler_params=pltpu.CompilerParams(vmem_limit_bytes=40 * 1024 * 1024),
        cost_estimate=pl.CostEstimate(
            flops=flops, bytes_accessed=2 * rows * inner * 4, transcendentals=0
        ),
    )(me, *flat, *tables)


def elementwise(left, right):
    return (left.astype(F32) * right.astype(F32)).astype(BF16)


def prepare_kernel(masks, scale, inner_gate, signal, taps, gain, *refs):
    count = len(masks)
    outs, (gates, values, filters, sems) = refs[:count], refs[count:]
    me = lax.axis_index("ctx")
    copies = []
    for k, mask in enumerate(masks):
        at = me ^ mask
        pairs = ((inner_gate, gates), (signal, values), (taps, filters))
        copies.append(
            [
                pltpu.make_async_copy(src.at[at], dst.at[k], sems.at[k, n])
                for n, (src, dst) in enumerate(pairs)
            ]
        )
    for group in copies:
        for copy in group:
            copy.start()
    rows, lanes = gates.shape[1], gain.shape[1]
    shape = (rows, lanes)
    diagonal = lax.broadcasted_iota(jnp.int32, shape, 0) == lax.broadcasted_iota(jnp.int32, shape, 1)
    at_zero = (me == 0) & (lax.broadcasted_iota(jnp.int32, filters.shape[1:], 1) == 0)
    for k, (mask, group, out) in enumerate(zip(masks, copies, outs)):
        row = gain[pl.ds(me ^ mask, 1), :]
        column = jnp.sum(jnp.where(diagonal, row, 0.0), axis=1, keepdims=True)
        for copy in group:
            copy.wait()
        out[0] = elementwise(gates[k], values[k])
        out[1] = (filters[k] * scale + jnp.where(at_zero, column, 0.0)).astype(BF16)


def prepare_call(masks, scale, inner_gate, signal, taps, gain):
    count, (rows, lanes) = len(masks), taps.shape[1:]
    out = jax.ShapeDtypeStruct((2, rows, lanes), BF16)
    anywhere = pl.BlockSpec(memory_space=pl.ANY)
    inside = pl.BlockSpec(memory_space=pltpu.VMEM)
    return pl.pallas_call(
        functools.partial(prepare_kernel, masks, scale),
        in_specs=[anywhere, anywhere, anywhere, inside],
        out_specs=[inside] * count,
        out_shape=[out] * count,
        scratch_shapes=[
            pltpu.VMEM((count, rows, lanes), BF16),
            pltpu.VMEM((count, rows, lanes), BF16),
            pltpu.VMEM((count, rows, lanes), F32),
            pltpu.SemaphoreType.DMA((count, 3)),
        ],
        compiler_params=pltpu.CompilerParams(vmem_limit_bytes=62 * 1024 * 1024),
        cost_estimate=pl.CostEstimate(
            flops=8 * count * rows * lanes, bytes_accessed=12 * count * rows * lanes, transcendentals=0
        ),
    )(inner_gate, signal, taps, gain)


def project_kernel(chunks, members, me, *refs):
    weights, blocks = refs[:members], refs[members : 2 * members]
    gate, upstream, *outs = refs[2 * members :]
    step = pl.program_id(0)
    rows = weights[0].shape[0] // 2
    total = jnp.dot(weights[0][...], blocks[0][...], preferred_element_type=F32)
    for weight, block in zip(weights[1:], blocks[1:]):
        total += jnp.dot(weight[...], block[...], preferred_element_type=F32)
    total = total.astype(BF16)
    upstream[...] = total.reshape(upstream.shape)
    low = elementwise(total[:rows], gate[0])
    high = elementwise(total[rows:], gate[1])
    swapped = (me[0] & 1) == 1
    place = partners(chunks).index
    for pair in range(chunks // 2):

        @pl.when(step == pair)
        def _():
            outs[place(2 * pair)][...] = jnp.where(swapped, high, low)
            outs[place(2 * pair + 1)][...] = jnp.where(swapped, low, high)


def outer_kernel(chunks, me, upstream, *refs):
    chunk, out = refs[:chunks], refs[chunks]
    for d, piece in zip(partners(chunks), chunk):
        at = me[0] ^ d
        out[at] = elementwise(upstream[at], piece[...])


def finish_kernel(count, me, *refs):
    gates, refs = refs[:count], refs[count:]
    values, refs = refs[:count], refs[count:]
    chunk, (grad_inner, grad_signal, grad_taps) = refs[:count], refs[-3:]
    step = pl.program_id(0)
    for k in range(count):

        @pl.when(step == k)
        def _(k=k):
            back = chunk[k][0]
            grad_inner[0] = elementwise(back, values[k][0])
            grad_signal[0] = elementwise(back, gates[k][0])
            grad_taps[0] = chunk[k][1].astype(F32)


def finish_call(me, masks, inner_gate, signal, chunks, earlier):
    count, shape = len(masks), inner_gate.shape
    block = (1,) + shape[1:]

    def place(i, me):
        mask = masks[0]
        for k in range(1, count):
            mask = jnp.where(i == k, masks[k], mask)
        return (me[0] ^ mask, 0, 0)

    gates = [pl.BlockSpec(block, lambda i, me, mask=mask: (me[0] ^ mask, 0, 0)) for mask in masks]
    pieces = [pl.BlockSpec(chunk.shape, lambda i, me: (0, 0, 0)) for chunk in chunks]
    return pl.pallas_call(
        functools.partial(finish_kernel, count),
        grid_spec=pltpu.PrefetchScalarGridSpec(
            num_scalar_prefetch=1,
            grid=(count,),
            in_specs=gates * 2 + pieces + [pl.BlockSpec(memory_space=pl.ANY)] * len(earlier),
            out_specs=[pl.BlockSpec(block, place)] * 3,
        ),
        out_shape=[jax.ShapeDtypeStruct(shape, dtype) for dtype in (BF16, BF16, F32)],
        input_output_aliases={1 + 3 * count + n: n for n in range(len(earlier))},
        compiler_params=pltpu.CompilerParams(vmem_limit_bytes=32 * 1024 * 1024),
        cost_estimate=pl.CostEstimate(
            flops=2 * count * math.prod(shape[1:]),
            bytes_accessed=16 * count * math.prod(shape[1:]),
            transcendentals=0,
        ),
    )(me, *[inner_gate] * count, *[signal] * count, *chunks, *earlier)


def rowwise_call(kernel, me, wholes, pieces, out_shapes, rows, limit=32):
    def spec(shape):
        lead = shape[:-2]
        return pl.BlockSpec(
            lead + (rows, shape[-1]), lambda i, me: (0,) * len(lead) + (i, 0)
        )

    channels = wholes[0].shape[1]
    size = sum(math.prod(x.shape) * x.dtype.itemsize for x in (*wholes, *pieces, *out_shapes))
    return pl.pallas_call(
        kernel,
        grid_spec=pltpu.PrefetchScalarGridSpec(
            num_scalar_prefetch=1,
            grid=(channels // rows,),
            in_specs=[spec(x.shape) for x in (*wholes, *pieces)],
            out_specs=[spec(x.shape) for x in out_shapes],
        ),
        out_shape=out_shapes,
        compiler_params=pltpu.CompilerParams(vmem_limit_bytes=limit * 1024 * 1024),
        cost_estimate=pl.CostEstimate(flops=size, bytes_accessed=size, transcendentals=0),
    )(me, *wholes, *pieces)


def project_call(me, weight, blocks, gate):
    chunks, channels, local = gate.shape
    members, depth = len(blocks), blocks[0].shape[0]

    def pair(i, me):
        return (me[0] >> 1) ^ i

    rows = 2 * channels
    return pl.pallas_call(
        functools.partial(project_kernel, chunks, members),
        grid_spec=pltpu.PrefetchScalarGridSpec(
            num_scalar_prefetch=1,
            grid=(chunks // 2,),
            in_specs=[
                pl.BlockSpec((rows, depth), lambda i, me, j=j: (pair(i, me), me[1] ^ j))
                for j in range(members)
            ]
            + [pl.BlockSpec((depth, local), lambda i, me: (0, 0))] * members
            + [pl.BlockSpec((2, channels, local), lambda i, me: (pair(i, me), 0, 0))],
            out_specs=[pl.BlockSpec((2, channels, local), lambda i, me: (pair(i, me), 0, 0))]
            + [pl.BlockSpec((channels, local), lambda i, me: (0, 0))] * chunks,
        ),
        out_shape=[jax.ShapeDtypeStruct(gate.shape, BF16)]
        + [jax.ShapeDtypeStruct((channels, local), BF16)] * chunks,
        compiler_params=pltpu.CompilerParams(vmem_limit_bytes=40 * 1024 * 1024),
        cost_estimate=pl.CostEstimate(
            flops=2 * weight.size * local, bytes_accessed=2 * weight.size, transcendentals=0
        ),
    )(me, *[weight] * members, *blocks, gate)


def gather_start(block):
    count = lax.axis_size("group")
    return lax.ppermute(block, "group", [(g, g ^ (count // 2)) for g in range(count)])


def gather_rest(block, far, other):
    count = lax.axis_size("group")
    bit = count // 2
    held = {0: block, bit: far}
    bit //= 2
    while bit:
        pairs = [(g, g ^ bit) for g in range(count)]
        for j in list(held):
            sent = held[j]
            if j:
                sent, _ = lax.optimization_barrier((sent, other))
            held[j ^ bit] = lax.ppermute(sent, "group", pairs)
        bit //= 2
    return [held[j] for j in range(count)]


def exchange(parts):
    count = len(parts)
    order = partners(count)
    if count > 8:
        blocks = lax.axis_index("ctx") ^ jnp.arange(count)
        where = np.argsort(order)
        sent = jnp.take(jnp.take(jnp.stack(parts), where, axis=0), blocks, axis=0)
        came = lax.all_to_all(sent, "ctx", split_axis=0, concat_axis=0, tiled=True)
        return list(jnp.take(jnp.take(came, blocks, axis=0), np.array(order), axis=0))
    return [parts[0]] + [
        lax.ppermute(part, "ctx", [(p, p ^ d) for p in range(count)])
        for d, part in zip(order[1:], parts[1:])
    ]


def after(parts, other):
    held, _ = lax.optimization_barrier((parts[0], other))
    return [held] + list(parts[1:])


def per_device(outer_gate, inner_gate, signal, cotangent, out_weight, filter_taps, skip_gain):
    ch_dev, tok_local = outer_gate.shape
    n_ctx = lax.axis_size("ctx")
    ch_slice = ch_dev // n_ctx
    seq_len = n_ctx * tok_local
    inner = seq_len // SLABS
    scale = 1.0 / math.sqrt(seq_len)
    me = jnp.stack([lax.axis_index("ctx"), lax.axis_index("group")])

    def split(array):
        return array.reshape(n_ctx, ch_slice, -1)

    def flat(array):
        return array.reshape(ch_dev, tok_local)

    def shapes(lead, dtype, count):
        return [jax.ShapeDtypeStruct(lead + (ch_slice, tok_local), dtype)] * count

    tables = [jnp.asarray(table) for table in make_tables(inner, n_ctx)]
    tables = [table if table.ndim == 2 else table[me[0]] for table in tables]
    masks = partners(n_ctx)
    first = min(3, n_ctx)
    sources = (scale, split(inner_gate), split(signal), split(filter_taps), split(skip_gain)[:, :, 0])
    head = prepare_call(masks[1:first], *sources)
    cotangent, _ = lax.optimization_barrier((cotangent, head[0]))
    far = gather_start(cotangent)
    own, *rest = prepare_call([0] + masks[first:], *sources)
    pair = exchange([own, *head, *rest])
    gathered = gather_rest(cotangent, far, (pair[1:first], rest[:1]))
    gathered = after(gathered, pair[-3:-1])
    upstream, *grad = project_call(me, out_weight, gathered, split(outer_gate))
    response = conv_call(
        functools.partial(response_kernel, n_ctx, inner), me, (after(pair, grad[0]),), tables, (), inner, 3
    )
    grad[-2:], _ = lax.optimization_barrier((grad[-2:], response[0]))
    grad_came = exchange(grad)
    resp_came = exchange(response)
    backs = conv_call(
        functools.partial(backward_kernel, n_ctx, inner, scale),
        me,
        (pair, after(grad_came, response[0])),
        tables,
        (2,),
        inner,
        5,
    )
    backs_came = exchange(backs)
    (grad_outer,) = rowwise_call(
        functools.partial(outer_kernel, n_ctx),
        me,
        (upstream,),
        after(resp_came, backs[0]),
        shapes((n_ctx,), BF16, 1),
        32,
    )
    outs = []
    last = range(3, 5)
    for part in ([k for k in range(n_ctx) if k not in last], last):
        outs = finish_call(
            me,
            [masks[k] for k in part],
            split(inner_gate),
            split(signal),
            [backs_came[k] for k in part],
            outs,
        )
    grad_inner, grad_signal, grad_taps = outs
    return (flat(grad_outer), flat(grad_inner), flat(grad_signal), flat(grad_taps))


def solution(mesh):
    in_specs = (
        P("group", "ctx"),
        P("group", "ctx"),
        P("group", "ctx"),
        P("group", "ctx"),
        P("group", None),
        P("group", "ctx"),
        P("group"),
    )
    out_specs = (P("group", "ctx"), P("group", "ctx"), P("group", "ctx"), P("group", "ctx"))
    return jax.shard_map(
        per_device, mesh=mesh, in_specs=in_specs, out_specs=out_specs, check_vma=False
    )
```

```python
import functools
import math

import jax
import jax.numpy as jnp
import ml_dtypes
import numpy as np
from jax import lax
from jax.experimental import pallas as pl
from jax.experimental.pallas import tpu as pltpu
from jax.sharding import PartitionSpec as P

SLABS = 32
GROUP = 8
STEP = 2 * GROUP
F32 = jnp.float32
BF16 = jnp.bfloat16


def partners(count):
    return [0] + list(reversed(range(1, count)))


def make_tables(inner, chunks):
    slab = np.arange(SLABS)
    freq = np.arange(SLABS) + 0.5
    angle = 2.0 * np.pi / (2 * SLABS) * np.outer(freq, slab)
    eye = np.eye(GROUP)
    first = np.concatenate([np.kron(np.cos(angle), eye), np.kron(-np.sin(angle), eye)], axis=0)
    blocks = first.reshape(first.shape[0], chunks, -1)
    order = np.array(partners(chunks))
    first = np.stack([blocks[:, order ^ p].reshape(first.shape) for p in range(chunks)])
    last = first.transpose(0, 2, 1)
    within = np.arange(inner)
    turn = np.repeat(2.0 * np.pi / (2 * SLABS * inner) * np.outer(freq, within), GROUP, axis=0)
    circle = 2.0 * np.pi / inner * (np.outer(within, within) % inner)
    cos, sin = np.cos(circle), np.sin(circle)
    forward = np.block([[cos, -sin], [sin, cos]])
    narrow = ml_dtypes.bfloat16
    return (
        first.astype(narrow),
        last.astype(narrow),
        np.cos(turn).astype(np.float32),
        np.sin(turn).astype(np.float32),
        forward.astype(narrow),
        forward.T.astype(narrow),
    )


def gather_slabs(blocks, inner):
    local = blocks[0].shape[1]
    wide = [block.astype(F32) for block in blocks]
    halves = []
    for half in range(2):
        rows = slice(half * GROUP, (half + 1) * GROUP)
        pieces = [block[rows, at : at + inner] for block in wide for at in range(0, local, inner)]
        halves.append(jnp.concatenate(pieces, axis=0))
    return jnp.concatenate(halves, axis=1).astype(BF16)


def forward_dft(rows, first, cos, sin, forward, inner):
    stage = jnp.dot(first, rows, preferred_element_type=F32)
    half_rows = SLABS * GROUP
    turned = []
    for half in range(2):
        lanes = slice(half * inner, (half + 1) * inner)
        real, imag = stage[:half_rows, lanes], stage[half_rows:, lanes]
        turned.append(
            jnp.concatenate([real * cos + imag * sin, imag * cos - real * sin], axis=1).astype(BF16)
        )
    spec = jnp.dot(jnp.concatenate(turned, axis=0), forward, preferred_element_type=F32)
    return (spec[:, :inner], spec[:, inner:])


def inverse_dft(spec, last, cos, sin, backward, inner):
    both = jnp.concatenate(spec, axis=1).astype(BF16)
    stage = jnp.dot(both, backward, preferred_element_type=F32)
    half_rows = SLABS * GROUP
    turned = []
    for half in range(2):
        rows = slice(half * half_rows, (half + 1) * half_rows)
        real, imag = stage[rows, :inner], stage[rows, inner:]
        turned.append(
            jnp.concatenate([real * cos - imag * sin, imag * cos + real * sin], axis=0).astype(BF16)
        )
    return jnp.dot(last, jnp.concatenate(turned, axis=1), preferred_element_type=F32)


def scatter_slabs(rows, scale, outs, lead, inner):
    local = outs[0].shape[-1]
    per = local // inner
    scaled = rows * scale
    for src, out in enumerate(outs):
        for part in range(per):
            at = (src * per + part) * GROUP
            tile = jnp.concatenate(
                [scaled[at : at + GROUP, :inner], scaled[at : at + GROUP, inner:]], axis=0
            ).astype(BF16)
            lanes = slice(part * inner, (part + 1) * inner)
            if lead is None:
                out[:, lanes] = tile
            else:
                out[lead, :, lanes] = tile


def times_plain(left, right):
    return (left[0] * right[0] - left[1] * right[1], left[0] * right[1] + left[1] * right[0])


def times_conj(left, right):
    return (left[0] * right[0] + left[1] * right[1], left[1] * right[0] - left[0] * right[1])


def response_kernel(chunks, inner, me, *refs):
    pair, refs = refs[:chunks], refs[chunks:]
    (first, last, cos, sin, forward, backward), outs = refs[:6], refs[6:]
    tables = (first[...], cos[...], sin[...], forward[...], inner)
    prod = forward_dft(gather_slabs([ref[0] for ref in pair], inner), *tables)
    taps = forward_dft(gather_slabs([ref[1] for ref in pair], inner), *tables)
    rows = inverse_dft(times_plain(prod, taps), last[...], cos[...], sin[...], backward[...], inner)
    scatter_slabs(rows, 1.0 / (SLABS * inner), outs, None, inner)


def backward_kernel(chunks, inner, scale, me, *refs):
    pair, grad, refs = refs[:chunks], refs[chunks : 2 * chunks], refs[2 * chunks :]
    (first, last, cos, sin, forward, backward), outs = refs[:6], refs[6:]
    tables = (first[...], cos[...], sin[...], forward[...], inner)
    back_tables = (last[...], cos[...], sin[...], backward[...], inner)
    grad_spec = forward_dft(gather_slabs([ref[...] for ref in grad], inner), *tables)
    taps = forward_dft(gather_slabs([ref[1] for ref in pair], inner), *tables)
    rows = inverse_dft(times_conj(grad_spec, taps), *back_tables)
    scatter_slabs(rows, 1.0 / (SLABS * inner), outs, 0, inner)
    prod = forward_dft(gather_slabs([ref[0] for ref in pair], inner), *tables)
    rows = inverse_dft(times_conj(grad_spec, prod), *back_tables)
    scatter_slabs(rows, scale / (SLABS * inner), outs, 1, inner)


def conv_call(kernel, me, operands, tables, lead, inner, transforms):
    chunks, shape = len(operands[0]), operands[0][0].shape
    channels, local = shape[-2:]
    def rows_of(shape):
        middle = shape[:-2]
        return pl.BlockSpec(
            middle + (STEP, local), lambda i, me: (0,) * len(middle) + (i, 0)
        )

    def whole(table):
        return pl.BlockSpec(table.shape, lambda i, me: (0, 0))

    out_shape = lead + (channels, local)
    rows = channels * SLABS
    flops = transforms * rows * (2 * (2 * inner) ** 2 + 4 * SLABS * GROUP * inner)
    flat = [chunk for operand in operands for chunk in operand]
    return pl.pallas_call(
        kernel,
        grid_spec=pltpu.PrefetchScalarGridSpec(
            num_scalar_prefetch=1,
            grid=(channels // STEP,),
            in_specs=[rows_of(chunk.shape) for chunk in flat] + [whole(t) for t in tables],
            out_specs=[rows_of(out_shape)] * chunks,
        ),
        out_shape=[jax.ShapeDtypeStruct(out_shape, BF16)] * chunks,
        compiler_params=pltpu.CompilerParams(vmem_limit_bytes=40 * 1024 * 1024),
        cost_estimate=pl.CostEstimate(
            flops=flops, bytes_accessed=2 * rows * inner * 4, transcendentals=0
        ),
    )(me, *flat, *tables)


def elementwise(left, right):
    return (left.astype(F32) * right.astype(F32)).astype(BF16)


def prepare_kernel(masks, scale, inner_gate, signal, taps, gain, *refs):
    count = len(masks)
    outs, (gates, values, filters, sems) = refs[:count], refs[count:]
    me = lax.axis_index("ctx")
    copies = []
    for k, mask in enumerate(masks):
        at = me ^ mask
        pairs = ((inner_gate, gates), (signal, values), (taps, filters))
        copies.append(
            [
                pltpu.make_async_copy(src.at[at], dst.at[k], sems.at[k, n])
                for n, (src, dst) in enumerate(pairs)
            ]
        )
    for group in copies:
        for copy in group:
            copy.start()
    rows, lanes = gates.shape[1], gain.shape[1]
    shape = (rows, lanes)
    diagonal = lax.broadcasted_iota(jnp.int32, shape, 0) == lax.broadcasted_iota(jnp.int32, shape, 1)
    at_zero = (me == 0) & (lax.broadcasted_iota(jnp.int32, filters.shape[1:], 1) == 0)
    for k, (mask, group, out) in enumerate(zip(masks, copies, outs)):
        row = gain[pl.ds(me ^ mask, 1), :]
        column = jnp.sum(jnp.where(diagonal, row, 0.0), axis=1, keepdims=True)
        for copy in group:
            copy.wait()
        out[0] = elementwise(gates[k], values[k])
        out[1] = (filters[k] * scale + jnp.where(at_zero, column, 0.0)).astype(BF16)


def prepare_call(masks, scale, inner_gate, signal, taps, gain):
    count, (rows, lanes) = len(masks), taps.shape[1:]
    out = jax.ShapeDtypeStruct((2, rows, lanes), BF16)
    anywhere = pl.BlockSpec(memory_space=pl.ANY)
    inside = pl.BlockSpec(memory_space=pltpu.VMEM)
    return pl.pallas_call(
        functools.partial(prepare_kernel, masks, scale),
        in_specs=[anywhere, anywhere, anywhere, inside],
        out_specs=[inside] * count,
        out_shape=[out] * count,
        scratch_shapes=[
            pltpu.VMEM((count, rows, lanes), BF16),
            pltpu.VMEM((count, rows, lanes), BF16),
            pltpu.VMEM((count, rows, lanes), F32),
            pltpu.SemaphoreType.DMA((count, 3)),
        ],
        compiler_params=pltpu.CompilerParams(vmem_limit_bytes=62 * 1024 * 1024),
        cost_estimate=pl.CostEstimate(
            flops=8 * count * rows * lanes, bytes_accessed=12 * count * rows * lanes, transcendentals=0
        ),
    )(inner_gate, signal, taps, gain)


def project_kernel(chunks, members, me, *refs):
    weights, blocks = refs[:members], refs[members : 2 * members]
    gate, upstream, *outs = refs[2 * members :]
    step = pl.program_id(0)
    rows = weights[0].shape[0] // 2
    total = jnp.dot(weights[0][...], blocks[0][...], preferred_element_type=F32)
    for weight, block in zip(weights[1:], blocks[1:]):
        total += jnp.dot(weight[...], block[...], preferred_element_type=F32)
    total = total.astype(BF16)
    upstream[...] = total.reshape(upstream.shape)
    low = elementwise(total[:rows], gate[0])
    high = elementwise(total[rows:], gate[1])
    swapped = (me[0] & 1) == 1
    place = partners(chunks).index
    for pair in range(chunks // 2):

        @pl.when(step == pair)
        def _():
            outs[place(2 * pair)][...] = jnp.where(swapped, high, low)
            outs[place(2 * pair + 1)][...] = jnp.where(swapped, low, high)


def outer_kernel(chunks, me, upstream, *refs):
    chunk, out = refs[:chunks], refs[chunks]
    for d, piece in zip(partners(chunks), chunk):
        at = me[0] ^ d
        out[at] = elementwise(upstream[at], piece[...])


def finish_kernel(count, me, *refs):
    gates, refs = refs[:count], refs[count:]
    values, refs = refs[:count], refs[count:]
    chunk, (grad_inner, grad_signal, grad_taps) = refs[:count], refs[-3:]
    step = pl.program_id(0)
    for k in range(count):

        @pl.when(step == k)
        def _(k=k):
            back = chunk[k][0]
            grad_inner[0] = elementwise(back, values[k][0])
            grad_signal[0] = elementwise(back, gates[k][0])
            grad_taps[0] = chunk[k][1].astype(F32)


def finish_call(me, masks, inner_gate, signal, chunks, earlier):
    count, shape = len(masks), inner_gate.shape
    block = (1,) + shape[1:]

    def place(i, me):
        mask = masks[0]
        for k in range(1, count):
            mask = jnp.where(i == k, masks[k], mask)
        return (me[0] ^ mask, 0, 0)

    gates = [pl.BlockSpec(block, lambda i, me, mask=mask: (me[0] ^ mask, 0, 0)) for mask in masks]
    pieces = [pl.BlockSpec(chunk.shape, lambda i, me: (0, 0, 0)) for chunk in chunks]
    return pl.pallas_call(
        functools.partial(finish_kernel, count),
        grid_spec=pltpu.PrefetchScalarGridSpec(
            num_scalar_prefetch=1,
            grid=(count,),
            in_specs=gates * 2 + pieces + [pl.BlockSpec(memory_space=pl.ANY)] * len(earlier),
            out_specs=[pl.BlockSpec(block, place)] * 3,
        ),
        out_shape=[jax.ShapeDtypeStruct(shape, dtype) for dtype in (BF16, BF16, F32)],
        input_output_aliases={1 + 3 * count + n: n for n in range(len(earlier))},
        compiler_params=pltpu.CompilerParams(vmem_limit_bytes=32 * 1024 * 1024),
        cost_estimate=pl.CostEstimate(
            flops=2 * count * math.prod(shape[1:]),
            bytes_accessed=16 * count * math.prod(shape[1:]),
            transcendentals=0,
        ),
    )(me, *[inner_gate] * count, *[signal] * count, *chunks, *earlier)


def rowwise_call(kernel, me, wholes, pieces, out_shapes, rows, limit=32):
    def spec(shape):
        lead = shape[:-2]
        return pl.BlockSpec(
            lead + (rows, shape[-1]), lambda i, me: (0,) * len(lead) + (i, 0)
        )

    channels = wholes[0].shape[1]
    size = sum(math.prod(x.shape) * x.dtype.itemsize for x in (*wholes, *pieces, *out_shapes))
    return pl.pallas_call(
        kernel,
        grid_spec=pltpu.PrefetchScalarGridSpec(
            num_scalar_prefetch=1,
            grid=(channels // rows,),
            in_specs=[spec(x.shape) for x in (*wholes, *pieces)],
            out_specs=[spec(x.shape) for x in out_shapes],
        ),
        out_shape=out_shapes,
        compiler_params=pltpu.CompilerParams(vmem_limit_bytes=limit * 1024 * 1024),
        cost_estimate=pl.CostEstimate(flops=size, bytes_accessed=size, transcendentals=0),
    )(me, *wholes, *pieces)


def project_call(me, weight, blocks, gate):
    chunks, channels, local = gate.shape
    members, depth = len(blocks), blocks[0].shape[0]

    def pair(i, me):
        return (me[0] >> 1) ^ i

    rows = 2 * channels
    return pl.pallas_call(
        functools.partial(project_kernel, chunks, members),
        grid_spec=pltpu.PrefetchScalarGridSpec(
            num_scalar_prefetch=1,
            grid=(chunks // 2,),
            in_specs=[
                pl.BlockSpec((rows, depth), lambda i, me, j=j: (pair(i, me), me[1] ^ j))
                for j in range(members)
            ]
            + [pl.BlockSpec((depth, local), lambda i, me: (0, 0))] * members
            + [pl.BlockSpec((2, channels, local), lambda i, me: (pair(i, me), 0, 0))],
            out_specs=[pl.BlockSpec((2, channels, local), lambda i, me: (pair(i, me), 0, 0))]
            + [pl.BlockSpec((channels, local), lambda i, me: (0, 0))] * chunks,
        ),
        out_shape=[jax.ShapeDtypeStruct(gate.shape, BF16)]
        + [jax.ShapeDtypeStruct((channels, local), BF16)] * chunks,
        compiler_params=pltpu.CompilerParams(vmem_limit_bytes=40 * 1024 * 1024),
        cost_estimate=pl.CostEstimate(
            flops=2 * weight.size * local, bytes_accessed=2 * weight.size, transcendentals=0
        ),
    )(me, *[weight] * members, *blocks, gate)


def gather_start(block):
    count = lax.axis_size("group")
    return lax.ppermute(block, "group", [(g, g ^ (count // 2)) for g in range(count)])


def gather_rest(block, far, other):
    count = lax.axis_size("group")
    bit = count // 2
    held = {0: block, bit: far}
    bit //= 2
    while bit:
        pairs = [(g, g ^ bit) for g in range(count)]
        for j in list(held):
            sent = held[j]
            if j:
                sent, _ = lax.optimization_barrier((sent, other))
            held[j ^ bit] = lax.ppermute(sent, "group", pairs)
        bit //= 2
    return [held[j] for j in range(count)]


def send(part, d, count):
    return lax.ppermute(part, "ctx", [(p, p ^ d) for p in range(count)])


def exchange(parts):
    count = len(parts)
    order = partners(count)
    if count > 8:
        blocks = lax.axis_index("ctx") ^ jnp.arange(count)
        where = np.argsort(order)
        sent = jnp.take(jnp.take(jnp.stack(parts), where, axis=0), blocks, axis=0)
        came = lax.all_to_all(sent, "ctx", split_axis=0, concat_axis=0, tiled=True)
        return list(jnp.take(jnp.take(came, blocks, axis=0), np.array(order), axis=0))
    return [parts[0]] + [send(part, d, count) for d, part in zip(order[1:], parts[1:])]


def after(parts, other):
    held, _ = lax.optimization_barrier((parts[0], other))
    return [held] + list(parts[1:])


def per_device(outer_gate, inner_gate, signal, cotangent, out_weight, filter_taps, skip_gain):
    ch_dev, tok_local = outer_gate.shape
    n_ctx = lax.axis_size("ctx")
    ch_slice = ch_dev // n_ctx
    seq_len = n_ctx * tok_local
    inner = seq_len // SLABS
    scale = 1.0 / math.sqrt(seq_len)
    me = jnp.stack([lax.axis_index("ctx"), lax.axis_index("group")])

    def split(array):
        return array.reshape(n_ctx, ch_slice, -1)

    def flat(array):
        return array.reshape(ch_dev, tok_local)

    def shapes(lead, dtype, count):
        return [jax.ShapeDtypeStruct(lead + (ch_slice, tok_local), dtype)] * count

    tables = [jnp.asarray(table) for table in make_tables(inner, n_ctx)]
    tables = [table if table.ndim == 2 else table[me[0]] for table in tables]
    masks = partners(n_ctx)
    first = min(3, n_ctx)
    sources = (scale, split(inner_gate), split(signal), split(filter_taps), split(skip_gain)[:, :, 0])
    head = prepare_call(masks[1:first], *sources)
    cotangent, _ = lax.optimization_barrier((cotangent, head[0]))
    far = gather_start(cotangent)
    own, *rest = prepare_call([0] + masks[first:], *sources)
    parts = [own, *head, *rest]
    held = 4 <= n_ctx <= 8
    near = slice(n_ctx // 2 + 1, n_ctx - 1)
    if held:
        pair = list(parts)
        for k in (*range(1, near.start), n_ctx - 1):
            pair[k] = send(parts[k], masks[k], n_ctx)
    else:
        pair = exchange(parts)
    gathered = gather_rest(cotangent, far, (pair[1:first], pair[-1:], rest[:1]))
    upstream, *grad = project_call(me, out_weight, gathered, split(outer_gate))
    if held:
        waiting, _ = lax.optimization_barrier((parts[near], grad[0]))
        pair[near] = [send(part, d, n_ctx) for d, part in zip(masks[near], waiting)]
    response = conv_call(
        functools.partial(response_kernel, n_ctx, inner), me, (after(pair, grad[0]),), tables, (), inner, 3
    )
    grad[-2:], _ = lax.optimization_barrier((grad[-2:], response[0]))
    grad_came = exchange(grad)
    resp_came = exchange(response)
    backs = conv_call(
        functools.partial(backward_kernel, n_ctx, inner, scale),
        me,
        (pair, after(grad_came, response[0])),
        tables,
        (2,),
        inner,
        5,
    )
    backs_came = exchange(backs)
    (grad_outer,) = rowwise_call(
        functools.partial(outer_kernel, n_ctx),
        me,
        (upstream,),
        after(resp_came, backs[0]),
        shapes((n_ctx,), BF16, 1),
        32,
    )
    outs = []
    last = range(3, 5)
    for part in ([k for k in range(n_ctx) if k not in last], last):
        outs = finish_call(
            me,
            [masks[k] for k in part],
            split(inner_gate),
            split(signal),
            [backs_came[k] for k in part],
            outs,
        )
    grad_inner, grad_signal, grad_taps = outs
    return (flat(grad_outer), flat(grad_inner), flat(grad_signal), flat(grad_taps))


def solution(mesh):
    in_specs = (
        P("group", "ctx"),
        P("group", "ctx"),
        P("group", "ctx"),
        P("group", "ctx"),
        P("group", None),
        P("group", "ctx"),
        P("group"),
    )
    out_specs = (P("group", "ctx"), P("group", "ctx"), P("group", "ctx"), P("group", "ctx"))
    return jax.shard_map(
        per_device, mesh=mesh, in_specs=in_specs, out_specs=out_specs, check_vma=False
    )
```

```python
import functools
import math

import jax
import jax.numpy as jnp
import ml_dtypes
import numpy as np
from jax import lax
from jax.experimental import pallas as pl
from jax.experimental.pallas import tpu as pltpu
from jax.sharding import PartitionSpec as P

SLABS = 32
GROUP = 8
STEP = 2 * GROUP
F32 = jnp.float32
BF16 = jnp.bfloat16


def partners(count):
    return [0] + list(reversed(range(1, count)))


def make_tables(inner, chunks):
    slab = np.arange(SLABS)
    freq = np.arange(SLABS) + 0.5
    angle = 2.0 * np.pi / (2 * SLABS) * np.outer(freq, slab)
    eye = np.eye(GROUP)
    first = np.concatenate([np.kron(np.cos(angle), eye), np.kron(-np.sin(angle), eye)], axis=0)
    blocks = first.reshape(first.shape[0], chunks, -1)
    order = np.array(partners(chunks))
    first = np.stack([blocks[:, order ^ p].reshape(first.shape) for p in range(chunks)])
    last = first.transpose(0, 2, 1)
    within = np.arange(inner)
    turn = np.repeat(2.0 * np.pi / (2 * SLABS * inner) * np.outer(freq, within), GROUP, axis=0)
    circle = 2.0 * np.pi / inner * (np.outer(within, within) % inner)
    cos, sin = np.cos(circle), np.sin(circle)
    forward = np.block([[cos, -sin], [sin, cos]])
    narrow = ml_dtypes.bfloat16
    return (
        first.astype(narrow),
        last.astype(narrow),
        np.cos(turn).astype(np.float32),
        np.sin(turn).astype(np.float32),
        forward.astype(narrow),
        forward.T.astype(narrow),
    )


def gather_slabs(blocks, inner):
    local = blocks[0].shape[1]
    wide = [block.astype(F32) for block in blocks]
    halves = []
    for half in range(2):
        rows = slice(half * GROUP, (half + 1) * GROUP)
        pieces = [block[rows, at : at + inner] for block in wide for at in range(0, local, inner)]
        halves.append(jnp.concatenate(pieces, axis=0))
    return jnp.concatenate(halves, axis=1).astype(BF16)


def forward_dft(rows, first, cos, sin, forward, inner):
    stage = jnp.dot(first, rows, preferred_element_type=F32)
    half_rows = SLABS * GROUP
    turned = []
    for half in range(2):
        lanes = slice(half * inner, (half + 1) * inner)
        real, imag = stage[:half_rows, lanes], stage[half_rows:, lanes]
        turned.append(
            jnp.concatenate([real * cos + imag * sin, imag * cos - real * sin], axis=1).astype(BF16)
        )
    spec = jnp.dot(jnp.concatenate(turned, axis=0), forward, preferred_element_type=F32)
    return (spec[:, :inner], spec[:, inner:])


def inverse_dft(spec, last, cos, sin, backward, inner):
    both = jnp.concatenate(spec, axis=1).astype(BF16)
    stage = jnp.dot(both, backward, preferred_element_type=F32)
    half_rows = SLABS * GROUP
    turned = []
    for half in range(2):
        rows = slice(half * half_rows, (half + 1) * half_rows)
        real, imag = stage[rows, :inner], stage[rows, inner:]
        turned.append(
            jnp.concatenate([real * cos - imag * sin, imag * cos + real * sin], axis=0).astype(BF16)
        )
    return jnp.dot(last, jnp.concatenate(turned, axis=1), preferred_element_type=F32)


def scatter_slabs(rows, scale, outs, lead, inner):
    local = outs[0].shape[-1]
    per = local // inner
    scaled = rows * scale
    for src, out in enumerate(outs):
        for part in range(per):
            at = (src * per + part) * GROUP
            tile = jnp.concatenate(
                [scaled[at : at + GROUP, :inner], scaled[at : at + GROUP, inner:]], axis=0
            ).astype(BF16)
            lanes = slice(part * inner, (part + 1) * inner)
            if lead is None:
                out[:, lanes] = tile
            else:
                out[lead, :, lanes] = tile


def times_plain(left, right):
    return (left[0] * right[0] - left[1] * right[1], left[0] * right[1] + left[1] * right[0])


def times_conj(left, right):
    return (left[0] * right[0] + left[1] * right[1], left[1] * right[0] - left[0] * right[1])


def response_kernel(chunks, inner, me, *refs):
    pair, refs = refs[:chunks], refs[chunks:]
    (first, last, cos, sin, forward, backward), outs = refs[:6], refs[6:]
    tables = (first[...], cos[...], sin[...], forward[...], inner)
    prod = forward_dft(gather_slabs([ref[0] for ref in pair], inner), *tables)
    taps = forward_dft(gather_slabs([ref[1] for ref in pair], inner), *tables)
    rows = inverse_dft(times_plain(prod, taps), last[...], cos[...], sin[...], backward[...], inner)
    scatter_slabs(rows, 1.0 / (SLABS * inner), outs, None, inner)


def backward_kernel(chunks, inner, scale, me, *refs):
    pair, grad, refs = refs[:chunks], refs[chunks : 2 * chunks], refs[2 * chunks :]
    (first, last, cos, sin, forward, backward), outs = refs[:6], refs[6:]
    tables = (first[...], cos[...], sin[...], forward[...], inner)
    back_tables = (last[...], cos[...], sin[...], backward[...], inner)
    grad_spec = forward_dft(gather_slabs([ref[...] for ref in grad], inner), *tables)
    taps = forward_dft(gather_slabs([ref[1] for ref in pair], inner), *tables)
    rows = inverse_dft(times_conj(grad_spec, taps), *back_tables)
    scatter_slabs(rows, 1.0 / (SLABS * inner), outs, 0, inner)
    prod = forward_dft(gather_slabs([ref[0] for ref in pair], inner), *tables)
    rows = inverse_dft(times_conj(grad_spec, prod), *back_tables)
    scatter_slabs(rows, scale / (SLABS * inner), outs, 1, inner)


def conv_call(kernel, me, operands, tables, lead, inner, transforms):
    chunks, shape = len(operands[0]), operands[0][0].shape
    channels, local = shape[-2:]
    def rows_of(shape):
        middle = shape[:-2]
        return pl.BlockSpec(
            middle + (STEP, local), lambda i, me: (0,) * len(middle) + (i, 0)
        )

    def whole(table):
        return pl.BlockSpec(table.shape, lambda i, me: (0, 0))

    out_shape = lead + (channels, local)
    rows = channels * SLABS
    flops = transforms * rows * (2 * (2 * inner) ** 2 + 4 * SLABS * GROUP * inner)
    flat = [chunk for operand in operands for chunk in operand]
    return pl.pallas_call(
        kernel,
        grid_spec=pltpu.PrefetchScalarGridSpec(
            num_scalar_prefetch=1,
            grid=(channels // STEP,),
            in_specs=[rows_of(chunk.shape) for chunk in flat] + [whole(t) for t in tables],
            out_specs=[rows_of(out_shape)] * chunks,
        ),
        out_shape=[jax.ShapeDtypeStruct(out_shape, BF16)] * chunks,
        compiler_params=pltpu.CompilerParams(vmem_limit_bytes=40 * 1024 * 1024),
        cost_estimate=pl.CostEstimate(
            flops=flops, bytes_accessed=2 * rows * inner * 4, transcendentals=0
        ),
    )(me, *flat, *tables)


def elementwise(left, right):
    return (left.astype(F32) * right.astype(F32)).astype(BF16)


def prepare_kernel(masks, scale, inner_gate, signal, taps, gain, *refs):
    count = len(masks)
    outs, (gates, values, filters, sems) = refs[:count], refs[count:]
    me = lax.axis_index("ctx")
    copies = []
    for k, mask in enumerate(masks):
        at = me ^ mask
        pairs = ((inner_gate, gates), (signal, values), (taps, filters))
        copies.append(
            [
                pltpu.make_async_copy(src.at[at], dst.at[k], sems.at[k, n])
                for n, (src, dst) in enumerate(pairs)
            ]
        )
    for group in copies:
        for copy in group:
            copy.start()
    rows, lanes = gates.shape[1], gain.shape[1]
    shape = (rows, lanes)
    diagonal = lax.broadcasted_iota(jnp.int32, shape, 0) == lax.broadcasted_iota(jnp.int32, shape, 1)
    at_zero = (me == 0) & (lax.broadcasted_iota(jnp.int32, filters.shape[1:], 1) == 0)
    for k, (mask, group, out) in enumerate(zip(masks, copies, outs)):
        row = gain[pl.ds(me ^ mask, 1), :]
        column = jnp.sum(jnp.where(diagonal, row, 0.0), axis=1, keepdims=True)
        for copy in group:
            copy.wait()
        out[0] = elementwise(gates[k], values[k])
        out[1] = (filters[k] * scale + jnp.where(at_zero, column, 0.0)).astype(BF16)


def prepare_call(masks, scale, inner_gate, signal, taps, gain):
    count, (rows, lanes) = len(masks), taps.shape[1:]
    out = jax.ShapeDtypeStruct((2, rows, lanes), BF16)
    anywhere = pl.BlockSpec(memory_space=pl.ANY)
    inside = pl.BlockSpec(memory_space=pltpu.VMEM)
    return pl.pallas_call(
        functools.partial(prepare_kernel, masks, scale),
        in_specs=[anywhere, anywhere, anywhere, inside],
        out_specs=[inside] * count,
        out_shape=[out] * count,
        scratch_shapes=[
            pltpu.VMEM((count, rows, lanes), BF16),
            pltpu.VMEM((count, rows, lanes), BF16),
            pltpu.VMEM((count, rows, lanes), F32),
            pltpu.SemaphoreType.DMA((count, 3)),
        ],
        compiler_params=pltpu.CompilerParams(vmem_limit_bytes=62 * 1024 * 1024),
        cost_estimate=pl.CostEstimate(
            flops=8 * count * rows * lanes, bytes_accessed=12 * count * rows * lanes, transcendentals=0
        ),
    )(inner_gate, signal, taps, gain)


def project_kernel(chunks, members, me, *refs):
    weights, blocks = refs[:members], refs[members : 2 * members]
    gate, upstream, *outs = refs[2 * members :]
    step = pl.program_id(0)
    rows = weights[0].shape[0] // 2
    total = jnp.dot(weights[0][...], blocks[0][...], preferred_element_type=F32)
    for weight, block in zip(weights[1:], blocks[1:]):
        total += jnp.dot(weight[...], block[...], preferred_element_type=F32)
    total = total.astype(BF16)
    upstream[...] = total.reshape(upstream.shape)
    low = elementwise(total[:rows], gate[0])
    high = elementwise(total[rows:], gate[1])
    swapped = (me[0] & 1) == 1
    place = partners(chunks).index
    for pair in range(chunks // 2):

        @pl.when(step == pair)
        def _():
            outs[place(2 * pair)][...] = jnp.where(swapped, high, low)
            outs[place(2 * pair + 1)][...] = jnp.where(swapped, low, high)


def outer_kernel(chunks, me, upstream, *refs):
    chunk, out = refs[:chunks], refs[chunks]
    for d, piece in zip(partners(chunks), chunk):
        at = me[0] ^ d
        out[at] = elementwise(upstream[at], piece[...])


def finish_kernel(count, me, *refs):
    gates, refs = refs[:count], refs[count:]
    values, refs = refs[:count], refs[count:]
    chunk, (grad_inner, grad_signal, grad_taps) = refs[:count], refs[-3:]
    step = pl.program_id(0)
    for k in range(count):

        @pl.when(step == k)
        def _(k=k):
            back = chunk[k][0]
            grad_inner[0] = elementwise(back, values[k][0])
            grad_signal[0] = elementwise(back, gates[k][0])
            grad_taps[0] = chunk[k][1].astype(F32)


def finish_call(me, masks, inner_gate, signal, chunks, earlier):
    count, shape = len(masks), inner_gate.shape
    block = (1,) + shape[1:]

    def place(i, me):
        mask = masks[0]
        for k in range(1, count):
            mask = jnp.where(i == k, masks[k], mask)
        return (me[0] ^ mask, 0, 0)

    gates = [pl.BlockSpec(block, lambda i, me, mask=mask: (me[0] ^ mask, 0, 0)) for mask in masks]
    pieces = [pl.BlockSpec(chunk.shape, lambda i, me: (0, 0, 0)) for chunk in chunks]
    return pl.pallas_call(
        functools.partial(finish_kernel, count),
        grid_spec=pltpu.PrefetchScalarGridSpec(
            num_scalar_prefetch=1,
            grid=(count,),
            in_specs=gates * 2 + pieces + [pl.BlockSpec(memory_space=pl.ANY)] * len(earlier),
            out_specs=[pl.BlockSpec(block, place)] * 3,
        ),
        out_shape=[jax.ShapeDtypeStruct(shape, dtype) for dtype in (BF16, BF16, F32)],
        input_output_aliases={1 + 3 * count + n: n for n in range(len(earlier))},
        compiler_params=pltpu.CompilerParams(vmem_limit_bytes=32 * 1024 * 1024),
        cost_estimate=pl.CostEstimate(
            flops=2 * count * math.prod(shape[1:]),
            bytes_accessed=16 * count * math.prod(shape[1:]),
            transcendentals=0,
        ),
    )(me, *[inner_gate] * count, *[signal] * count, *chunks, *earlier)


def rowwise_call(kernel, me, wholes, pieces, out_shapes, rows, limit=32):
    def spec(shape):
        lead = shape[:-2]
        return pl.BlockSpec(
            lead + (rows, shape[-1]), lambda i, me: (0,) * len(lead) + (i, 0)
        )

    channels = wholes[0].shape[1]
    size = sum(math.prod(x.shape) * x.dtype.itemsize for x in (*wholes, *pieces, *out_shapes))
    return pl.pallas_call(
        kernel,
        grid_spec=pltpu.PrefetchScalarGridSpec(
            num_scalar_prefetch=1,
            grid=(channels // rows,),
            in_specs=[spec(x.shape) for x in (*wholes, *pieces)],
            out_specs=[spec(x.shape) for x in out_shapes],
        ),
        out_shape=out_shapes,
        compiler_params=pltpu.CompilerParams(vmem_limit_bytes=limit * 1024 * 1024),
        cost_estimate=pl.CostEstimate(flops=size, bytes_accessed=size, transcendentals=0),
    )(me, *wholes, *pieces)


def project_call(me, weight, blocks, gate):
    chunks, channels, local = gate.shape
    members, depth = len(blocks), blocks[0].shape[0]

    def pair(i, me):
        return (me[0] >> 1) ^ i

    rows = 2 * channels
    return pl.pallas_call(
        functools.partial(project_kernel, chunks, members),
        grid_spec=pltpu.PrefetchScalarGridSpec(
            num_scalar_prefetch=1,
            grid=(chunks // 2,),
            in_specs=[
                pl.BlockSpec((rows, depth), lambda i, me, j=j: (pair(i, me), me[1] ^ j))
                for j in range(members)
            ]
            + [pl.BlockSpec((depth, local), lambda i, me: (0, 0))] * members
            + [pl.BlockSpec((2, channels, local), lambda i, me: (pair(i, me), 0, 0))],
            out_specs=[pl.BlockSpec((2, channels, local), lambda i, me: (pair(i, me), 0, 0))]
            + [pl.BlockSpec((channels, local), lambda i, me: (0, 0))] * chunks,
        ),
        out_shape=[jax.ShapeDtypeStruct(gate.shape, BF16)]
        + [jax.ShapeDtypeStruct((channels, local), BF16)] * chunks,
        compiler_params=pltpu.CompilerParams(vmem_limit_bytes=40 * 1024 * 1024),
        cost_estimate=pl.CostEstimate(
            flops=2 * weight.size * local, bytes_accessed=2 * weight.size, transcendentals=0
        ),
    )(me, *[weight] * members, *blocks, gate)


def gather_start(block):
    count = lax.axis_size("group")
    return lax.ppermute(block, "group", [(g, g ^ (count // 2)) for g in range(count)])


def gather_rest(block, far, other):
    count = lax.axis_size("group")
    bit = count // 2
    held = {0: block, bit: far}
    bit //= 2
    while bit:
        pairs = [(g, g ^ bit) for g in range(count)]
        for j in list(held):
            sent = held[j]
            if j:
                sent, _ = lax.optimization_barrier((sent, other))
            held[j ^ bit] = lax.ppermute(sent, "group", pairs)
        bit //= 2
    return [held[j] for j in range(count)]


def send(part, d, count):
    return lax.ppermute(part, "ctx", [(p, p ^ d) for p in range(count)])


def exchange(parts):
    count = len(parts)
    order = partners(count)
    if count > 8:
        blocks = lax.axis_index("ctx") ^ jnp.arange(count)
        where = np.argsort(order)
        sent = jnp.take(jnp.take(jnp.stack(parts), where, axis=0), blocks, axis=0)
        came = lax.all_to_all(sent, "ctx", split_axis=0, concat_axis=0, tiled=True)
        return list(jnp.take(jnp.take(came, blocks, axis=0), np.array(order), axis=0))
    return [parts[0]] + [send(part, d, count) for d, part in zip(order[1:], parts[1:])]


def after(parts, other):
    held, _ = lax.optimization_barrier((parts[0], other))
    return [held] + list(parts[1:])


def per_device(outer_gate, inner_gate, signal, cotangent, out_weight, filter_taps, skip_gain):
    ch_dev, tok_local = outer_gate.shape
    n_ctx = lax.axis_size("ctx")
    ch_slice = ch_dev // n_ctx
    seq_len = n_ctx * tok_local
    inner = seq_len // SLABS
    scale = 1.0 / math.sqrt(seq_len)
    me = jnp.stack([lax.axis_index("ctx"), lax.axis_index("group")])

    def split(array):
        return array.reshape(n_ctx, ch_slice, -1)

    def flat(array):
        return array.reshape(ch_dev, tok_local)

    def shapes(lead, dtype, count):
        return [jax.ShapeDtypeStruct(lead + (ch_slice, tok_local), dtype)] * count

    tables = [jnp.asarray(table) for table in make_tables(inner, n_ctx)]
    tables = [table if table.ndim == 2 else table[me[0]] for table in tables]
    masks = partners(n_ctx)
    first = min(3, n_ctx)
    sources = (scale, split(inner_gate), split(signal), split(filter_taps), split(skip_gain)[:, :, 0])
    head = prepare_call(masks[1:first], *sources)
    cotangent, _ = lax.optimization_barrier((cotangent, head[0]))
    far = gather_start(cotangent)
    own, *rest = prepare_call([0] + masks[first:], *sources)
    pair = exchange([own, *head, *rest])
    gathered = gather_rest(cotangent, far, (pair[1:first], pair[-1:], rest[:1]))
    upstream, *grad = project_call(me, out_weight, gathered, split(outer_gate))
    response = conv_call(
        functools.partial(response_kernel, n_ctx, inner), me, (after(pair, grad[0]),), tables, (), inner, 3
    )
    grad[-2:], _ = lax.optimization_barrier((grad[-2:], response[0]))
    grad_came = exchange(grad)
    resp_came = exchange(response)
    backs = conv_call(
        functools.partial(backward_kernel, n_ctx, inner, scale),
        me,
        (pair, after(grad_came, response[0])),
        tables,
        (2,),
        inner,
        5,
    )
    backs_came = exchange(backs)
    (grad_outer,) = rowwise_call(
        functools.partial(outer_kernel, n_ctx),
        me,
        (upstream,),
        after(resp_came, backs[0]),
        shapes((n_ctx,), BF16, 1),
        32,
    )
    outs = []
    last = range(3, 5)
    for part in ([k for k in range(n_ctx) if k not in last], last):
        outs = finish_call(
            me,
            [masks[k] for k in part],
            split(inner_gate),
            split(signal),
            [backs_came[k] for k in part],
            outs,
        )
    grad_inner, grad_signal, grad_taps = outs
    return (flat(grad_outer), flat(grad_inner), flat(grad_signal), flat(grad_taps))


def solution(mesh):
    in_specs = (
        P("group", "ctx"),
        P("group", "ctx"),
        P("group", "ctx"),
        P("group", "ctx"),
        P("group", None),
        P("group", "ctx"),
        P("group"),
    )
    out_specs = (P("group", "ctx"), P("group", "ctx"), P("group", "ctx"), P("group", "ctx"))
    return jax.shard_map(
        per_device, mesh=mesh, in_specs=in_specs, out_specs=out_specs, check_vma=False
    )
```

```python
import functools
import math

import jax
import jax.numpy as jnp
import ml_dtypes
import numpy as np
from jax import lax
from jax.experimental import pallas as pl
from jax.experimental.pallas import tpu as pltpu
from jax.sharding import PartitionSpec as P

SLABS = 32
GROUP = 8
STEP = 2 * GROUP
F32 = jnp.float32
BF16 = jnp.bfloat16


def partners(count):
    return [0] + list(reversed(range(1, count)))


def make_tables(inner, chunks):
    slab = np.arange(SLABS)
    freq = np.arange(SLABS) + 0.5
    angle = 2.0 * np.pi / (2 * SLABS) * np.outer(freq, slab)
    eye = np.eye(GROUP)
    first = np.concatenate([np.kron(np.cos(angle), eye), np.kron(-np.sin(angle), eye)], axis=0)
    blocks = first.reshape(first.shape[0], chunks, -1)
    order = np.array(partners(chunks))
    first = np.stack([blocks[:, order ^ p].reshape(first.shape) for p in range(chunks)])
    last = first.transpose(0, 2, 1)
    within = np.arange(inner)
    turn = np.repeat(2.0 * np.pi / (2 * SLABS * inner) * np.outer(freq, within), GROUP, axis=0)
    circle = 2.0 * np.pi / inner * (np.outer(within, within) % inner)
    cos, sin = np.cos(circle), np.sin(circle)
    forward = np.block([[cos, -sin], [sin, cos]])
    narrow = ml_dtypes.bfloat16
    return (
        first.astype(narrow),
        last.astype(narrow),
        np.cos(turn).astype(np.float32),
        np.sin(turn).astype(np.float32),
        forward.astype(narrow),
        forward.T.astype(narrow),
    )


def gather_slabs(blocks, inner):
    local = blocks[0].shape[1]
    wide = [block.astype(F32) for block in blocks]
    halves = []
    for half in range(2):
        rows = slice(half * GROUP, (half + 1) * GROUP)
        pieces = [block[rows, at : at + inner] for block in wide for at in range(0, local, inner)]
        halves.append(jnp.concatenate(pieces, axis=0))
    return jnp.concatenate(halves, axis=1).astype(BF16)


def forward_dft(rows, first, cos, sin, forward, inner):
    stage = jnp.dot(first, rows, preferred_element_type=F32)
    half_rows = SLABS * GROUP
    turned = []
    for half in range(2):
        lanes = slice(half * inner, (half + 1) * inner)
        real, imag = stage[:half_rows, lanes], stage[half_rows:, lanes]
        turned.append(
            jnp.concatenate([real * cos + imag * sin, imag * cos - real * sin], axis=1).astype(BF16)
        )
    spec = jnp.dot(jnp.concatenate(turned, axis=0), forward, preferred_element_type=F32)
    return (spec[:, :inner], spec[:, inner:])


def inverse_dft(spec, last, cos, sin, backward, inner):
    both = jnp.concatenate(spec, axis=1).astype(BF16)
    stage = jnp.dot(both, backward, preferred_element_type=F32)
    half_rows = SLABS * GROUP
    turned = []
    for half in range(2):
        rows = slice(half * half_rows, (half + 1) * half_rows)
        real, imag = stage[rows, :inner], stage[rows, inner:]
        turned.append(
            jnp.concatenate([real * cos - imag * sin, imag * cos + real * sin], axis=0).astype(BF16)
        )
    return jnp.dot(last, jnp.concatenate(turned, axis=1), preferred_element_type=F32)


def scatter_slabs(rows, scale, outs, lead, inner):
    local = outs[0].shape[-1]
    per = local // inner
    scaled = rows * scale
    for src, out in enumerate(outs):
        for part in range(per):
            at = (src * per + part) * GROUP
            tile = jnp.concatenate(
                [scaled[at : at + GROUP, :inner], scaled[at : at + GROUP, inner:]], axis=0
            ).astype(BF16)
            lanes = slice(part * inner, (part + 1) * inner)
            if lead is None:
                out[:, lanes] = tile
            else:
                out[lead, :, lanes] = tile


def times_plain(left, right):
    return (left[0] * right[0] - left[1] * right[1], left[0] * right[1] + left[1] * right[0])


def times_conj(left, right):
    return (left[0] * right[0] + left[1] * right[1], left[1] * right[0] - left[0] * right[1])


def response_kernel(chunks, inner, me, *refs):
    pair, refs = refs[:chunks], refs[chunks:]
    (first, last, cos, sin, forward, backward), outs = refs[:6], refs[6:]
    tables = (first[...], cos[...], sin[...], forward[...], inner)
    prod = forward_dft(gather_slabs([ref[0] for ref in pair], inner), *tables)
    taps = forward_dft(gather_slabs([ref[1] for ref in pair], inner), *tables)
    rows = inverse_dft(times_plain(prod, taps), last[...], cos[...], sin[...], backward[...], inner)
    scatter_slabs(rows, 1.0 / (SLABS * inner), outs, None, inner)


def near_first(chunks):
    return [0, 1, *range(chunks // 2 + 1, chunks), *range(2, chunks // 2 + 1)]


def backward_kernel(chunks, inner, scale, me, *refs):
    pair, grad, refs = refs[:chunks], refs[chunks : 2 * chunks], refs[2 * chunks :]
    grad = sorted(zip(near_first(chunks), grad), key=lambda item: item[0])
    grad = [ref for _, ref in grad]
    (first, last, cos, sin, forward, backward), outs = refs[:6], refs[6:]
    tables = (first[...], cos[...], sin[...], forward[...], inner)
    back_tables = (last[...], cos[...], sin[...], backward[...], inner)
    grad_spec = forward_dft(gather_slabs([ref[...] for ref in grad], inner), *tables)
    taps = forward_dft(gather_slabs([ref[1] for ref in pair], inner), *tables)
    rows = inverse_dft(times_conj(grad_spec, taps), *back_tables)
    scatter_slabs(rows, 1.0 / (SLABS * inner), outs, 0, inner)
    prod = forward_dft(gather_slabs([ref[0] for ref in pair], inner), *tables)
    rows = inverse_dft(times_conj(grad_spec, prod), *back_tables)
    scatter_slabs(rows, scale / (SLABS * inner), outs, 1, inner)


def conv_call(kernel, me, operands, tables, lead, inner, transforms):
    chunks, shape = len(operands[0]), operands[0][0].shape
    channels, local = shape[-2:]
    def rows_of(shape):
        middle = shape[:-2]
        return pl.BlockSpec(
            middle + (STEP, local), lambda i, me: (0,) * len(middle) + (i, 0)
        )

    def whole(table):
        return pl.BlockSpec(table.shape, lambda i, me: (0, 0))

    out_shape = lead + (channels, local)
    rows = channels * SLABS
    flops = transforms * rows * (2 * (2 * inner) ** 2 + 4 * SLABS * GROUP * inner)
    flat = [chunk for operand in operands for chunk in operand]
    return pl.pallas_call(
        kernel,
        grid_spec=pltpu.PrefetchScalarGridSpec(
            num_scalar_prefetch=1,
            grid=(channels // STEP,),
            in_specs=[rows_of(chunk.shape) for chunk in flat] + [whole(t) for t in tables],
            out_specs=[rows_of(out_shape)] * chunks,
        ),
        out_shape=[jax.ShapeDtypeStruct(out_shape, BF16)] * chunks,
        compiler_params=pltpu.CompilerParams(vmem_limit_bytes=40 * 1024 * 1024),
        cost_estimate=pl.CostEstimate(
            flops=flops, bytes_accessed=2 * rows * inner * 4, transcendentals=0
        ),
    )(me, *flat, *tables)


def elementwise(left, right):
    return (left.astype(F32) * right.astype(F32)).astype(BF16)


def prepare_kernel(masks, scale, inner_gate, signal, taps, gain, *refs):
    count = len(masks)
    outs, (gates, values, filters, sems) = refs[:count], refs[count:]
    me = lax.axis_index("ctx")
    copies = []
    for k, mask in enumerate(masks):
        at = me ^ mask
        pairs = ((inner_gate, gates), (signal, values), (taps, filters))
        copies.append(
            [
                pltpu.make_async_copy(src.at[at], dst.at[k], sems.at[k, n])
                for n, (src, dst) in enumerate(pairs)
            ]
        )
    for group in copies:
        for copy in group:
            copy.start()
    rows, lanes = gates.shape[1], gain.shape[1]
    shape = (rows, lanes)
    diagonal = lax.broadcasted_iota(jnp.int32, shape, 0) == lax.broadcasted_iota(jnp.int32, shape, 1)
    at_zero = (me == 0) & (lax.broadcasted_iota(jnp.int32, filters.shape[1:], 1) == 0)
    for k, (mask, group, out) in enumerate(zip(masks, copies, outs)):
        row = gain[pl.ds(me ^ mask, 1), :]
        column = jnp.sum(jnp.where(diagonal, row, 0.0), axis=1, keepdims=True)
        for copy in group:
            copy.wait()
        out[0] = elementwise(gates[k], values[k])
        out[1] = (filters[k] * scale + jnp.where(at_zero, column, 0.0)).astype(BF16)


def prepare_call(masks, scale, inner_gate, signal, taps, gain):
    count, (rows, lanes) = len(masks), taps.shape[1:]
    out = jax.ShapeDtypeStruct((2, rows, lanes), BF16)
    anywhere = pl.BlockSpec(memory_space=pl.ANY)
    inside = pl.BlockSpec(memory_space=pltpu.VMEM)
    return pl.pallas_call(
        functools.partial(prepare_kernel, masks, scale),
        in_specs=[anywhere, anywhere, anywhere, inside],
        out_specs=[inside] * count,
        out_shape=[out] * count,
        scratch_shapes=[
            pltpu.VMEM((count, rows, lanes), BF16),
            pltpu.VMEM((count, rows, lanes), BF16),
            pltpu.VMEM((count, rows, lanes), F32),
            pltpu.SemaphoreType.DMA((count, 3)),
        ],
        compiler_params=pltpu.CompilerParams(vmem_limit_bytes=62 * 1024 * 1024),
        cost_estimate=pl.CostEstimate(
            flops=8 * count * rows * lanes, bytes_accessed=12 * count * rows * lanes, transcendentals=0
        ),
    )(inner_gate, signal, taps, gain)


def project_kernel(chunks, members, me, *refs):
    weights, blocks = refs[:members], refs[members : 2 * members]
    gate, upstream, *outs = refs[2 * members :]
    step = pl.program_id(0)
    rows = weights[0].shape[0] // 2
    total = jnp.dot(weights[0][...], blocks[0][...], preferred_element_type=F32)
    for weight, block in zip(weights[1:], blocks[1:]):
        total += jnp.dot(weight[...], block[...], preferred_element_type=F32)
    total = total.astype(BF16)
    upstream[...] = total.reshape(upstream.shape)
    low = elementwise(total[:rows], gate[0])
    high = elementwise(total[rows:], gate[1])
    swapped = (me[0] & 1) == 1
    place = partners(chunks).index
    for pair in range(chunks // 2):

        @pl.when(step == pair)
        def _():
            outs[place(2 * pair)][...] = jnp.where(swapped, high, low)
            outs[place(2 * pair + 1)][...] = jnp.where(swapped, low, high)


def outer_kernel(chunks, me, upstream, *refs):
    chunk, out = refs[:chunks], refs[chunks]
    for d, piece in zip(partners(chunks), chunk):
        at = me[0] ^ d
        out[at] = elementwise(upstream[at], piece[...])


def finish_kernel(count, me, *refs):
    gates, refs = refs[:count], refs[count:]
    values, refs = refs[:count], refs[count:]
    chunk, (grad_inner, grad_signal, grad_taps) = refs[:count], refs[-3:]
    step = pl.program_id(0)
    for k in range(count):

        @pl.when(step == k)
        def _(k=k):
            back = chunk[k][0]
            grad_inner[0] = elementwise(back, values[k][0])
            grad_signal[0] = elementwise(back, gates[k][0])
            grad_taps[0] = chunk[k][1].astype(F32)


def finish_call(me, masks, inner_gate, signal, chunks, earlier):
    count, shape = len(masks), inner_gate.shape
    block = (1,) + shape[1:]

    def place(i, me):
        mask = masks[0]
        for k in range(1, count):
            mask = jnp.where(i == k, masks[k], mask)
        return (me[0] ^ mask, 0, 0)

    gates = [pl.BlockSpec(block, lambda i, me, mask=mask: (me[0] ^ mask, 0, 0)) for mask in masks]
    pieces = [pl.BlockSpec(chunk.shape, lambda i, me: (0, 0, 0)) for chunk in chunks]
    return pl.pallas_call(
        functools.partial(finish_kernel, count),
        grid_spec=pltpu.PrefetchScalarGridSpec(
            num_scalar_prefetch=1,
            grid=(count,),
            in_specs=gates * 2 + pieces + [pl.BlockSpec(memory_space=pl.ANY)] * len(earlier),
            out_specs=[pl.BlockSpec(block, place)] * 3,
        ),
        out_shape=[jax.ShapeDtypeStruct(shape, dtype) for dtype in (BF16, BF16, F32)],
        input_output_aliases={1 + 3 * count + n: n for n in range(len(earlier))},
        compiler_params=pltpu.CompilerParams(vmem_limit_bytes=32 * 1024 * 1024),
        cost_estimate=pl.CostEstimate(
            flops=2 * count * math.prod(shape[1:]),
            bytes_accessed=16 * count * math.prod(shape[1:]),
            transcendentals=0,
        ),
    )(me, *[inner_gate] * count, *[signal] * count, *chunks, *earlier)


def rowwise_call(kernel, me, wholes, pieces, out_shapes, rows, limit=32):
    def spec(shape):
        lead = shape[:-2]
        return pl.BlockSpec(
            lead + (rows, shape[-1]), lambda i, me: (0,) * len(lead) + (i, 0)
        )

    channels = wholes[0].shape[1]
    size = sum(math.prod(x.shape) * x.dtype.itemsize for x in (*wholes, *pieces, *out_shapes))
    return pl.pallas_call(
        kernel,
        grid_spec=pltpu.PrefetchScalarGridSpec(
            num_scalar_prefetch=1,
            grid=(channels // rows,),
            in_specs=[spec(x.shape) for x in (*wholes, *pieces)],
            out_specs=[spec(x.shape) for x in out_shapes],
        ),
        out_shape=out_shapes,
        compiler_params=pltpu.CompilerParams(vmem_limit_bytes=limit * 1024 * 1024),
        cost_estimate=pl.CostEstimate(flops=size, bytes_accessed=size, transcendentals=0),
    )(me, *wholes, *pieces)


def project_call(me, weight, blocks, gate):
    chunks, channels, local = gate.shape
    members, depth = len(blocks), blocks[0].shape[0]

    def pair(i, me):
        return (me[0] >> 1) ^ i

    rows = 2 * channels
    return pl.pallas_call(
        functools.partial(project_kernel, chunks, members),
        grid_spec=pltpu.PrefetchScalarGridSpec(
            num_scalar_prefetch=1,
            grid=(chunks // 2,),
            in_specs=[
                pl.BlockSpec((rows, depth), lambda i, me, j=j: (pair(i, me), me[1] ^ j))
                for j in range(members)
            ]
            + [pl.BlockSpec((depth, local), lambda i, me: (0, 0))] * members
            + [pl.BlockSpec((2, channels, local), lambda i, me: (pair(i, me), 0, 0))],
            out_specs=[pl.BlockSpec((2, channels, local), lambda i, me: (pair(i, me), 0, 0))]
            + [pl.BlockSpec((channels, local), lambda i, me: (0, 0))] * chunks,
        ),
        out_shape=[jax.ShapeDtypeStruct(gate.shape, BF16)]
        + [jax.ShapeDtypeStruct((channels, local), BF16)] * chunks,
        compiler_params=pltpu.CompilerParams(vmem_limit_bytes=40 * 1024 * 1024),
        cost_estimate=pl.CostEstimate(
            flops=2 * weight.size * local, bytes_accessed=2 * weight.size, transcendentals=0
        ),
    )(me, *[weight] * members, *blocks, gate)


def gather_start(block):
    count = lax.axis_size("group")
    return lax.ppermute(block, "group", [(g, g ^ (count // 2)) for g in range(count)])


def gather_rest(block, far, other):
    count = lax.axis_size("group")
    bit = count // 2
    held = {0: block, bit: far}
    bit //= 2
    while bit:
        pairs = [(g, g ^ bit) for g in range(count)]
        for j in list(held):
            sent = held[j]
            if j:
                sent, _ = lax.optimization_barrier((sent, other))
            held[j ^ bit] = lax.ppermute(sent, "group", pairs)
        bit //= 2
    return [held[j] for j in range(count)]


def send(part, d, count):
    return lax.ppermute(part, "ctx", [(p, p ^ d) for p in range(count)])


def exchange(parts):
    count = len(parts)
    order = partners(count)
    if count > 8:
        blocks = lax.axis_index("ctx") ^ jnp.arange(count)
        where = np.argsort(order)
        sent = jnp.take(jnp.take(jnp.stack(parts), where, axis=0), blocks, axis=0)
        came = lax.all_to_all(sent, "ctx", split_axis=0, concat_axis=0, tiled=True)
        return list(jnp.take(jnp.take(came, blocks, axis=0), np.array(order), axis=0))
    return [parts[0]] + [send(part, d, count) for d, part in zip(order[1:], parts[1:])]


def after(parts, other):
    held, _ = lax.optimization_barrier((parts[0], other))
    return [held] + list(parts[1:])


def per_device(outer_gate, inner_gate, signal, cotangent, out_weight, filter_taps, skip_gain):
    ch_dev, tok_local = outer_gate.shape
    n_ctx = lax.axis_size("ctx")
    ch_slice = ch_dev // n_ctx
    seq_len = n_ctx * tok_local
    inner = seq_len // SLABS
    scale = 1.0 / math.sqrt(seq_len)
    me = jnp.stack([lax.axis_index("ctx"), lax.axis_index("group")])

    def split(array):
        return array.reshape(n_ctx, ch_slice, -1)

    def flat(array):
        return array.reshape(ch_dev, tok_local)

    def shapes(lead, dtype, count):
        return [jax.ShapeDtypeStruct(lead + (ch_slice, tok_local), dtype)] * count

    tables = [jnp.asarray(table) for table in make_tables(inner, n_ctx)]
    tables = [table if table.ndim == 2 else table[me[0]] for table in tables]
    masks = partners(n_ctx)
    first = min(3, n_ctx)
    sources = (scale, split(inner_gate), split(signal), split(filter_taps), split(skip_gain)[:, :, 0])
    head = prepare_call(masks[1:first], *sources)
    cotangent, _ = lax.optimization_barrier((cotangent, head[0]))
    far = gather_start(cotangent)
    own, *rest = prepare_call([0] + masks[first:], *sources)
    pair = exchange([own, *head, *rest])
    gathered = gather_rest(cotangent, far, (pair[1:first], pair[-1:], rest[:1]))
    upstream, *grad = project_call(me, out_weight, gathered, split(outer_gate))
    response = conv_call(
        functools.partial(response_kernel, n_ctx, inner), me, (after(pair, grad[0]),), tables, (), inner, 3
    )
    grad_came = exchange(grad)
    resp_came = exchange(response)
    backs = conv_call(
        functools.partial(backward_kernel, n_ctx, inner, scale),
        me,
        (pair, after([grad_came[k] for k in near_first(n_ctx)], response[0])),
        tables,
        (2,),
        inner,
        5,
    )
    backs_came = exchange(backs)
    (grad_outer,) = rowwise_call(
        functools.partial(outer_kernel, n_ctx),
        me,
        (upstream,),
        after(resp_came, backs[0]),
        shapes((n_ctx,), BF16, 1),
        32,
    )
    outs = []
    last = range(3, 5)
    for part in ([k for k in range(n_ctx) if k not in last], last):
        outs = finish_call(
            me,
            [masks[k] for k in part],
            split(inner_gate),
            split(signal),
            [backs_came[k] for k in part],
            outs,
        )
    grad_inner, grad_signal, grad_taps = outs
    return (flat(grad_outer), flat(grad_inner), flat(grad_signal), flat(grad_taps))


def solution(mesh):
    in_specs = (
        P("group", "ctx"),
        P("group", "ctx"),
        P("group", "ctx"),
        P("group", "ctx"),
        P("group", None),
        P("group", "ctx"),
        P("group"),
    )
    out_specs = (P("group", "ctx"), P("group", "ctx"), P("group", "ctx"), P("group", "ctx"))
    return jax.shard_map(
        per_device, mesh=mesh, in_specs=in_specs, out_specs=out_specs, check_vma=False
    )
```

```python
import functools
import math

import jax
import jax.numpy as jnp
import ml_dtypes
import numpy as np
from jax import lax
from jax.experimental import pallas as pl
from jax.experimental.pallas import tpu as pltpu
from jax.sharding import PartitionSpec as P

SLABS = 32
GROUP = 8
STEP = 2 * GROUP
F32 = jnp.float32
BF16 = jnp.bfloat16


def partners(count):
    return [0] + list(reversed(range(1, count)))


def make_tables(inner, chunks):
    slab = np.arange(SLABS)
    freq = np.arange(SLABS) + 0.5
    angle = 2.0 * np.pi / (2 * SLABS) * np.outer(freq, slab)
    eye = np.eye(GROUP)
    first = np.concatenate([np.kron(np.cos(angle), eye), np.kron(-np.sin(angle), eye)], axis=0)
    blocks = first.reshape(first.shape[0], chunks, -1)
    order = np.array(partners(chunks))
    first = np.stack([blocks[:, order ^ p].reshape(first.shape) for p in range(chunks)])
    last = first.transpose(0, 2, 1)
    within = np.arange(inner)
    turn = np.repeat(2.0 * np.pi / (2 * SLABS * inner) * np.outer(freq, within), GROUP, axis=0)
    circle = 2.0 * np.pi / inner * (np.outer(within, within) % inner)
    cos, sin = np.cos(circle), np.sin(circle)
    forward = np.block([[cos, -sin], [sin, cos]])
    narrow = ml_dtypes.bfloat16
    return (
        first.astype(narrow),
        last.astype(narrow),
        np.cos(turn).astype(np.float32),
        np.sin(turn).astype(np.float32),
        forward.astype(narrow),
        forward.T.astype(narrow),
    )


def gather_slabs(blocks, inner):
    local = blocks[0].shape[1]
    wide = [block.astype(F32) for block in blocks]
    halves = []
    for half in range(2):
        rows = slice(half * GROUP, (half + 1) * GROUP)
        pieces = [block[rows, at : at + inner] for block in wide for at in range(0, local, inner)]
        halves.append(jnp.concatenate(pieces, axis=0))
    return jnp.concatenate(halves, axis=1).astype(BF16)


def forward_dft(rows, first, cos, sin, forward, inner):
    stage = jnp.dot(first, rows, preferred_element_type=F32)
    half_rows = SLABS * GROUP
    turned = []
    for half in range(2):
        lanes = slice(half * inner, (half + 1) * inner)
        real, imag = stage[:half_rows, lanes], stage[half_rows:, lanes]
        turned.append(
            jnp.concatenate([real * cos + imag * sin, imag * cos - real * sin], axis=1).astype(BF16)
        )
    spec = jnp.dot(jnp.concatenate(turned, axis=0), forward, preferred_element_type=F32)
    return (spec[:, :inner], spec[:, inner:])


def inverse_dft(spec, last, cos, sin, backward, inner):
    both = jnp.concatenate(spec, axis=1).astype(BF16)
    stage = jnp.dot(both, backward, preferred_element_type=F32)
    half_rows = SLABS * GROUP
    turned = []
    for half in range(2):
        rows = slice(half * half_rows, (half + 1) * half_rows)
        real, imag = stage[rows, :inner], stage[rows, inner:]
        turned.append(
            jnp.concatenate([real * cos - imag * sin, imag * cos + real * sin], axis=0).astype(BF16)
        )
    return jnp.dot(last, jnp.concatenate(turned, axis=1), preferred_element_type=F32)


def scatter_slabs(rows, scale, outs, lead, inner):
    local = outs[0].shape[-1]
    per = local // inner
    scaled = rows * scale
    for src, out in enumerate(outs):
        for part in range(per):
            at = (src * per + part) * GROUP
            tile = jnp.concatenate(
                [scaled[at : at + GROUP, :inner], scaled[at : at + GROUP, inner:]], axis=0
            ).astype(BF16)
            lanes = slice(part * inner, (part + 1) * inner)
            if lead is None:
                out[:, lanes] = tile
            else:
                out[lead, :, lanes] = tile


def times_plain(left, right):
    return (left[0] * right[0] - left[1] * right[1], left[0] * right[1] + left[1] * right[0])


def times_conj(left, right):
    return (left[0] * right[0] + left[1] * right[1], left[1] * right[0] - left[0] * right[1])


def pair_order(chunks):
    half = chunks // 2
    return [*range(half), *range(half + 1, chunks - 1), half, chunks - 1]


def grad_order(chunks):
    half = chunks // 2
    return [0, 1, *range(half + 1, chunks), *range(2, half + 1)]


def in_place(refs, order):
    return [refs[order.index(k)] for k in range(len(refs))]


def response_kernel(chunks, inner, me, *refs):
    pair, refs = in_place(refs[:chunks], pair_order(chunks)), refs[chunks:]
    (first, last, cos, sin, forward, backward), outs = refs[:6], refs[6:]
    tables = (first[...], cos[...], sin[...], forward[...], inner)
    prod = forward_dft(gather_slabs([ref[0] for ref in pair], inner), *tables)
    taps = forward_dft(gather_slabs([ref[1] for ref in pair], inner), *tables)
    rows = inverse_dft(times_plain(prod, taps), last[...], cos[...], sin[...], backward[...], inner)
    scatter_slabs(rows, 1.0 / (SLABS * inner), outs, None, inner)


def backward_kernel(chunks, inner, scale, me, *refs):
    pair, grad, refs = refs[:chunks], refs[chunks : 2 * chunks], refs[2 * chunks :]
    pair, grad = in_place(pair, pair_order(chunks)), in_place(grad, grad_order(chunks))
    (first, last, cos, sin, forward, backward), outs = refs[:6], refs[6:]
    tables = (first[...], cos[...], sin[...], forward[...], inner)
    back_tables = (last[...], cos[...], sin[...], backward[...], inner)
    grad_spec = forward_dft(gather_slabs([ref[...] for ref in grad], inner), *tables)
    taps = forward_dft(gather_slabs([ref[1] for ref in pair], inner), *tables)
    rows = inverse_dft(times_conj(grad_spec, taps), *back_tables)
    scatter_slabs(rows, 1.0 / (SLABS * inner), outs, 0, inner)
    prod = forward_dft(gather_slabs([ref[0] for ref in pair], inner), *tables)
    rows = inverse_dft(times_conj(grad_spec, prod), *back_tables)
    scatter_slabs(rows, scale / (SLABS * inner), outs, 1, inner)


def conv_call(kernel, me, operands, tables, lead, inner, transforms):
    chunks, shape = len(operands[0]), operands[0][0].shape
    channels, local = shape[-2:]
    def rows_of(shape):
        middle = shape[:-2]
        return pl.BlockSpec(
            middle + (STEP, local), lambda i, me: (0,) * len(middle) + (i, 0)
        )

    def whole(table):
        return pl.BlockSpec(table.shape, lambda i, me: (0, 0))

    out_shape = lead + (channels, local)
    rows = channels * SLABS
    flops = transforms * rows * (2 * (2 * inner) ** 2 + 4 * SLABS * GROUP * inner)
    flat = [chunk for operand in operands for chunk in operand]
    return pl.pallas_call(
        kernel,
        grid_spec=pltpu.PrefetchScalarGridSpec(
            num_scalar_prefetch=1,
            grid=(channels // STEP,),
            in_specs=[rows_of(chunk.shape) for chunk in flat] + [whole(t) for t in tables],
            out_specs=[rows_of(out_shape)] * chunks,
        ),
        out_shape=[jax.ShapeDtypeStruct(out_shape, BF16)] * chunks,
        compiler_params=pltpu.CompilerParams(vmem_limit_bytes=40 * 1024 * 1024),
        cost_estimate=pl.CostEstimate(
            flops=flops, bytes_accessed=2 * rows * inner * 4, transcendentals=0
        ),
    )(me, *flat, *tables)


def elementwise(left, right):
    return (left.astype(F32) * right.astype(F32)).astype(BF16)


def prepare_kernel(masks, scale, inner_gate, signal, taps, gain, *refs):
    count = len(masks)
    outs, (gates, values, filters, sems) = refs[:count], refs[count:]
    me = lax.axis_index("ctx")
    copies = []
    for k, mask in enumerate(masks):
        at = me ^ mask
        pairs = ((inner_gate, gates), (signal, values), (taps, filters))
        copies.append(
            [
                pltpu.make_async_copy(src.at[at], dst.at[k], sems.at[k, n])
                for n, (src, dst) in enumerate(pairs)
            ]
        )
    for group in copies:
        for copy in group:
            copy.start()
    rows, lanes = gates.shape[1], gain.shape[1]
    shape = (rows, lanes)
    diagonal = lax.broadcasted_iota(jnp.int32, shape, 0) == lax.broadcasted_iota(jnp.int32, shape, 1)
    at_zero = (me == 0) & (lax.broadcasted_iota(jnp.int32, filters.shape[1:], 1) == 0)
    for k, (mask, group, out) in enumerate(zip(masks, copies, outs)):
        row = gain[pl.ds(me ^ mask, 1), :]
        column = jnp.sum(jnp.where(diagonal, row, 0.0), axis=1, keepdims=True)
        for copy in group:
            copy.wait()
        out[0] = elementwise(gates[k], values[k])
        out[1] = (filters[k] * scale + jnp.where(at_zero, column, 0.0)).astype(BF16)


def prepare_call(masks, scale, inner_gate, signal, taps, gain):
    count, (rows, lanes) = len(masks), taps.shape[1:]
    out = jax.ShapeDtypeStruct((2, rows, lanes), BF16)
    anywhere = pl.BlockSpec(memory_space=pl.ANY)
    inside = pl.BlockSpec(memory_space=pltpu.VMEM)
    return pl.pallas_call(
        functools.partial(prepare_kernel, masks, scale),
        in_specs=[anywhere, anywhere, anywhere, inside],
        out_specs=[inside] * count,
        out_shape=[out] * count,
        scratch_shapes=[
            pltpu.VMEM((count, rows, lanes), BF16),
            pltpu.VMEM((count, rows, lanes), BF16),
            pltpu.VMEM((count, rows, lanes), F32),
            pltpu.SemaphoreType.DMA((count, 3)),
        ],
        compiler_params=pltpu.CompilerParams(vmem_limit_bytes=62 * 1024 * 1024),
        cost_estimate=pl.CostEstimate(
            flops=8 * count * rows * lanes, bytes_accessed=12 * count * rows * lanes, transcendentals=0
        ),
    )(inner_gate, signal, taps, gain)


def project_kernel(chunks, members, me, *refs):
    weights, blocks = refs[:members], refs[members : 2 * members]
    gate, upstream, *outs = refs[2 * members :]
    step = pl.program_id(0)
    rows = weights[0].shape[0] // 2
    total = jnp.dot(weights[0][...], blocks[0][...], preferred_element_type=F32)
    for weight, block in zip(weights[1:], blocks[1:]):
        total += jnp.dot(weight[...], block[...], preferred_element_type=F32)
    total = total.astype(BF16)
    upstream[...] = total.reshape(upstream.shape)
    low = elementwise(total[:rows], gate[0])
    high = elementwise(total[rows:], gate[1])
    swapped = (me[0] & 1) == 1
    place = partners(chunks).index
    for pair in range(chunks // 2):

        @pl.when(step == pair)
        def _():
            outs[place(2 * pair)][...] = jnp.where(swapped, high, low)
            outs[place(2 * pair + 1)][...] = jnp.where(swapped, low, high)


def outer_kernel(chunks, me, upstream, *refs):
    chunk, out = refs[:chunks], refs[chunks]
    for d, piece in zip(partners(chunks), chunk):
        at = me[0] ^ d
        out[at] = elementwise(upstream[at], piece[...])


def finish_kernel(count, me, *refs):
    gates, refs = refs[:count], refs[count:]
    values, refs = refs[:count], refs[count:]
    chunk, (grad_inner, grad_signal, grad_taps) = refs[:count], refs[-3:]
    step = pl.program_id(0)
    for k in range(count):

        @pl.when(step == k)
        def _(k=k):
            back = chunk[k][0]
            grad_inner[0] = elementwise(back, values[k][0])
            grad_signal[0] = elementwise(back, gates[k][0])
            grad_taps[0] = chunk[k][1].astype(F32)


def finish_call(me, masks, inner_gate, signal, chunks, earlier):
    count, shape = len(masks), inner_gate.shape
    block = (1,) + shape[1:]

    def place(i, me):
        mask = masks[0]
        for k in range(1, count):
            mask = jnp.where(i == k, masks[k], mask)
        return (me[0] ^ mask, 0, 0)

    gates = [pl.BlockSpec(block, lambda i, me, mask=mask: (me[0] ^ mask, 0, 0)) for mask in masks]
    pieces = [pl.BlockSpec(chunk.shape, lambda i, me: (0, 0, 0)) for chunk in chunks]
    return pl.pallas_call(
        functools.partial(finish_kernel, count),
        grid_spec=pltpu.PrefetchScalarGridSpec(
            num_scalar_prefetch=1,
            grid=(count,),
            in_specs=gates * 2 + pieces + [pl.BlockSpec(memory_space=pl.ANY)] * len(earlier),
            out_specs=[pl.BlockSpec(block, place)] * 3,
        ),
        out_shape=[jax.ShapeDtypeStruct(shape, dtype) for dtype in (BF16, BF16, F32)],
        input_output_aliases={1 + 3 * count + n: n for n in range(len(earlier))},
        compiler_params=pltpu.CompilerParams(vmem_limit_bytes=32 * 1024 * 1024),
        cost_estimate=pl.CostEstimate(
            flops=2 * count * math.prod(shape[1:]),
            bytes_accessed=16 * count * math.prod(shape[1:]),
            transcendentals=0,
        ),
    )(me, *[inner_gate] * count, *[signal] * count, *chunks, *earlier)


def rowwise_call(kernel, me, wholes, pieces, out_shapes, rows, limit=32):
    def spec(shape):
        lead = shape[:-2]
        return pl.BlockSpec(
            lead + (rows, shape[-1]), lambda i, me: (0,) * len(lead) + (i, 0)
        )

    channels = wholes[0].shape[1]
    size = sum(math.prod(x.shape) * x.dtype.itemsize for x in (*wholes, *pieces, *out_shapes))
    return pl.pallas_call(
        kernel,
        grid_spec=pltpu.PrefetchScalarGridSpec(
            num_scalar_prefetch=1,
            grid=(channels // rows,),
            in_specs=[spec(x.shape) for x in (*wholes, *pieces)],
            out_specs=[spec(x.shape) for x in out_shapes],
        ),
        out_shape=out_shapes,
        compiler_params=pltpu.CompilerParams(vmem_limit_bytes=limit * 1024 * 1024),
        cost_estimate=pl.CostEstimate(flops=size, bytes_accessed=size, transcendentals=0),
    )(me, *wholes, *pieces)


def project_call(me, weight, blocks, gate):
    chunks, channels, local = gate.shape
    members, depth = len(blocks), blocks[0].shape[0]

    def pair(i, me):
        return (me[0] >> 1) ^ i

    rows = 2 * channels
    return pl.pallas_call(
        functools.partial(project_kernel, chunks, members),
        grid_spec=pltpu.PrefetchScalarGridSpec(
            num_scalar_prefetch=1,
            grid=(chunks // 2,),
            in_specs=[
                pl.BlockSpec((rows, depth), lambda i, me, j=j: (pair(i, me), me[1] ^ j))
                for j in range(members)
            ]
            + [pl.BlockSpec((depth, local), lambda i, me: (0, 0))] * members
            + [pl.BlockSpec((2, channels, local), lambda i, me: (pair(i, me), 0, 0))],
            out_specs=[pl.BlockSpec((2, channels, local), lambda i, me: (pair(i, me), 0, 0))]
            + [pl.BlockSpec((channels, local), lambda i, me: (0, 0))] * chunks,
        ),
        out_shape=[jax.ShapeDtypeStruct(gate.shape, BF16)]
        + [jax.ShapeDtypeStruct((channels, local), BF16)] * chunks,
        compiler_params=pltpu.CompilerParams(vmem_limit_bytes=40 * 1024 * 1024),
        cost_estimate=pl.CostEstimate(
            flops=2 * weight.size * local, bytes_accessed=2 * weight.size, transcendentals=0
        ),
    )(me, *[weight] * members, *blocks, gate)


def gather_start(block):
    count = lax.axis_size("group")
    return lax.ppermute(block, "group", [(g, g ^ (count // 2)) for g in range(count)])


def gather_rest(block, far, other):
    count = lax.axis_size("group")
    bit = count // 2
    held = {0: block, bit: far}
    bit //= 2
    while bit:
        pairs = [(g, g ^ bit) for g in range(count)]
        for j in list(held):
            sent = held[j]
            if j:
                sent, _ = lax.optimization_barrier((sent, other))
            held[j ^ bit] = lax.ppermute(sent, "group", pairs)
        bit //= 2
    return [held[j] for j in range(count)]


def send(part, d, count):
    return lax.ppermute(part, "ctx", [(p, p ^ d) for p in range(count)])


def exchange(parts):
    count = len(parts)
    order = partners(count)
    if count > 8:
        blocks = lax.axis_index("ctx") ^ jnp.arange(count)
        where = np.argsort(order)
        sent = jnp.take(jnp.take(jnp.stack(parts), where, axis=0), blocks, axis=0)
        came = lax.all_to_all(sent, "ctx", split_axis=0, concat_axis=0, tiled=True)
        return list(jnp.take(jnp.take(came, blocks, axis=0), np.array(order), axis=0))
    return [parts[0]] + [send(part, d, count) for d, part in zip(order[1:], parts[1:])]


def after(parts, other):
    held, _ = lax.optimization_barrier((parts[0], other))
    return [held] + list(parts[1:])


def per_device(outer_gate, inner_gate, signal, cotangent, out_weight, filter_taps, skip_gain):
    ch_dev, tok_local = outer_gate.shape
    n_ctx = lax.axis_size("ctx")
    ch_slice = ch_dev // n_ctx
    seq_len = n_ctx * tok_local
    inner = seq_len // SLABS
    scale = 1.0 / math.sqrt(seq_len)
    me = jnp.stack([lax.axis_index("ctx"), lax.axis_index("group")])

    def split(array):
        return array.reshape(n_ctx, ch_slice, -1)

    def flat(array):
        return array.reshape(ch_dev, tok_local)

    def shapes(lead, dtype, count):
        return [jax.ShapeDtypeStruct(lead + (ch_slice, tok_local), dtype)] * count

    tables = [jnp.asarray(table) for table in make_tables(inner, n_ctx)]
    tables = [table if table.ndim == 2 else table[me[0]] for table in tables]
    masks = partners(n_ctx)
    first = min(3, n_ctx)
    sources = (scale, split(inner_gate), split(signal), split(filter_taps), split(skip_gain)[:, :, 0])
    head = prepare_call(masks[1:first], *sources)
    cotangent, _ = lax.optimization_barrier((cotangent, head[0]))
    far = gather_start(cotangent)
    own, *rest = prepare_call([0] + masks[first:], *sources)
    pair = exchange([own, *head, *rest])
    gathered = gather_rest(cotangent, far, (pair[1:first], pair[-1:], rest[:1], tables[:2]))
    pair_sent = [pair[k] for k in pair_order(n_ctx)]
    upstream, *grad = project_call(me, out_weight, gathered, split(outer_gate))
    response = conv_call(
        functools.partial(response_kernel, n_ctx, inner), me, (after(pair_sent, grad[0]),), tables, (), inner, 3
    )
    grad_came = exchange(grad)
    resp_came = exchange(response)
    backs = conv_call(
        functools.partial(backward_kernel, n_ctx, inner, scale),
        me,
        (pair_sent, after([grad_came[k] for k in grad_order(n_ctx)], response[0])),
        tables,
        (2,),
        inner,
        5,
    )
    backs_came = exchange(backs)
    (grad_outer,) = rowwise_call(
        functools.partial(outer_kernel, n_ctx),
        me,
        (upstream,),
        after(resp_came, backs[0]),
        shapes((n_ctx,), BF16, 1),
        32,
    )
    outs = []
    last = range(3, 5)
    for part in ([k for k in range(n_ctx) if k not in last], last):
        outs = finish_call(
            me,
            [masks[k] for k in part],
            split(inner_gate),
            split(signal),
            [backs_came[k] for k in part],
            outs,
        )
    grad_inner, grad_signal, grad_taps = outs
    return (flat(grad_outer), flat(grad_inner), flat(grad_signal), flat(grad_taps))


def solution(mesh):
    in_specs = (
        P("group", "ctx"),
        P("group", "ctx"),
        P("group", "ctx"),
        P("group", "ctx"),
        P("group", None),
        P("group", "ctx"),
        P("group"),
    )
    out_specs = (P("group", "ctx"), P("group", "ctx"), P("group", "ctx"), P("group", "ctx"))
    return jax.shard_map(
        per_device, mesh=mesh, in_specs=in_specs, out_specs=out_specs, check_vma=False
    )
```

```python
import functools
import math

import jax
import jax.numpy as jnp
import ml_dtypes
import numpy as np
from jax import lax
from jax.experimental import pallas as pl
from jax.experimental.pallas import tpu as pltpu
from jax.sharding import PartitionSpec as P

SLABS = 32
GROUP = 8
STEP = 2 * GROUP
F32 = jnp.float32
BF16 = jnp.bfloat16


def partners(count):
    return [0] + list(reversed(range(1, count)))


def make_tables(inner, chunks):
    slab = np.arange(SLABS)
    freq = np.arange(SLABS) + 0.5
    angle = 2.0 * np.pi / (2 * SLABS) * np.outer(freq, slab)
    eye = np.eye(GROUP)
    first = np.concatenate([np.kron(np.cos(angle), eye), np.kron(-np.sin(angle), eye)], axis=0)
    blocks = first.reshape(first.shape[0], chunks, -1)
    order = np.array(partners(chunks))
    first = np.stack([blocks[:, order ^ p].reshape(first.shape) for p in range(chunks)])
    last = first.transpose(0, 2, 1)
    within = np.arange(inner)
    turn = np.repeat(2.0 * np.pi / (2 * SLABS * inner) * np.outer(freq, within), GROUP, axis=0)
    circle = 2.0 * np.pi / inner * (np.outer(within, within) % inner)
    cos, sin = np.cos(circle), np.sin(circle)
    forward = np.block([[cos, -sin], [sin, cos]])
    narrow = ml_dtypes.bfloat16
    return (
        first.astype(narrow),
        last.astype(narrow),
        np.cos(turn).astype(np.float32),
        np.sin(turn).astype(np.float32),
        forward.astype(narrow),
        forward.T.astype(narrow),
    )


def gather_slabs(blocks, inner):
    local = blocks[0].shape[1]
    wide = [block.astype(F32) for block in blocks]
    halves = []
    for half in range(2):
        rows = slice(half * GROUP, (half + 1) * GROUP)
        pieces = [block[rows, at : at + inner] for block in wide for at in range(0, local, inner)]
        halves.append(jnp.concatenate(pieces, axis=0))
    return jnp.concatenate(halves, axis=1).astype(BF16)


def forward_dft(rows, first, cos, sin, forward, inner):
    stage = jnp.dot(first, rows, preferred_element_type=F32)
    half_rows = SLABS * GROUP
    turned = []
    for half in range(2):
        lanes = slice(half * inner, (half + 1) * inner)
        real, imag = stage[:half_rows, lanes], stage[half_rows:, lanes]
        turned.append(
            jnp.concatenate([real * cos + imag * sin, imag * cos - real * sin], axis=1).astype(BF16)
        )
    spec = jnp.dot(jnp.concatenate(turned, axis=0), forward, preferred_element_type=F32)
    return (spec[:, :inner], spec[:, inner:])


def inverse_dft(spec, last, cos, sin, backward, inner):
    both = jnp.concatenate(spec, axis=1).astype(BF16)
    stage = jnp.dot(both, backward, preferred_element_type=F32)
    half_rows = SLABS * GROUP
    turned = []
    for half in range(2):
        rows = slice(half * half_rows, (half + 1) * half_rows)
        real, imag = stage[rows, :inner], stage[rows, inner:]
        turned.append(
            jnp.concatenate([real * cos - imag * sin, imag * cos + real * sin], axis=0).astype(BF16)
        )
    return jnp.dot(last, jnp.concatenate(turned, axis=1), preferred_element_type=F32)


def scatter_slabs(rows, scale, outs, lead, inner):
    local = outs[0].shape[-1]
    per = local // inner
    scaled = rows * scale
    for src, out in enumerate(outs):
        for part in range(per):
            at = (src * per + part) * GROUP
            tile = jnp.concatenate(
                [scaled[at : at + GROUP, :inner], scaled[at : at + GROUP, inner:]], axis=0
            ).astype(BF16)
            lanes = slice(part * inner, (part + 1) * inner)
            if lead is None:
                out[:, lanes] = tile
            else:
                out[lead, :, lanes] = tile


def times_plain(left, right):
    return (left[0] * right[0] - left[1] * right[1], left[0] * right[1] + left[1] * right[0])


def times_conj(left, right):
    return (left[0] * right[0] + left[1] * right[1], left[1] * right[0] - left[0] * right[1])


def pair_order(chunks):
    half = chunks // 2
    return [*range(half), *range(half + 1, chunks - 1), half, chunks - 1]


def grad_order(chunks):
    half = chunks // 2
    return [0, 1, *range(half + 1, chunks), *range(2, half + 1)]


def in_place(refs, order):
    return [refs[order.index(k)] for k in range(len(refs))]


def response_kernel(chunks, inner, me, *refs):
    pair, refs = in_place(refs[:chunks], pair_order(chunks)), refs[chunks:]
    (first, last, cos, sin, forward, backward), outs = refs[:6], refs[6:]
    tables = (first[...], cos[...], sin[...], forward[...], inner)
    prod = forward_dft(gather_slabs([ref[0] for ref in pair], inner), *tables)
    taps = forward_dft(gather_slabs([ref[1] for ref in pair], inner), *tables)
    rows = inverse_dft(times_plain(prod, taps), last[...], cos[...], sin[...], backward[...], inner)
    scatter_slabs(rows, 1.0 / (SLABS * inner), outs, None, inner)


def backward_kernel(chunks, inner, scale, me, *refs):
    pair, grad, refs = refs[:chunks], refs[chunks : 2 * chunks], refs[2 * chunks :]
    pair, grad = in_place(pair, pair_order(chunks)), in_place(grad, grad_order(chunks))
    (first, last, cos, sin, forward, backward), outs = refs[:6], refs[6:]
    tables = (first[...], cos[...], sin[...], forward[...], inner)
    back_tables = (last[...], cos[...], sin[...], backward[...], inner)
    grad_spec = forward_dft(gather_slabs([ref[...] for ref in grad], inner), *tables)
    taps = forward_dft(gather_slabs([ref[1] for ref in pair], inner), *tables)
    rows = inverse_dft(times_conj(grad_spec, taps), *back_tables)
    scatter_slabs(rows, 1.0 / (SLABS * inner), outs, 0, inner)
    prod = forward_dft(gather_slabs([ref[0] for ref in pair], inner), *tables)
    rows = inverse_dft(times_conj(grad_spec, prod), *back_tables)
    scatter_slabs(rows, scale / (SLABS * inner), outs, 1, inner)


def conv_call(kernel, me, operands, tables, lead, inner, transforms):
    chunks, shape = len(operands[0]), operands[0][0].shape
    channels, local = shape[-2:]
    def rows_of(shape):
        middle = shape[:-2]
        return pl.BlockSpec(
            middle + (STEP, local), lambda i, me: (0,) * len(middle) + (i, 0)
        )

    def whole(table):
        return pl.BlockSpec(table.shape, lambda i, me: (0, 0))

    out_shape = lead + (channels, local)
    rows = channels * SLABS
    flops = transforms * rows * (2 * (2 * inner) ** 2 + 4 * SLABS * GROUP * inner)
    flat = [chunk for operand in operands for chunk in operand]
    return pl.pallas_call(
        kernel,
        grid_spec=pltpu.PrefetchScalarGridSpec(
            num_scalar_prefetch=1,
            grid=(channels // STEP,),
            in_specs=[rows_of(chunk.shape) for chunk in flat] + [whole(t) for t in tables],
            out_specs=[rows_of(out_shape)] * chunks,
        ),
        out_shape=[jax.ShapeDtypeStruct(out_shape, BF16)] * chunks,
        compiler_params=pltpu.CompilerParams(vmem_limit_bytes=40 * 1024 * 1024),
        cost_estimate=pl.CostEstimate(
            flops=flops, bytes_accessed=2 * rows * inner * 4, transcendentals=0
        ),
    )(me, *flat, *tables)


def elementwise(left, right):
    return (left.astype(F32) * right.astype(F32)).astype(BF16)


def prepare_kernel(masks, scale, inner_gate, signal, taps, gain, *refs):
    count = len(masks)
    outs, (gates, values, filters, sems) = refs[:count], refs[count:]
    me = lax.axis_index("ctx")
    copies = []
    for k, mask in enumerate(masks):
        at = me ^ mask
        pairs = ((inner_gate, gates), (signal, values), (taps, filters))
        copies.append(
            [
                pltpu.make_async_copy(src.at[at], dst.at[k], sems.at[k, n])
                for n, (src, dst) in enumerate(pairs)
            ]
        )
    for group in copies:
        for copy in group:
            copy.start()
    rows, lanes = gates.shape[1], gain.shape[1]
    shape = (rows, lanes)
    diagonal = lax.broadcasted_iota(jnp.int32, shape, 0) == lax.broadcasted_iota(jnp.int32, shape, 1)
    at_zero = (me == 0) & (lax.broadcasted_iota(jnp.int32, filters.shape[1:], 1) == 0)
    for k, (mask, group, out) in enumerate(zip(masks, copies, outs)):
        row = gain[pl.ds(me ^ mask, 1), :]
        column = jnp.sum(jnp.where(diagonal, row, 0.0), axis=1, keepdims=True)
        for copy in group:
            copy.wait()
        out[0] = elementwise(gates[k], values[k])
        out[1] = (filters[k] * scale + jnp.where(at_zero, column, 0.0)).astype(BF16)


def prepare_call(masks, scale, inner_gate, signal, taps, gain):
    count, (rows, lanes) = len(masks), taps.shape[1:]
    out = jax.ShapeDtypeStruct((2, rows, lanes), BF16)
    anywhere = pl.BlockSpec(memory_space=pl.ANY)
    inside = pl.BlockSpec(memory_space=pltpu.VMEM)
    return pl.pallas_call(
        functools.partial(prepare_kernel, masks, scale),
        in_specs=[anywhere, anywhere, anywhere, inside],
        out_specs=[inside] * count,
        out_shape=[out] * count,
        scratch_shapes=[
            pltpu.VMEM((count, rows, lanes), BF16),
            pltpu.VMEM((count, rows, lanes), BF16),
            pltpu.VMEM((count, rows, lanes), F32),
            pltpu.SemaphoreType.DMA((count, 3)),
        ],
        compiler_params=pltpu.CompilerParams(vmem_limit_bytes=62 * 1024 * 1024),
        cost_estimate=pl.CostEstimate(
            flops=8 * count * rows * lanes, bytes_accessed=12 * count * rows * lanes, transcendentals=0
        ),
    )(inner_gate, signal, taps, gain)


def project_kernel(chunks, members, me, *refs):
    weights, blocks = refs[:members], refs[members : 2 * members]
    gate, upstream, *outs = refs[2 * members :]
    step = pl.program_id(0)
    rows = weights[0].shape[0] // 2
    total = jnp.dot(weights[0][...], blocks[0][...], preferred_element_type=F32)
    for weight, block in zip(weights[1:], blocks[1:]):
        total += jnp.dot(weight[...], block[...], preferred_element_type=F32)
    total = total.astype(BF16)
    upstream[...] = total.reshape(upstream.shape)
    low = elementwise(total[:rows], gate[0])
    high = elementwise(total[rows:], gate[1])
    swapped = (me[0] & 1) == 1
    place = partners(chunks).index
    for pair in range(chunks // 2):

        @pl.when(step == pair)
        def _():
            outs[place(2 * pair)][...] = jnp.where(swapped, high, low)
            outs[place(2 * pair + 1)][...] = jnp.where(swapped, low, high)


def outer_kernel(chunks, me, upstream, *refs):
    chunk, out = refs[:chunks], refs[chunks]
    for d, piece in zip(partners(chunks), chunk):
        at = me[0] ^ d
        out[at] = elementwise(upstream[at], piece[...])


def finish_kernel(count, me, *refs):
    gates, refs = refs[:count], refs[count:]
    values, refs = refs[:count], refs[count:]
    chunk, (grad_inner, grad_signal, grad_taps) = refs[:count], refs[-3:]
    step = pl.program_id(0)
    for k in range(count):

        @pl.when(step == k)
        def _(k=k):
            back = chunk[k][0]
            grad_inner[0] = elementwise(back, values[k][0])
            grad_signal[0] = elementwise(back, gates[k][0])
            grad_taps[0] = chunk[k][1].astype(F32)


def finish_call(me, masks, inner_gate, signal, chunks, earlier):
    count, shape = len(masks), inner_gate.shape
    block = (1,) + shape[1:]

    def place(i, me):
        mask = masks[0]
        for k in range(1, count):
            mask = jnp.where(i == k, masks[k], mask)
        return (me[0] ^ mask, 0, 0)

    gates = [pl.BlockSpec(block, lambda i, me, mask=mask: (me[0] ^ mask, 0, 0)) for mask in masks]
    pieces = [pl.BlockSpec(chunk.shape, lambda i, me: (0, 0, 0)) for chunk in chunks]
    return pl.pallas_call(
        functools.partial(finish_kernel, count),
        grid_spec=pltpu.PrefetchScalarGridSpec(
            num_scalar_prefetch=1,
            grid=(count,),
            in_specs=gates * 2 + pieces + [pl.BlockSpec(memory_space=pl.ANY)] * len(earlier),
            out_specs=[pl.BlockSpec(block, place)] * 3,
        ),
        out_shape=[jax.ShapeDtypeStruct(shape, dtype) for dtype in (BF16, BF16, F32)],
        input_output_aliases={1 + 3 * count + n: n for n in range(len(earlier))},
        compiler_params=pltpu.CompilerParams(vmem_limit_bytes=32 * 1024 * 1024),
        cost_estimate=pl.CostEstimate(
            flops=2 * count * math.prod(shape[1:]),
            bytes_accessed=16 * count * math.prod(shape[1:]),
            transcendentals=0,
        ),
    )(me, *[inner_gate] * count, *[signal] * count, *chunks, *earlier)


def rowwise_call(kernel, me, wholes, pieces, out_shapes, rows, limit=32):
    def spec(shape):
        lead = shape[:-2]
        return pl.BlockSpec(
            lead + (rows, shape[-1]), lambda i, me: (0,) * len(lead) + (i, 0)
        )

    channels = wholes[0].shape[1]
    size = sum(math.prod(x.shape) * x.dtype.itemsize for x in (*wholes, *pieces, *out_shapes))
    return pl.pallas_call(
        kernel,
        grid_spec=pltpu.PrefetchScalarGridSpec(
            num_scalar_prefetch=1,
            grid=(channels // rows,),
            in_specs=[spec(x.shape) for x in (*wholes, *pieces)],
            out_specs=[spec(x.shape) for x in out_shapes],
        ),
        out_shape=out_shapes,
        compiler_params=pltpu.CompilerParams(vmem_limit_bytes=limit * 1024 * 1024),
        cost_estimate=pl.CostEstimate(flops=size, bytes_accessed=size, transcendentals=0),
    )(me, *wholes, *pieces)


def project_call(me, weight, blocks, gate):
    chunks, channels, local = gate.shape
    members, depth = len(blocks), blocks[0].shape[0]

    def pair(i, me):
        return (me[0] >> 1) ^ i

    rows = 2 * channels
    return pl.pallas_call(
        functools.partial(project_kernel, chunks, members),
        grid_spec=pltpu.PrefetchScalarGridSpec(
            num_scalar_prefetch=1,
            grid=(chunks // 2,),
            in_specs=[
                pl.BlockSpec((rows, depth), lambda i, me, j=j: (pair(i, me), me[1] ^ j))
                for j in range(members)
            ]
            + [pl.BlockSpec((depth, local), lambda i, me: (0, 0))] * members
            + [pl.BlockSpec((2, channels, local), lambda i, me: (pair(i, me), 0, 0))],
            out_specs=[pl.BlockSpec((2, channels, local), lambda i, me: (pair(i, me), 0, 0))]
            + [pl.BlockSpec((channels, local), lambda i, me: (0, 0))] * chunks,
        ),
        out_shape=[jax.ShapeDtypeStruct(gate.shape, BF16)]
        + [jax.ShapeDtypeStruct((channels, local), BF16)] * chunks,
        compiler_params=pltpu.CompilerParams(vmem_limit_bytes=40 * 1024 * 1024),
        cost_estimate=pl.CostEstimate(
            flops=2 * weight.size * local, bytes_accessed=2 * weight.size, transcendentals=0
        ),
    )(me, *[weight] * members, *blocks, gate)


def gather_start(block):
    count = lax.axis_size("group")
    return lax.ppermute(block, "group", [(g, g ^ (count // 2)) for g in range(count)])


def gather_rest(block, far, other):
    count = lax.axis_size("group")
    bit = count // 2
    held = {0: block, bit: far}
    bit //= 2
    while bit:
        pairs = [(g, g ^ bit) for g in range(count)]
        for j in list(held):
            sent = held[j]
            if j:
                sent, _ = lax.optimization_barrier((sent, other))
            held[j ^ bit] = lax.ppermute(sent, "group", pairs)
        bit //= 2
    return [held[j] for j in range(count)]


def send(part, d, count):
    return lax.ppermute(part, "ctx", [(p, p ^ d) for p in range(count)])


def exchange(parts):
    count = len(parts)
    order = partners(count)
    if count > 8:
        blocks = lax.axis_index("ctx") ^ jnp.arange(count)
        where = np.argsort(order)
        sent = jnp.take(jnp.take(jnp.stack(parts), where, axis=0), blocks, axis=0)
        came = lax.all_to_all(sent, "ctx", split_axis=0, concat_axis=0, tiled=True)
        return list(jnp.take(jnp.take(came, blocks, axis=0), np.array(order), axis=0))
    return [parts[0]] + [send(part, d, count) for d, part in zip(order[1:], parts[1:])]


def after(parts, other):
    held, _ = lax.optimization_barrier((parts[0], other))
    return [held] + list(parts[1:])


def per_device(outer_gate, inner_gate, signal, cotangent, out_weight, filter_taps, skip_gain):
    ch_dev, tok_local = outer_gate.shape
    n_ctx = lax.axis_size("ctx")
    ch_slice = ch_dev // n_ctx
    seq_len = n_ctx * tok_local
    inner = seq_len // SLABS
    scale = 1.0 / math.sqrt(seq_len)
    me = jnp.stack([lax.axis_index("ctx"), lax.axis_index("group")])

    def split(array):
        return array.reshape(n_ctx, ch_slice, -1)

    def flat(array):
        return array.reshape(ch_dev, tok_local)

    def shapes(lead, dtype, count):
        return [jax.ShapeDtypeStruct(lead + (ch_slice, tok_local), dtype)] * count

    tables = [jnp.asarray(table) for table in make_tables(inner, n_ctx)]
    tables = [table if table.ndim == 2 else table[me[0]] for table in tables]
    masks = partners(n_ctx)
    first = min(3, n_ctx)
    sources = (scale, split(inner_gate), split(signal), split(filter_taps), split(skip_gain)[:, :, 0])
    head = prepare_call(masks[1:first], *sources)
    cotangent, _ = lax.optimization_barrier((cotangent, head[0]))
    far = gather_start(cotangent)
    own, *rest = prepare_call([0] + masks[first:], *sources)
    pair = exchange([own, *head, *rest])
    gathered = gather_rest(cotangent, far, (pair[1:first], pair[-1:], rest[:1], tables[:2]))
    pair_sent = [pair[k] for k in pair_order(n_ctx)]
    upstream, *grad = project_call(me, out_weight, gathered, split(outer_gate))
    response = conv_call(
        functools.partial(response_kernel, n_ctx, inner), me, (after(pair_sent, grad[0]),), tables, (), inner, 3
    )
    grad_came = exchange(grad)
    waiting, _ = lax.optimization_barrier((list(response[2:]), grad_came[1:]))
    resp_came = exchange([*response[:2], *waiting])
    backs = conv_call(
        functools.partial(backward_kernel, n_ctx, inner, scale),
        me,
        (pair_sent, after([grad_came[k] for k in grad_order(n_ctx)], response[0])),
        tables,
        (2,),
        inner,
        5,
    )
    backs_came = exchange(backs)
    (grad_outer,) = rowwise_call(
        functools.partial(outer_kernel, n_ctx),
        me,
        (upstream,),
        after(resp_came, backs[0]),
        shapes((n_ctx,), BF16, 1),
        32,
    )
    outs = []
    last = range(3, 5)
    for part in ([k for k in range(n_ctx) if k not in last], last):
        outs = finish_call(
            me,
            [masks[k] for k in part],
            split(inner_gate),
            split(signal),
            [backs_came[k] for k in part],
            outs,
        )
    grad_inner, grad_signal, grad_taps = outs
    return (flat(grad_outer), flat(grad_inner), flat(grad_signal), flat(grad_taps))


def solution(mesh):
    in_specs = (
        P("group", "ctx"),
        P("group", "ctx"),
        P("group", "ctx"),
        P("group", "ctx"),
        P("group", None),
        P("group", "ctx"),
        P("group"),
    )
    out_specs = (P("group", "ctx"), P("group", "ctx"), P("group", "ctx"), P("group", "ctx"))
    return jax.shard_map(
        per_device, mesh=mesh, in_specs=in_specs, out_specs=out_specs, check_vma=False
    )
```

```python
import functools
import math

import jax
import jax.numpy as jnp
import ml_dtypes
import numpy as np
from jax import lax
from jax.experimental import pallas as pl
from jax.experimental.pallas import tpu as pltpu
from jax.sharding import PartitionSpec as P

SLABS = 32
GROUP = 8
STEP = 2 * GROUP
F32 = jnp.float32
BF16 = jnp.bfloat16


def partners(count):
    return [0] + list(reversed(range(1, count)))


def make_tables(inner, chunks):
    slab = np.arange(SLABS)
    freq = np.arange(SLABS) + 0.5
    angle = 2.0 * np.pi / (2 * SLABS) * np.outer(freq, slab)
    eye = np.eye(GROUP)
    first = np.concatenate([np.kron(np.cos(angle), eye), np.kron(-np.sin(angle), eye)], axis=0)
    blocks = first.reshape(first.shape[0], chunks, -1)
    order = np.array(partners(chunks))
    first = np.stack([blocks[:, order ^ p].reshape(first.shape) for p in range(chunks)])
    last = first.transpose(0, 2, 1)
    within = np.arange(inner)
    turn = np.repeat(2.0 * np.pi / (2 * SLABS * inner) * np.outer(freq, within), GROUP, axis=0)
    circle = 2.0 * np.pi / inner * (np.outer(within, within) % inner)
    cos, sin = np.cos(circle), np.sin(circle)
    forward = np.block([[cos, -sin], [sin, cos]])
    narrow = ml_dtypes.bfloat16
    return (
        first.astype(narrow),
        last.astype(narrow),
        np.cos(turn).astype(np.float32),
        np.sin(turn).astype(np.float32),
        forward.astype(narrow),
        forward.T.astype(narrow),
    )


def gather_slabs(blocks, inner):
    local = blocks[0].shape[1]
    wide = [block.astype(F32) for block in blocks]
    halves = []
    for half in range(2):
        rows = slice(half * GROUP, (half + 1) * GROUP)
        pieces = [block[rows, at : at + inner] for block in wide for at in range(0, local, inner)]
        halves.append(jnp.concatenate(pieces, axis=0))
    return jnp.concatenate(halves, axis=1).astype(BF16)


def forward_dft(rows, first, cos, sin, forward, inner):
    stage = jnp.dot(first, rows, preferred_element_type=F32)
    half_rows = SLABS * GROUP
    turned = []
    for half in range(2):
        lanes = slice(half * inner, (half + 1) * inner)
        real, imag = stage[:half_rows, lanes], stage[half_rows:, lanes]
        turned.append(
            jnp.concatenate([real * cos + imag * sin, imag * cos - real * sin], axis=1).astype(BF16)
        )
    spec = jnp.dot(jnp.concatenate(turned, axis=0), forward, preferred_element_type=F32)
    return (spec[:, :inner], spec[:, inner:])


def inverse_dft(spec, last, cos, sin, backward, inner):
    both = jnp.concatenate(spec, axis=1).astype(BF16)
    stage = jnp.dot(both, backward, preferred_element_type=F32)
    half_rows = SLABS * GROUP
    turned = []
    for half in range(2):
        rows = slice(half * half_rows, (half + 1) * half_rows)
        real, imag = stage[rows, :inner], stage[rows, inner:]
        turned.append(
            jnp.concatenate([real * cos - imag * sin, imag * cos + real * sin], axis=0).astype(BF16)
        )
    return jnp.dot(last, jnp.concatenate(turned, axis=1), preferred_element_type=F32)


def scatter_slabs(rows, scale, outs, lead, at_rows, inner):
    local = outs[0].shape[-1]
    per = local // inner
    scaled = rows * scale
    for src, out in enumerate(outs):
        for part in range(per):
            at = (src * per + part) * GROUP
            tile = jnp.concatenate(
                [scaled[at : at + GROUP, :inner], scaled[at : at + GROUP, inner:]], axis=0
            ).astype(BF16)
            lanes = slice(part * inner, (part + 1) * inner)
            if lead is None:
                out[at_rows, lanes] = tile
            else:
                out[lead, at_rows, lanes] = tile


def times_plain(left, right):
    return (left[0] * right[0] - left[1] * right[1], left[0] * right[1] + left[1] * right[0])


def times_conj(left, right):
    return (left[0] * right[0] + left[1] * right[1], left[1] * right[0] - left[0] * right[1])


def pair_order(chunks):
    half = chunks // 2
    return [*range(half), *range(half + 1, chunks - 1), half, chunks - 1]


def grad_order(chunks):
    half = chunks // 2
    return [0, 1, *range(half + 1, chunks), *range(2, half + 1)]


def in_place(refs, order):
    return [refs[order.index(k)] for k in range(len(refs))]


def response_kernel(chunks, inner, me, *refs):
    pair, refs = in_place(refs[:chunks], pair_order(chunks)), refs[chunks:]
    (first, last, cos, sin, forward, backward), outs = refs[:6], refs[6:]
    tables = (first[...], cos[...], sin[...], forward[...], inner)
    for at in range(0, outs[0].shape[-2], STEP):
        rows = slice(at, at + STEP)
        prod = forward_dft(gather_slabs([ref[0, rows] for ref in pair], inner), *tables)
        taps = forward_dft(gather_slabs([ref[1, rows] for ref in pair], inner), *tables)
        result = inverse_dft(
            times_plain(prod, taps), last[...], cos[...], sin[...], backward[...], inner
        )
        scatter_slabs(result, 1.0 / (SLABS * inner), outs, None, rows, inner)


def backward_kernel(chunks, inner, scale, me, *refs):
    pair, grad, refs = refs[:chunks], refs[chunks : 2 * chunks], refs[2 * chunks :]
    pair, grad = in_place(pair, pair_order(chunks)), in_place(grad, grad_order(chunks))
    (first, last, cos, sin, forward, backward), outs = refs[:6], refs[6:]
    tables = (first[...], cos[...], sin[...], forward[...], inner)
    back_tables = (last[...], cos[...], sin[...], backward[...], inner)
    for at in range(0, outs[0].shape[-2], STEP):
        rows = slice(at, at + STEP)
        grad_spec = forward_dft(gather_slabs([ref[rows] for ref in grad], inner), *tables)
        taps = forward_dft(gather_slabs([ref[1, rows] for ref in pair], inner), *tables)
        result = inverse_dft(times_conj(grad_spec, taps), *back_tables)
        scatter_slabs(result, 1.0 / (SLABS * inner), outs, 0, rows, inner)
        prod = forward_dft(gather_slabs([ref[0, rows] for ref in pair], inner), *tables)
        result = inverse_dft(times_conj(grad_spec, prod), *back_tables)
        scatter_slabs(result, scale / (SLABS * inner), outs, 1, rows, inner)


def conv_call(kernel, me, operands, tables, lead, inner, transforms):
    chunks, shape = len(operands[0]), operands[0][0].shape
    channels, local = shape[-2:]
    def rows_of(shape):
        middle = shape[:-2]
        return pl.BlockSpec(
            middle + (2 * STEP, local), lambda i, me: (0,) * len(middle) + (i, 0)
        )

    def whole(table):
        return pl.BlockSpec(table.shape, lambda i, me: (0, 0))

    out_shape = lead + (channels, local)
    rows = channels * SLABS
    flops = transforms * rows * (2 * (2 * inner) ** 2 + 4 * SLABS * GROUP * inner)
    flat = [chunk for operand in operands for chunk in operand]
    return pl.pallas_call(
        kernel,
        grid_spec=pltpu.PrefetchScalarGridSpec(
            num_scalar_prefetch=1,
            grid=(channels // (2 * STEP),),
            in_specs=[rows_of(chunk.shape) for chunk in flat] + [whole(t) for t in tables],
            out_specs=[rows_of(out_shape)] * chunks,
        ),
        out_shape=[jax.ShapeDtypeStruct(out_shape, BF16)] * chunks,
        compiler_params=pltpu.CompilerParams(vmem_limit_bytes=40 * 1024 * 1024),
        cost_estimate=pl.CostEstimate(
            flops=flops, bytes_accessed=2 * rows * inner * 4, transcendentals=0
        ),
    )(me, *flat, *tables)


def elementwise(left, right):
    return (left.astype(F32) * right.astype(F32)).astype(BF16)


def prepare_kernel(masks, scale, inner_gate, signal, taps, gain, *refs):
    count = len(masks)
    outs, (gates, values, filters, sems) = refs[:count], refs[count:]
    me = lax.axis_index("ctx")
    copies = []
    for k, mask in enumerate(masks):
        at = me ^ mask
        pairs = ((inner_gate, gates), (signal, values), (taps, filters))
        copies.append(
            [
                pltpu.make_async_copy(src.at[at], dst.at[k], sems.at[k, n])
                for n, (src, dst) in enumerate(pairs)
            ]
        )
    for group in copies:
        for copy in group:
            copy.start()
    rows, lanes = gates.shape[1], gain.shape[1]
    shape = (rows, lanes)
    diagonal = lax.broadcasted_iota(jnp.int32, shape, 0) == lax.broadcasted_iota(jnp.int32, shape, 1)
    at_zero = (me == 0) & (lax.broadcasted_iota(jnp.int32, filters.shape[1:], 1) == 0)
    for k, (mask, group, out) in enumerate(zip(masks, copies, outs)):
        row = gain[pl.ds(me ^ mask, 1), :]
        column = jnp.sum(jnp.where(diagonal, row, 0.0), axis=1, keepdims=True)
        for copy in group:
            copy.wait()
        out[0] = elementwise(gates[k], values[k])
        out[1] = (filters[k] * scale + jnp.where(at_zero, column, 0.0)).astype(BF16)


def prepare_call(masks, scale, inner_gate, signal, taps, gain):
    count, (rows, lanes) = len(masks), taps.shape[1:]
    out = jax.ShapeDtypeStruct((2, rows, lanes), BF16)
    anywhere = pl.BlockSpec(memory_space=pl.ANY)
    inside = pl.BlockSpec(memory_space=pltpu.VMEM)
    return pl.pallas_call(
        functools.partial(prepare_kernel, masks, scale),
        in_specs=[anywhere, anywhere, anywhere, inside],
        out_specs=[inside] * count,
        out_shape=[out] * count,
        scratch_shapes=[
            pltpu.VMEM((count, rows, lanes), BF16),
            pltpu.VMEM((count, rows, lanes), BF16),
            pltpu.VMEM((count, rows, lanes), F32),
            pltpu.SemaphoreType.DMA((count, 3)),
        ],
        compiler_params=pltpu.CompilerParams(vmem_limit_bytes=62 * 1024 * 1024),
        cost_estimate=pl.CostEstimate(
            flops=8 * count * rows * lanes, bytes_accessed=12 * count * rows * lanes, transcendentals=0
        ),
    )(inner_gate, signal, taps, gain)


def project_kernel(chunks, members, me, *refs):
    weights, blocks = refs[:members], refs[members : 2 * members]
    gate, upstream, *outs = refs[2 * members :]
    step = pl.program_id(0)
    rows = weights[0].shape[0] // 2
    total = jnp.dot(weights[0][...], blocks[0][...], preferred_element_type=F32)
    for weight, block in zip(weights[1:], blocks[1:]):
        total += jnp.dot(weight[...], block[...], preferred_element_type=F32)
    total = total.astype(BF16)
    upstream[...] = total.reshape(upstream.shape)
    low = elementwise(total[:rows], gate[0])
    high = elementwise(total[rows:], gate[1])
    swapped = (me[0] & 1) == 1
    place = partners(chunks).index
    for pair in range(chunks // 2):

        @pl.when(step == pair)
        def _():
            outs[place(2 * pair)][...] = jnp.where(swapped, high, low)
            outs[place(2 * pair + 1)][...] = jnp.where(swapped, low, high)


def outer_kernel(chunks, me, upstream, *refs):
    chunk, out = refs[:chunks], refs[chunks]
    for d, piece in zip(partners(chunks), chunk):
        at = me[0] ^ d
        out[at] = elementwise(upstream[at], piece[...])


def finish_kernel(count, me, *refs):
    gates, refs = refs[:count], refs[count:]
    values, refs = refs[:count], refs[count:]
    chunk, (grad_inner, grad_signal, grad_taps) = refs[:count], refs[-3:]
    step = pl.program_id(0)
    for k in range(count):

        @pl.when(step == k)
        def _(k=k):
            back = chunk[k][0]
            grad_inner[0] = elementwise(back, values[k][0])
            grad_signal[0] = elementwise(back, gates[k][0])
            grad_taps[0] = chunk[k][1].astype(F32)


def finish_call(me, masks, inner_gate, signal, chunks, earlier):
    count, shape = len(masks), inner_gate.shape
    block = (1,) + shape[1:]

    def place(i, me):
        mask = masks[0]
        for k in range(1, count):
            mask = jnp.where(i == k, masks[k], mask)
        return (me[0] ^ mask, 0, 0)

    gates = [pl.BlockSpec(block, lambda i, me, mask=mask: (me[0] ^ mask, 0, 0)) for mask in masks]
    pieces = [pl.BlockSpec(chunk.shape, lambda i, me: (0, 0, 0)) for chunk in chunks]
    return pl.pallas_call(
        functools.partial(finish_kernel, count),
        grid_spec=pltpu.PrefetchScalarGridSpec(
            num_scalar_prefetch=1,
            grid=(count,),
            in_specs=gates * 2 + pieces + [pl.BlockSpec(memory_space=pl.ANY)] * len(earlier),
            out_specs=[pl.BlockSpec(block, place)] * 3,
        ),
        out_shape=[jax.ShapeDtypeStruct(shape, dtype) for dtype in (BF16, BF16, F32)],
        input_output_aliases={1 + 3 * count + n: n for n in range(len(earlier))},
        compiler_params=pltpu.CompilerParams(vmem_limit_bytes=32 * 1024 * 1024),
        cost_estimate=pl.CostEstimate(
            flops=2 * count * math.prod(shape[1:]),
            bytes_accessed=16 * count * math.prod(shape[1:]),
            transcendentals=0,
        ),
    )(me, *[inner_gate] * count, *[signal] * count, *chunks, *earlier)


def rowwise_call(kernel, me, wholes, pieces, out_shapes, rows, limit=32):
    def spec(shape):
        lead = shape[:-2]
        return pl.BlockSpec(
            lead + (rows, shape[-1]), lambda i, me: (0,) * len(lead) + (i, 0)
        )

    channels = wholes[0].shape[1]
    size = sum(math.prod(x.shape) * x.dtype.itemsize for x in (*wholes, *pieces, *out_shapes))
    return pl.pallas_call(
        kernel,
        grid_spec=pltpu.PrefetchScalarGridSpec(
            num_scalar_prefetch=1,
            grid=(channels // rows,),
            in_specs=[spec(x.shape) for x in (*wholes, *pieces)],
            out_specs=[spec(x.shape) for x in out_shapes],
        ),
        out_shape=out_shapes,
        compiler_params=pltpu.CompilerParams(vmem_limit_bytes=limit * 1024 * 1024),
        cost_estimate=pl.CostEstimate(flops=size, bytes_accessed=size, transcendentals=0),
    )(me, *wholes, *pieces)


def project_call(me, weight, blocks, gate):
    chunks, channels, local = gate.shape
    members, depth = len(blocks), blocks[0].shape[0]

    def pair(i, me):
        return (me[0] >> 1) ^ i

    rows = 2 * channels
    return pl.pallas_call(
        functools.partial(project_kernel, chunks, members),
        grid_spec=pltpu.PrefetchScalarGridSpec(
            num_scalar_prefetch=1,
            grid=(chunks // 2,),
            in_specs=[
                pl.BlockSpec((rows, depth), lambda i, me, j=j: (pair(i, me), me[1] ^ j))
                for j in range(members)
            ]
            + [pl.BlockSpec((depth, local), lambda i, me: (0, 0))] * members
            + [pl.BlockSpec((2, channels, local), lambda i, me: (pair(i, me), 0, 0))],
            out_specs=[pl.BlockSpec((2, channels, local), lambda i, me: (pair(i, me), 0, 0))]
            + [pl.BlockSpec((channels, local), lambda i, me: (0, 0))] * chunks,
        ),
        out_shape=[jax.ShapeDtypeStruct(gate.shape, BF16)]
        + [jax.ShapeDtypeStruct((channels, local), BF16)] * chunks,
        compiler_params=pltpu.CompilerParams(vmem_limit_bytes=40 * 1024 * 1024),
        cost_estimate=pl.CostEstimate(
            flops=2 * weight.size * local, bytes_accessed=2 * weight.size, transcendentals=0
        ),
    )(me, *[weight] * members, *blocks, gate)


def gather_start(block):
    count = lax.axis_size("group")
    return lax.ppermute(block, "group", [(g, g ^ (count // 2)) for g in range(count)])


def gather_rest(block, far, other):
    count = lax.axis_size("group")
    bit = count // 2
    held = {0: block, bit: far}
    bit //= 2
    while bit:
        pairs = [(g, g ^ bit) for g in range(count)]
        for j in list(held):
            sent = held[j]
            if j:
                sent, _ = lax.optimization_barrier((sent, other))
            held[j ^ bit] = lax.ppermute(sent, "group", pairs)
        bit //= 2
    return [held[j] for j in range(count)]


def send(part, d, count):
    return lax.ppermute(part, "ctx", [(p, p ^ d) for p in range(count)])


def exchange(parts):
    count = len(parts)
    order = partners(count)
    if count > 8:
        blocks = lax.axis_index("ctx") ^ jnp.arange(count)
        where = np.argsort(order)
        sent = jnp.take(jnp.take(jnp.stack(parts), where, axis=0), blocks, axis=0)
        came = lax.all_to_all(sent, "ctx", split_axis=0, concat_axis=0, tiled=True)
        return list(jnp.take(jnp.take(came, blocks, axis=0), np.array(order), axis=0))
    return [parts[0]] + [send(part, d, count) for d, part in zip(order[1:], parts[1:])]


def after(parts, other):
    held, _ = lax.optimization_barrier((parts[0], other))
    return [held] + list(parts[1:])


def per_device(outer_gate, inner_gate, signal, cotangent, out_weight, filter_taps, skip_gain):
    ch_dev, tok_local = outer_gate.shape
    n_ctx = lax.axis_size("ctx")
    ch_slice = ch_dev // n_ctx
    seq_len = n_ctx * tok_local
    inner = seq_len // SLABS
    scale = 1.0 / math.sqrt(seq_len)
    me = jnp.stack([lax.axis_index("ctx"), lax.axis_index("group")])

    def split(array):
        return array.reshape(n_ctx, ch_slice, -1)

    def flat(array):
        return array.reshape(ch_dev, tok_local)

    def shapes(lead, dtype, count):
        return [jax.ShapeDtypeStruct(lead + (ch_slice, tok_local), dtype)] * count

    tables = [jnp.asarray(table) for table in make_tables(inner, n_ctx)]
    tables = [table if table.ndim == 2 else table[me[0]] for table in tables]
    masks = partners(n_ctx)
    first = min(3, n_ctx)
    sources = (scale, split(inner_gate), split(signal), split(filter_taps), split(skip_gain)[:, :, 0])
    head = prepare_call(masks[1:first], *sources)
    cotangent, _ = lax.optimization_barrier((cotangent, head[0]))
    far = gather_start(cotangent)
    own, *rest = prepare_call([0] + masks[first:], *sources)
    pair = exchange([own, *head, *rest])
    gathered = gather_rest(cotangent, far, (pair[1:first], pair[-1:], rest[:1], tables[:2]))
    pair_sent = [pair[k] for k in pair_order(n_ctx)]
    upstream, *grad = project_call(me, out_weight, gathered, split(outer_gate))
    response = conv_call(
        functools.partial(response_kernel, n_ctx, inner), me, (after(pair_sent, grad[0]),), tables, (), inner, 3
    )
    grad_came = exchange(grad)
    resp_came = exchange(response)
    backs = conv_call(
        functools.partial(backward_kernel, n_ctx, inner, scale),
        me,
        (pair_sent, after([grad_came[k] for k in grad_order(n_ctx)], response[0])),
        tables,
        (2,),
        inner,
        5,
    )
    backs_came = exchange(backs)
    (grad_outer,) = rowwise_call(
        functools.partial(outer_kernel, n_ctx),
        me,
        (upstream,),
        after(resp_came, backs[0]),
        shapes((n_ctx,), BF16, 1),
        32,
    )
    outs = []
    last = range(3, 5)
    for part in ([k for k in range(n_ctx) if k not in last], last):
        outs = finish_call(
            me,
            [masks[k] for k in part],
            split(inner_gate),
            split(signal),
            [backs_came[k] for k in part],
            outs,
        )
    grad_inner, grad_signal, grad_taps = outs
    return (flat(grad_outer), flat(grad_inner), flat(grad_signal), flat(grad_taps))


def solution(mesh):
    in_specs = (
        P("group", "ctx"),
        P("group", "ctx"),
        P("group", "ctx"),
        P("group", "ctx"),
        P("group", None),
        P("group", "ctx"),
        P("group"),
    )
    out_specs = (P("group", "ctx"), P("group", "ctx"), P("group", "ctx"), P("group", "ctx"))
    return jax.shard_map(
        per_device, mesh=mesh, in_specs=in_specs, out_specs=out_specs, check_vma=False
    )
```

```python
import functools
import math

import jax
import jax.numpy as jnp
import ml_dtypes
import numpy as np
from jax import lax
from jax.experimental import pallas as pl
from jax.experimental.pallas import tpu as pltpu
from jax.sharding import PartitionSpec as P

SLABS = 32
GROUP = 8
STEP = 2 * GROUP
F32 = jnp.float32
BF16 = jnp.bfloat16


def partners(count):
    return [0] + list(reversed(range(1, count)))


def make_tables(inner, chunks):
    slab = np.arange(SLABS)
    freq = np.arange(SLABS) + 0.5
    angle = 2.0 * np.pi / (2 * SLABS) * np.outer(freq, slab)
    eye = np.eye(GROUP)
    first = np.concatenate([np.kron(np.cos(angle), eye), np.kron(-np.sin(angle), eye)], axis=0)
    blocks = first.reshape(first.shape[0], chunks, -1)
    order = np.array(partners(chunks))
    first = np.stack([blocks[:, order ^ p].reshape(first.shape) for p in range(chunks)])
    last = first.transpose(0, 2, 1)
    within = np.arange(inner)
    turn = np.repeat(2.0 * np.pi / (2 * SLABS * inner) * np.outer(freq, within), GROUP, axis=0)
    circle = 2.0 * np.pi / inner * (np.outer(within, within) % inner)
    cos, sin = np.cos(circle), np.sin(circle)
    forward = np.block([[cos, -sin], [sin, cos]])
    narrow = ml_dtypes.bfloat16
    return (
        first.astype(narrow),
        last.astype(narrow),
        np.cos(turn).astype(np.float32),
        np.sin(turn).astype(np.float32),
        forward.astype(narrow),
        forward.T.astype(narrow),
    )


def gather_slabs(blocks, inner):
    local = blocks[0].shape[1]
    wide = [block.astype(F32) for block in blocks]
    halves = []
    for half in range(2):
        rows = slice(half * GROUP, (half + 1) * GROUP)
        pieces = [block[rows, at : at + inner] for block in wide for at in range(0, local, inner)]
        halves.append(jnp.concatenate(pieces, axis=0))
    return jnp.concatenate(halves, axis=1).astype(BF16)


def forward_dft(rows, first, cos, sin, forward, inner):
    stage = jnp.dot(first, rows, preferred_element_type=F32)
    half_rows = SLABS * GROUP
    turned = []
    for half in range(2):
        lanes = slice(half * inner, (half + 1) * inner)
        real, imag = stage[:half_rows, lanes], stage[half_rows:, lanes]
        turned.append(
            jnp.concatenate([real * cos + imag * sin, imag * cos - real * sin], axis=1).astype(BF16)
        )
    spec = jnp.dot(jnp.concatenate(turned, axis=0), forward, preferred_element_type=F32)
    return (spec[:, :inner], spec[:, inner:])


def inverse_dft(spec, last, cos, sin, backward, inner):
    both = jnp.concatenate(spec, axis=1).astype(BF16)
    stage = jnp.dot(both, backward, preferred_element_type=F32)
    half_rows = SLABS * GROUP
    turned = []
    for half in range(2):
        rows = slice(half * half_rows, (half + 1) * half_rows)
        real, imag = stage[rows, :inner], stage[rows, inner:]
        turned.append(
            jnp.concatenate([real * cos - imag * sin, imag * cos + real * sin], axis=0).astype(BF16)
        )
    return jnp.dot(last, jnp.concatenate(turned, axis=1), preferred_element_type=F32)


def scatter_slabs(rows, scale, outs, lead, at_rows, inner):
    local = outs[0].shape[-1]
    per = local // inner
    scaled = rows * scale
    for src, out in enumerate(outs):
        for part in range(per):
            at = (src * per + part) * GROUP
            tile = jnp.concatenate(
                [scaled[at : at + GROUP, :inner], scaled[at : at + GROUP, inner:]], axis=0
            ).astype(BF16)
            lanes = slice(part * inner, (part + 1) * inner)
            if lead is None:
                out[at_rows, lanes] = tile
            else:
                out[lead, at_rows, lanes] = tile


def times_plain(left, right):
    return (left[0] * right[0] - left[1] * right[1], left[0] * right[1] + left[1] * right[0])


def times_conj(left, right):
    return (left[0] * right[0] + left[1] * right[1], left[1] * right[0] - left[0] * right[1])


def pair_order(chunks):
    half = chunks // 2
    return [*range(half), *range(half + 1, chunks - 1), half, chunks - 1]


def grad_order(chunks):
    half = chunks // 2
    return [0, 1, *range(half + 1, chunks), *range(2, half + 1)]


def in_place(refs, order):
    return [refs[order.index(k)] for k in range(len(refs))]


def response_kernel(chunks, inner, me, *refs):
    pair, refs = in_place(refs[:chunks], pair_order(chunks)), refs[chunks:]
    (first, last, cos, sin, forward, backward), outs = refs[:6], refs[6:]
    tables = (first[...], cos[...], sin[...], forward[...], inner)
    for at in range(0, outs[0].shape[-2], STEP):
        rows = slice(at, at + STEP)
        prod = forward_dft(gather_slabs([ref[0, rows] for ref in pair], inner), *tables)
        taps = forward_dft(gather_slabs([ref[1, rows] for ref in pair], inner), *tables)
        result = inverse_dft(
            times_plain(prod, taps), last[...], cos[...], sin[...], backward[...], inner
        )
        scatter_slabs(result, 1.0 / (SLABS * inner), outs, None, rows, inner)


def backward_kernel(chunks, inner, scale, me, *refs):
    pair, grad, refs = refs[:chunks], refs[chunks : 2 * chunks], refs[2 * chunks :]
    pair, grad = in_place(pair, pair_order(chunks)), in_place(grad, grad_order(chunks))
    (first, last, cos, sin, forward, backward), outs = refs[:6], refs[6:]
    tables = (first[...], cos[...], sin[...], forward[...], inner)
    back_tables = (last[...], cos[...], sin[...], backward[...], inner)
    for at in range(0, outs[0].shape[-2], STEP):
        rows = slice(at, at + STEP)
        grad_spec = forward_dft(gather_slabs([ref[rows] for ref in grad], inner), *tables)
        taps = forward_dft(gather_slabs([ref[1, rows] for ref in pair], inner), *tables)
        result = inverse_dft(times_conj(grad_spec, taps), *back_tables)
        scatter_slabs(result, 1.0 / (SLABS * inner), outs, 0, rows, inner)
        prod = forward_dft(gather_slabs([ref[0, rows] for ref in pair], inner), *tables)
        result = inverse_dft(times_conj(grad_spec, prod), *back_tables)
        scatter_slabs(result, scale / (SLABS * inner), outs, 1, rows, inner)


def conv_call(kernel, me, operands, tables, lead, inner, transforms):
    chunks, shape = len(operands[0]), operands[0][0].shape
    channels, local = shape[-2:]
    def rows_of(shape):
        middle = shape[:-2]
        return pl.BlockSpec(
            middle + (2 * STEP, local), lambda i, me: (0,) * len(middle) + (i, 0)
        )

    def whole(table):
        return pl.BlockSpec(table.shape, lambda i, me: (0, 0))

    out_shape = lead + (channels, local)
    rows = channels * SLABS
    flops = transforms * rows * (2 * (2 * inner) ** 2 + 4 * SLABS * GROUP * inner)
    flat = [chunk for operand in operands for chunk in operand]
    return pl.pallas_call(
        kernel,
        grid_spec=pltpu.PrefetchScalarGridSpec(
            num_scalar_prefetch=1,
            grid=(channels // (2 * STEP),),
            in_specs=[rows_of(chunk.shape) for chunk in flat] + [whole(t) for t in tables],
            out_specs=[rows_of(out_shape)] * chunks,
        ),
        out_shape=[jax.ShapeDtypeStruct(out_shape, BF16)] * chunks,
        compiler_params=pltpu.CompilerParams(vmem_limit_bytes=40 * 1024 * 1024),
        cost_estimate=pl.CostEstimate(
            flops=flops, bytes_accessed=2 * rows * inner * 4, transcendentals=0
        ),
    )(me, *flat, *tables)


def elementwise(left, right):
    return (left.astype(F32) * right.astype(F32)).astype(BF16)


def prepare_kernel(masks, scale, inner_gate, signal, taps, gain, *refs):
    count = len(masks)
    outs, (gates, values, filters, sems) = refs[:count], refs[count:]
    me = lax.axis_index("ctx")
    copies = []
    for k, mask in enumerate(masks):
        at = me ^ mask
        pairs = ((inner_gate, gates), (signal, values), (taps, filters))
        copies.append(
            [
                pltpu.make_async_copy(src.at[at], dst.at[k], sems.at[k, n])
                for n, (src, dst) in enumerate(pairs)
            ]
        )
    for group in copies:
        for copy in group:
            copy.start()
    rows, lanes = gates.shape[1], gain.shape[1]
    shape = (rows, lanes)
    diagonal = lax.broadcasted_iota(jnp.int32, shape, 0) == lax.broadcasted_iota(jnp.int32, shape, 1)
    at_zero = (me == 0) & (lax.broadcasted_iota(jnp.int32, filters.shape[1:], 1) == 0)
    for k, (mask, group, out) in enumerate(zip(masks, copies, outs)):
        row = gain[pl.ds(me ^ mask, 1), :]
        column = jnp.sum(jnp.where(diagonal, row, 0.0), axis=1, keepdims=True)
        for copy in group:
            copy.wait()
        out[0] = elementwise(gates[k], values[k])
        out[1] = (filters[k] * scale + jnp.where(at_zero, column, 0.0)).astype(BF16)


def prepare_call(masks, scale, inner_gate, signal, taps, gain):
    count, (rows, lanes) = len(masks), taps.shape[1:]
    out = jax.ShapeDtypeStruct((2, rows, lanes), BF16)
    anywhere = pl.BlockSpec(memory_space=pl.ANY)
    inside = pl.BlockSpec(memory_space=pltpu.VMEM)
    return pl.pallas_call(
        functools.partial(prepare_kernel, masks, scale),
        in_specs=[anywhere, anywhere, anywhere, inside],
        out_specs=[inside] * count,
        out_shape=[out] * count,
        scratch_shapes=[
            pltpu.VMEM((count, rows, lanes), BF16),
            pltpu.VMEM((count, rows, lanes), BF16),
            pltpu.VMEM((count, rows, lanes), F32),
            pltpu.SemaphoreType.DMA((count, 3)),
        ],
        compiler_params=pltpu.CompilerParams(vmem_limit_bytes=62 * 1024 * 1024),
        cost_estimate=pl.CostEstimate(
            flops=8 * count * rows * lanes, bytes_accessed=12 * count * rows * lanes, transcendentals=0
        ),
    )(inner_gate, signal, taps, gain)


def project_kernel(chunks, members, me, *refs):
    weights, blocks = refs[:members], refs[members : 2 * members]
    gate, upstream, *outs = refs[2 * members :]
    step = pl.program_id(0)
    rows = weights[0].shape[0] // 2
    total = jnp.dot(weights[0][...], blocks[0][...], preferred_element_type=F32)
    for weight, block in zip(weights[1:], blocks[1:]):
        total += jnp.dot(weight[...], block[...], preferred_element_type=F32)
    total = total.astype(BF16)
    upstream[...] = total.reshape(upstream.shape)
    low = elementwise(total[:rows], gate[0])
    high = elementwise(total[rows:], gate[1])
    swapped = (me[0] & 1) == 1
    place = partners(chunks).index
    for pair in range(chunks // 2):

        @pl.when(step == pair)
        def _():
            outs[place(2 * pair)][...] = jnp.where(swapped, high, low)
            outs[place(2 * pair + 1)][...] = jnp.where(swapped, low, high)


def outer_kernel(chunks, me, upstream, *refs):
    chunk, out = refs[:chunks], refs[chunks]
    for d, piece in zip(partners(chunks), chunk):
        at = me[0] ^ d
        out[at] = elementwise(upstream[at], piece[...])


def finish_kernel(count, me, *refs):
    gates, refs = refs[:count], refs[count:]
    values, refs = refs[:count], refs[count:]
    chunk, (grad_inner, grad_signal, grad_taps) = refs[:count], refs[-3:]
    step = pl.program_id(0)
    for k in range(count):

        @pl.when(step == k)
        def _(k=k):
            back = chunk[k][0]
            grad_inner[0] = elementwise(back, values[k][0])
            grad_signal[0] = elementwise(back, gates[k][0])
            grad_taps[0] = chunk[k][1].astype(F32)


def finish_call(me, masks, inner_gate, signal, chunks, earlier):
    count, shape = len(masks), inner_gate.shape
    block = (1,) + shape[1:]

    def place(i, me):
        mask = masks[0]
        for k in range(1, count):
            mask = jnp.where(i == k, masks[k], mask)
        return (me[0] ^ mask, 0, 0)

    gates = [pl.BlockSpec(block, lambda i, me, mask=mask: (me[0] ^ mask, 0, 0)) for mask in masks]
    pieces = [pl.BlockSpec(chunk.shape, lambda i, me: (0, 0, 0)) for chunk in chunks]
    return pl.pallas_call(
        functools.partial(finish_kernel, count),
        grid_spec=pltpu.PrefetchScalarGridSpec(
            num_scalar_prefetch=1,
            grid=(count,),
            in_specs=gates * 2 + pieces + [pl.BlockSpec(memory_space=pl.ANY)] * len(earlier),
            out_specs=[pl.BlockSpec(block, place)] * 3,
        ),
        out_shape=[jax.ShapeDtypeStruct(shape, dtype) for dtype in (BF16, BF16, F32)],
        input_output_aliases={1 + 3 * count + n: n for n in range(len(earlier))},
        compiler_params=pltpu.CompilerParams(vmem_limit_bytes=32 * 1024 * 1024),
        cost_estimate=pl.CostEstimate(
            flops=2 * count * math.prod(shape[1:]),
            bytes_accessed=16 * count * math.prod(shape[1:]),
            transcendentals=0,
        ),
    )(me, *[inner_gate] * count, *[signal] * count, *chunks, *earlier)


def rowwise_call(kernel, me, wholes, pieces, out_shapes, rows, limit=32):
    def spec(shape):
        lead = shape[:-2]
        return pl.BlockSpec(
            lead + (rows, shape[-1]), lambda i, me: (0,) * len(lead) + (i, 0)
        )

    channels = wholes[0].shape[1]
    size = sum(math.prod(x.shape) * x.dtype.itemsize for x in (*wholes, *pieces, *out_shapes))
    return pl.pallas_call(
        kernel,
        grid_spec=pltpu.PrefetchScalarGridSpec(
            num_scalar_prefetch=1,
            grid=(channels // rows,),
            in_specs=[spec(x.shape) for x in (*wholes, *pieces)],
            out_specs=[spec(x.shape) for x in out_shapes],
        ),
        out_shape=out_shapes,
        compiler_params=pltpu.CompilerParams(vmem_limit_bytes=limit * 1024 * 1024),
        cost_estimate=pl.CostEstimate(flops=size, bytes_accessed=size, transcendentals=0),
    )(me, *wholes, *pieces)


def project_call(me, weight, blocks, gate):
    chunks, channels, local = gate.shape
    members, depth = len(blocks), blocks[0].shape[0]

    def pair(i, me):
        return (me[0] >> 1) ^ i

    rows = 2 * channels
    return pl.pallas_call(
        functools.partial(project_kernel, chunks, members),
        grid_spec=pltpu.PrefetchScalarGridSpec(
            num_scalar_prefetch=1,
            grid=(chunks // 2,),
            in_specs=[
                pl.BlockSpec((rows, depth), lambda i, me, j=j: (pair(i, me), me[1] ^ j))
                for j in range(members)
            ]
            + [pl.BlockSpec((depth, local), lambda i, me: (0, 0))] * members
            + [pl.BlockSpec((2, channels, local), lambda i, me: (pair(i, me), 0, 0))],
            out_specs=[pl.BlockSpec((2, channels, local), lambda i, me: (pair(i, me), 0, 0))]
            + [pl.BlockSpec((channels, local), lambda i, me: (0, 0))] * chunks,
        ),
        out_shape=[jax.ShapeDtypeStruct(gate.shape, BF16)]
        + [jax.ShapeDtypeStruct((channels, local), BF16)] * chunks,
        compiler_params=pltpu.CompilerParams(vmem_limit_bytes=40 * 1024 * 1024),
        cost_estimate=pl.CostEstimate(
            flops=2 * weight.size * local, bytes_accessed=2 * weight.size, transcendentals=0
        ),
    )(me, *[weight] * members, *blocks, gate)


def gather_start(block):
    count = lax.axis_size("group")
    return lax.ppermute(block, "group", [(g, g ^ (count // 2)) for g in range(count)])


def gather_rest(block, far, other):
    count = lax.axis_size("group")
    bit = count // 2
    held = {0: block, bit: far}
    bit //= 2
    while bit:
        pairs = [(g, g ^ bit) for g in range(count)]
        for j in list(held):
            sent = held[j]
            if j:
                sent, _ = lax.optimization_barrier((sent, other))
            held[j ^ bit] = lax.ppermute(sent, "group", pairs)
        bit //= 2
    return [held[j] for j in range(count)]


def send(part, d, count):
    return lax.ppermute(part, "ctx", [(p, p ^ d) for p in range(count)])


def exchange(parts):
    count = len(parts)
    order = partners(count)
    if count > 8:
        blocks = lax.axis_index("ctx") ^ jnp.arange(count)
        where = np.argsort(order)
        sent = jnp.take(jnp.take(jnp.stack(parts), where, axis=0), blocks, axis=0)
        came = lax.all_to_all(sent, "ctx", split_axis=0, concat_axis=0, tiled=True)
        return list(jnp.take(jnp.take(came, blocks, axis=0), np.array(order), axis=0))
    return [parts[0]] + [send(part, d, count) for d, part in zip(order[1:], parts[1:])]


def after(parts, other):
    held, _ = lax.optimization_barrier((parts[0], other))
    return [held] + list(parts[1:])


def per_device(outer_gate, inner_gate, signal, cotangent, out_weight, filter_taps, skip_gain):
    ch_dev, tok_local = outer_gate.shape
    n_ctx = lax.axis_size("ctx")
    ch_slice = ch_dev // n_ctx
    seq_len = n_ctx * tok_local
    inner = seq_len // SLABS
    scale = 1.0 / math.sqrt(seq_len)
    me = jnp.stack([lax.axis_index("ctx"), lax.axis_index("group")])

    def split(array):
        return array.reshape(n_ctx, ch_slice, -1)

    def flat(array):
        return array.reshape(ch_dev, tok_local)

    def shapes(lead, dtype, count):
        return [jax.ShapeDtypeStruct(lead + (ch_slice, tok_local), dtype)] * count

    tables = [jnp.asarray(table) for table in make_tables(inner, n_ctx)]
    tables = [table if table.ndim == 2 else table[me[0]] for table in tables]
    masks = partners(n_ctx)
    first = min(3, n_ctx)
    sources = (scale, split(inner_gate), split(signal), split(filter_taps), split(skip_gain)[:, :, 0])
    head = prepare_call(masks[1:first], *sources)
    cotangent, _ = lax.optimization_barrier((cotangent, head[0]))
    far = gather_start(cotangent)
    own, *rest = prepare_call([0] + masks[first:], *sources)
    pair = exchange([own, *head, *rest])
    gathered = gather_rest(cotangent, far, (pair[1:first], pair[-1:], rest[:1], tables[:2]))
    pair_sent = [pair[k] for k in pair_order(n_ctx)]
    upstream, *grad = project_call(me, out_weight, gathered, split(outer_gate))
    response = conv_call(
        functools.partial(response_kernel, n_ctx, inner), me, (after(pair_sent, grad[0]),), tables, (), inner, 3
    )
    grad_came = exchange(grad)
    waiting, _ = lax.optimization_barrier((list(response[2:]), grad_came[1:]))
    resp_came = exchange([*response[:2], *waiting])
    backs = conv_call(
        functools.partial(backward_kernel, n_ctx, inner, scale),
        me,
        (pair_sent, after([grad_came[k] for k in grad_order(n_ctx)], response[0])),
        tables,
        (2,),
        inner,
        5,
    )
    backs_came = exchange(backs)
    (grad_outer,) = rowwise_call(
        functools.partial(outer_kernel, n_ctx),
        me,
        (upstream,),
        after(resp_came, backs[0]),
        shapes((n_ctx,), BF16, 1),
        32,
    )
    outs = []
    last = range(3, 5)
    for part in ([k for k in range(n_ctx) if k not in last], last):
        outs = finish_call(
            me,
            [masks[k] for k in part],
            split(inner_gate),
            split(signal),
            [backs_came[k] for k in part],
            outs,
        )
    grad_inner, grad_signal, grad_taps = outs
    return (flat(grad_outer), flat(grad_inner), flat(grad_signal), flat(grad_taps))


def solution(mesh):
    in_specs = (
        P("group", "ctx"),
        P("group", "ctx"),
        P("group", "ctx"),
        P("group", "ctx"),
        P("group", None),
        P("group", "ctx"),
        P("group"),
    )
    out_specs = (P("group", "ctx"), P("group", "ctx"), P("group", "ctx"), P("group", "ctx"))
    return jax.shard_map(
        per_device, mesh=mesh, in_specs=in_specs, out_specs=out_specs, check_vma=False
    )
```

```python
import functools
import math

import jax
import jax.numpy as jnp
import ml_dtypes
import numpy as np
from jax import lax
from jax.experimental import pallas as pl
from jax.experimental.pallas import tpu as pltpu
from jax.sharding import PartitionSpec as P

SLABS = 32
GROUP = 8
STEP = 2 * GROUP
F32 = jnp.float32
BF16 = jnp.bfloat16


def partners(count):
    return [0] + list(reversed(range(1, count)))


def make_tables(inner, chunks):
    slab = np.arange(SLABS)
    freq = np.arange(SLABS) + 0.5
    angle = 2.0 * np.pi / (2 * SLABS) * np.outer(freq, slab)
    eye = np.eye(GROUP)
    first = np.concatenate([np.kron(np.cos(angle), eye), np.kron(-np.sin(angle), eye)], axis=0)
    blocks = first.reshape(first.shape[0], chunks, -1)
    order = np.array(partners(chunks))
    first = np.stack([blocks[:, order ^ p].reshape(first.shape) for p in range(chunks)])
    last = first.transpose(0, 2, 1)
    within = np.arange(inner)
    turn = np.repeat(2.0 * np.pi / (2 * SLABS * inner) * np.outer(freq, within), GROUP, axis=0)
    circle = 2.0 * np.pi / inner * (np.outer(within, within) % inner)
    cos, sin = np.cos(circle), np.sin(circle)
    forward = np.block([[cos, -sin], [sin, cos]])
    narrow = ml_dtypes.bfloat16
    return (
        first.astype(narrow),
        last.astype(narrow),
        np.cos(turn).astype(np.float32),
        np.sin(turn).astype(np.float32),
        forward.astype(narrow),
        forward.T.astype(narrow),
    )


def gather_slabs(blocks, inner):
    local = blocks[0].shape[1]
    wide = [block.astype(F32) for block in blocks]
    halves = []
    for half in range(2):
        rows = slice(half * GROUP, (half + 1) * GROUP)
        pieces = [block[rows, at : at + inner] for block in wide for at in range(0, local, inner)]
        halves.append(jnp.concatenate(pieces, axis=0))
    return jnp.concatenate(halves, axis=1).astype(BF16)


def forward_dft(rows, first, cos, sin, forward, inner):
    stage = jnp.dot(first, rows, preferred_element_type=F32)
    half_rows = SLABS * GROUP
    turned = []
    for half in range(2):
        lanes = slice(half * inner, (half + 1) * inner)
        real, imag = stage[:half_rows, lanes], stage[half_rows:, lanes]
        turned.append(
            jnp.concatenate([real * cos + imag * sin, imag * cos - real * sin], axis=1).astype(BF16)
        )
    spec = jnp.dot(jnp.concatenate(turned, axis=0), forward, preferred_element_type=F32)
    return (spec[:, :inner], spec[:, inner:])


def inverse_dft(spec, last, cos, sin, backward, inner):
    both = jnp.concatenate(spec, axis=1).astype(BF16)
    stage = jnp.dot(both, backward, preferred_element_type=F32)
    half_rows = SLABS * GROUP
    turned = []
    for half in range(2):
        rows = slice(half * half_rows, (half + 1) * half_rows)
        real, imag = stage[rows, :inner], stage[rows, inner:]
        turned.append(
            jnp.concatenate([real * cos - imag * sin, imag * cos + real * sin], axis=0).astype(BF16)
        )
    return jnp.dot(last, jnp.concatenate(turned, axis=1), preferred_element_type=F32)


def scatter_slabs(rows, scale, outs, lead, at_rows, inner):
    local = outs[0].shape[-1]
    per = local // inner
    scaled = rows * scale
    for src, out in enumerate(outs):
        for part in range(per):
            at = (src * per + part) * GROUP
            tile = jnp.concatenate(
                [scaled[at : at + GROUP, :inner], scaled[at : at + GROUP, inner:]], axis=0
            ).astype(BF16)
            lanes = slice(part * inner, (part + 1) * inner)
            if lead is None:
                out[at_rows, lanes] = tile
            else:
                out[lead, at_rows, lanes] = tile


def times_plain(left, right):
    return (left[0] * right[0] - left[1] * right[1], left[0] * right[1] + left[1] * right[0])


def times_conj(left, right):
    return (left[0] * right[0] + left[1] * right[1], left[1] * right[0] - left[0] * right[1])


def pair_order(chunks):
    half = chunks // 2
    return [*range(half), *range(half + 1, chunks - 1), half, chunks - 1]


def grad_order(chunks):
    half = chunks // 2
    return [0, 1, *range(half + 1, chunks), *range(2, half + 1)]


def in_place(refs, order):
    return [refs[order.index(k)] for k in range(len(refs))]


def response_kernel(chunks, inner, me, *refs):
    pair, refs = in_place(refs[:chunks], pair_order(chunks)), refs[chunks:]
    (first, last, cos, sin, forward, backward), outs = refs[:6], refs[6:]
    tables = (first[...], cos[...], sin[...], forward[...], inner)
    for at in range(0, outs[0].shape[-2], STEP):
        rows = slice(at, at + STEP)
        prod = forward_dft(gather_slabs([ref[0, rows] for ref in pair], inner), *tables)
        taps = forward_dft(gather_slabs([ref[1, rows] for ref in pair], inner), *tables)
        result = inverse_dft(
            times_plain(prod, taps), last[...], cos[...], sin[...], backward[...], inner
        )
        scatter_slabs(result, 1.0 / (SLABS * inner), outs, None, rows, inner)


def backward_kernel(chunks, inner, scale, me, *refs):
    pair, grad, refs = refs[:chunks], refs[chunks : 2 * chunks], refs[2 * chunks :]
    pair, grad = in_place(pair, pair_order(chunks)), in_place(grad, grad_order(chunks))
    (first, last, cos, sin, forward, backward), outs = refs[:6], refs[6:]
    tables = (first[...], cos[...], sin[...], forward[...], inner)
    back_tables = (last[...], cos[...], sin[...], backward[...], inner)
    for at in range(0, outs[0].shape[-2], STEP):
        rows = slice(at, at + STEP)
        grad_spec = forward_dft(gather_slabs([ref[rows] for ref in grad], inner), *tables)
        taps = forward_dft(gather_slabs([ref[1, rows] for ref in pair], inner), *tables)
        result = inverse_dft(times_conj(grad_spec, taps), *back_tables)
        scatter_slabs(result, 1.0 / (SLABS * inner), outs, 0, rows, inner)
        prod = forward_dft(gather_slabs([ref[0, rows] for ref in pair], inner), *tables)
        result = inverse_dft(times_conj(grad_spec, prod), *back_tables)
        scatter_slabs(result, scale / (SLABS * inner), outs, 1, rows, inner)


def conv_call(kernel, me, operands, tables, lead, inner, transforms):
    chunks, shape = len(operands[0]), operands[0][0].shape
    channels, local = shape[-2:]
    def rows_of(shape):
        middle = shape[:-2]
        return pl.BlockSpec(
            middle + (2 * STEP, local), lambda i, me: (0,) * len(middle) + (i, 0)
        )

    def whole(table):
        return pl.BlockSpec(table.shape, lambda i, me: (0, 0))

    out_shape = lead + (channels, local)
    rows = channels * SLABS
    flops = transforms * rows * (2 * (2 * inner) ** 2 + 4 * SLABS * GROUP * inner)
    flat = [chunk for operand in operands for chunk in operand]
    return pl.pallas_call(
        kernel,
        grid_spec=pltpu.PrefetchScalarGridSpec(
            num_scalar_prefetch=1,
            grid=(channels // (2 * STEP),),
            in_specs=[rows_of(chunk.shape) for chunk in flat] + [whole(t) for t in tables],
            out_specs=[rows_of(out_shape)] * chunks,
        ),
        out_shape=[jax.ShapeDtypeStruct(out_shape, BF16)] * chunks,
        compiler_params=pltpu.CompilerParams(vmem_limit_bytes=40 * 1024 * 1024),
        cost_estimate=pl.CostEstimate(
            flops=flops, bytes_accessed=2 * rows * inner * 4, transcendentals=0
        ),
    )(me, *flat, *tables)


def elementwise(left, right):
    return (left.astype(F32) * right.astype(F32)).astype(BF16)


def prepare_kernel(masks, scale, inner_gate, signal, taps, gain, *refs):
    count = len(masks)
    outs, (gates, values, filters, sems) = refs[:count], refs[count:]
    me = lax.axis_index("ctx")
    copies = []
    for k, mask in enumerate(masks):
        at = me ^ mask
        pairs = ((inner_gate, gates), (signal, values), (taps, filters))
        copies.append(
            [
                pltpu.make_async_copy(src.at[at], dst.at[k], sems.at[k, n])
                for n, (src, dst) in enumerate(pairs)
            ]
        )
    for group in copies:
        for copy in group:
            copy.start()
    rows, lanes = gates.shape[1], gain.shape[1]
    shape = (rows, lanes)
    diagonal = lax.broadcasted_iota(jnp.int32, shape, 0) == lax.broadcasted_iota(jnp.int32, shape, 1)
    at_zero = (me == 0) & (lax.broadcasted_iota(jnp.int32, filters.shape[1:], 1) == 0)
    for k, (mask, group, out) in enumerate(zip(masks, copies, outs)):
        row = gain[pl.ds(me ^ mask, 1), :]
        column = jnp.sum(jnp.where(diagonal, row, 0.0), axis=1, keepdims=True)
        for copy in group:
            copy.wait()
        out[0] = elementwise(gates[k], values[k])
        out[1] = (filters[k] * scale + jnp.where(at_zero, column, 0.0)).astype(BF16)


def prepare_call(masks, scale, inner_gate, signal, taps, gain):
    count, (rows, lanes) = len(masks), taps.shape[1:]
    out = jax.ShapeDtypeStruct((2, rows, lanes), BF16)
    anywhere = pl.BlockSpec(memory_space=pl.ANY)
    inside = pl.BlockSpec(memory_space=pltpu.VMEM)
    return pl.pallas_call(
        functools.partial(prepare_kernel, masks, scale),
        in_specs=[anywhere, anywhere, anywhere, inside],
        out_specs=[inside] * count,
        out_shape=[out] * count,
        scratch_shapes=[
            pltpu.VMEM((count, rows, lanes), BF16),
            pltpu.VMEM((count, rows, lanes), BF16),
            pltpu.VMEM((count, rows, lanes), F32),
            pltpu.SemaphoreType.DMA((count, 3)),
        ],
        compiler_params=pltpu.CompilerParams(vmem_limit_bytes=62 * 1024 * 1024),
        cost_estimate=pl.CostEstimate(
            flops=8 * count * rows * lanes, bytes_accessed=12 * count * rows * lanes, transcendentals=0
        ),
    )(inner_gate, signal, taps, gain)


def project_kernel(chunks, members, me, *refs):
    weights, blocks = refs[:members], refs[members : 2 * members]
    gate, upstream, *outs = refs[2 * members :]
    step = pl.program_id(0)
    rows = weights[0].shape[0] // 2
    total = jnp.dot(weights[0][...], blocks[0][...], preferred_element_type=F32)
    for weight, block in zip(weights[1:], blocks[1:]):
        total += jnp.dot(weight[...], block[...], preferred_element_type=F32)
    total = total.astype(BF16)
    upstream[...] = total.reshape(upstream.shape)
    low = elementwise(total[:rows], gate[0])
    high = elementwise(total[rows:], gate[1])
    swapped = (me[0] & 1) == 1
    place = partners(chunks).index
    for pair in range(chunks // 2):

        @pl.when(step == pair)
        def _():
            outs[place(2 * pair)][...] = jnp.where(swapped, high, low)
            outs[place(2 * pair + 1)][...] = jnp.where(swapped, low, high)


def outer_kernel(chunks, me, upstream, *refs):
    chunk, out = refs[:chunks], refs[chunks]
    for d, piece in zip(partners(chunks), chunk):
        at = me[0] ^ d
        out[at] = elementwise(upstream[at], piece[...])


def finish_kernel(count, me, *refs):
    gates, refs = refs[:count], refs[count:]
    values, refs = refs[:count], refs[count:]
    chunk, (grad_inner, grad_signal, grad_taps) = refs[:count], refs[-3:]
    step = pl.program_id(0)
    for k in range(count):

        @pl.when(step == k)
        def _(k=k):
            back = chunk[k][0]
            grad_inner[0] = elementwise(back, values[k][0])
            grad_signal[0] = elementwise(back, gates[k][0])
            grad_taps[0] = chunk[k][1].astype(F32)


def finish_call(me, masks, inner_gate, signal, chunks, earlier):
    count, shape = len(masks), inner_gate.shape
    block = (1,) + shape[1:]

    def place(i, me):
        mask = masks[0]
        for k in range(1, count):
            mask = jnp.where(i == k, masks[k], mask)
        return (me[0] ^ mask, 0, 0)

    gates = [pl.BlockSpec(block, lambda i, me, mask=mask: (me[0] ^ mask, 0, 0)) for mask in masks]
    pieces = [pl.BlockSpec(chunk.shape, lambda i, me: (0, 0, 0)) for chunk in chunks]
    return pl.pallas_call(
        functools.partial(finish_kernel, count),
        grid_spec=pltpu.PrefetchScalarGridSpec(
            num_scalar_prefetch=1,
            grid=(count,),
            in_specs=gates * 2 + pieces + [pl.BlockSpec(memory_space=pl.ANY)] * len(earlier),
            out_specs=[pl.BlockSpec(block, place)] * 3,
        ),
        out_shape=[jax.ShapeDtypeStruct(shape, dtype) for dtype in (BF16, BF16, F32)],
        input_output_aliases={1 + 3 * count + n: n for n in range(len(earlier))},
        compiler_params=pltpu.CompilerParams(vmem_limit_bytes=32 * 1024 * 1024),
        cost_estimate=pl.CostEstimate(
            flops=2 * count * math.prod(shape[1:]),
            bytes_accessed=16 * count * math.prod(shape[1:]),
            transcendentals=0,
        ),
    )(me, *[inner_gate] * count, *[signal] * count, *chunks, *earlier)


def rowwise_call(kernel, me, wholes, pieces, out_shapes, rows, limit=32):
    def spec(shape):
        lead = shape[:-2]
        return pl.BlockSpec(
            lead + (rows, shape[-1]), lambda i, me: (0,) * len(lead) + (i, 0)
        )

    channels = wholes[0].shape[1]
    size = sum(math.prod(x.shape) * x.dtype.itemsize for x in (*wholes, *pieces, *out_shapes))
    return pl.pallas_call(
        kernel,
        grid_spec=pltpu.PrefetchScalarGridSpec(
            num_scalar_prefetch=1,
            grid=(channels // rows,),
            in_specs=[spec(x.shape) for x in (*wholes, *pieces)],
            out_specs=[spec(x.shape) for x in out_shapes],
        ),
        out_shape=out_shapes,
        compiler_params=pltpu.CompilerParams(vmem_limit_bytes=limit * 1024 * 1024),
        cost_estimate=pl.CostEstimate(flops=size, bytes_accessed=size, transcendentals=0),
    )(me, *wholes, *pieces)


def project_call(me, weight, blocks, gate):
    chunks, channels, local = gate.shape
    members, depth = len(blocks), blocks[0].shape[0]

    def pair(i, me):
        return (me[0] >> 1) ^ i

    rows = 2 * channels
    return pl.pallas_call(
        functools.partial(project_kernel, chunks, members),
        grid_spec=pltpu.PrefetchScalarGridSpec(
            num_scalar_prefetch=1,
            grid=(chunks // 2,),
            in_specs=[
                pl.BlockSpec((rows, depth), lambda i, me, j=j: (pair(i, me), me[1] ^ j))
                for j in range(members)
            ]
            + [pl.BlockSpec((depth, local), lambda i, me: (0, 0))] * members
            + [pl.BlockSpec((2, channels, local), lambda i, me: (pair(i, me), 0, 0))],
            out_specs=[pl.BlockSpec((2, channels, local), lambda i, me: (pair(i, me), 0, 0))]
            + [pl.BlockSpec((channels, local), lambda i, me: (0, 0))] * chunks,
        ),
        out_shape=[jax.ShapeDtypeStruct(gate.shape, BF16)]
        + [jax.ShapeDtypeStruct((channels, local), BF16)] * chunks,
        compiler_params=pltpu.CompilerParams(vmem_limit_bytes=40 * 1024 * 1024),
        cost_estimate=pl.CostEstimate(
            flops=2 * weight.size * local, bytes_accessed=2 * weight.size, transcendentals=0
        ),
    )(me, *[weight] * members, *blocks, gate)


def gather_start(block):
    count = lax.axis_size("group")
    return lax.ppermute(block, "group", [(g, g ^ (count // 2)) for g in range(count)])


def gather_rest(block, far, other):
    count = lax.axis_size("group")
    bit = count // 2
    held = {0: block, bit: far}
    bit //= 2
    while bit:
        pairs = [(g, g ^ bit) for g in range(count)]
        for j in list(held):
            sent = held[j]
            if j:
                sent, _ = lax.optimization_barrier((sent, other))
            held[j ^ bit] = lax.ppermute(sent, "group", pairs)
        bit //= 2
    return [held[j] for j in range(count)]


def send(part, d, count):
    return lax.ppermute(part, "ctx", [(p, p ^ d) for p in range(count)])


def exchange(parts):
    count = len(parts)
    order = partners(count)
    if count > 8:
        blocks = lax.axis_index("ctx") ^ jnp.arange(count)
        where = np.argsort(order)
        sent = jnp.take(jnp.take(jnp.stack(parts), where, axis=0), blocks, axis=0)
        came = lax.all_to_all(sent, "ctx", split_axis=0, concat_axis=0, tiled=True)
        return list(jnp.take(jnp.take(came, blocks, axis=0), np.array(order), axis=0))
    return [parts[0]] + [send(part, d, count) for d, part in zip(order[1:], parts[1:])]


def after(parts, other):
    held, _ = lax.optimization_barrier((parts[0], other))
    return [held] + list(parts[1:])


def per_device(outer_gate, inner_gate, signal, cotangent, out_weight, filter_taps, skip_gain):
    ch_dev, tok_local = outer_gate.shape
    n_ctx = lax.axis_size("ctx")
    ch_slice = ch_dev // n_ctx
    seq_len = n_ctx * tok_local
    inner = seq_len // SLABS
    scale = 1.0 / math.sqrt(seq_len)
    me = jnp.stack([lax.axis_index("ctx"), lax.axis_index("group")])

    def split(array):
        return array.reshape(n_ctx, ch_slice, -1)

    def flat(array):
        return array.reshape(ch_dev, tok_local)

    def shapes(lead, dtype, count):
        return [jax.ShapeDtypeStruct(lead + (ch_slice, tok_local), dtype)] * count

    tables = [jnp.asarray(table) for table in make_tables(inner, n_ctx)]
    tables = [table if table.ndim == 2 else table[me[0]] for table in tables]
    masks = partners(n_ctx)
    first = min(3, n_ctx)
    sources = (scale, split(inner_gate), split(signal), split(filter_taps), split(skip_gain)[:, :, 0])
    head = prepare_call(masks[1:first], *sources)
    cotangent, _ = lax.optimization_barrier((cotangent, head[0]))
    far = gather_start(cotangent)
    own, *rest = prepare_call([0] + masks[first:], *sources)
    pair = exchange([own, *head, *rest])
    gathered = gather_rest(cotangent, far, (pair[1:first], pair[-1:], rest[:1], tables[:2]))
    pair_sent = [pair[k] for k in pair_order(n_ctx)]
    upstream, *grad = project_call(me, out_weight, gathered, split(outer_gate))
    response = conv_call(
        functools.partial(response_kernel, n_ctx, inner), me, (after(pair_sent, grad[0]),), tables, (), inner, 3
    )
    grad_came = exchange(grad)
    waiting, _ = lax.optimization_barrier((list(response[3:]), grad_came[1:]))
    resp_came = exchange([*response[:3], *waiting])
    backs = conv_call(
        functools.partial(backward_kernel, n_ctx, inner, scale),
        me,
        (pair_sent, after([grad_came[k] for k in grad_order(n_ctx)], response[0])),
        tables,
        (2,),
        inner,
        5,
    )
    backs_came = exchange(backs)
    (grad_outer,) = rowwise_call(
        functools.partial(outer_kernel, n_ctx),
        me,
        (upstream,),
        after(resp_came, backs[0]),
        shapes((n_ctx,), BF16, 1),
        32,
    )
    outs = []
    last = range(3, 5)
    for part in ([k for k in range(n_ctx) if k not in last], last):
        outs = finish_call(
            me,
            [masks[k] for k in part],
            split(inner_gate),
            split(signal),
            [backs_came[k] for k in part],
            outs,
        )
    grad_inner, grad_signal, grad_taps = outs
    return (flat(grad_outer), flat(grad_inner), flat(grad_signal), flat(grad_taps))


def solution(mesh):
    in_specs = (
        P("group", "ctx"),
        P("group", "ctx"),
        P("group", "ctx"),
        P("group", "ctx"),
        P("group", None),
        P("group", "ctx"),
        P("group"),
    )
    out_specs = (P("group", "ctx"), P("group", "ctx"), P("group", "ctx"), P("group", "ctx"))
    return jax.shard_map(
        per_device, mesh=mesh, in_specs=in_specs, out_specs=out_specs, check_vma=False
    )
```
